128 devices in a mesh: lat: 4 (over z_lo, core), lon: 32 (over x, z_hi, y).
Axes of the slice: x: 4, y: 4, z: 4 (z_hi: 2, z_lo: 2; z = z_hi * 2 + z_lo), core: 2. Of those that a mesh axis runs over, the one named last changes fastest.
Arguments:
- in_field: bfloat16 [256, 1440, 256], P('lat', 'lon'), may hold values from -6 to 6
- out_grad: bfloat16 [256, 1440, 256], P('lat', 'lon'), may hold values from -6 to 6
- spec_weight: bfloat16 [4096, 2, 16, 256], P(('lat', 'lon')), may hold values from -1 to 1
- inner_weight: bfloat16 [256, 1024], replicated, may hold values from -0.375 to 0.375
- output_projection_weight: bfloat16 [1024, 256], replicated, may hold values from -0.1875 to 0.1875
- kept_modes: int32 [4096], P(('lat', 'lon')), may hold values from 0 to 63, as said below
Outputs:
- input_grad: bfloat16 [256, 1440, 256], P('lat', 'lon')
- spectral_grad: float32 [4096, 2, 16, 256], P(('lat', 'lon'))
The draws below stay inside these ranges and needn't reach their ends.
Inputs may be any that keep to these rules, and one draw needn't show every extreme that they name: `kept_modes`: the 32 entries of each aligned block of 32 are distinct; entry v names the mode v // 2 of the block's latitude wavenumbers and v mod 2 of its longitude wavenumbers.
All inputs are finite; a program needn't handle non-finite values.
Results may differ from the reference program's by a relative error of at most 0.029.
Values may be sent and summed in bfloat16 or wider, within the bound.
A program may use at most 128 MiB of HBM per device.

```python
import math
import jax
import jax.numpy as jnp
from jax import lax

C = 256
HID = 1024
BS = 16
NLON = 1440
KM = 64
KLAT = 128
KEEP_DEV = 32
NLAT = 256
NB = 16
MB = 2
KB = 32
KEPT = 4096
N_LON = 32


def draw_kept_modes(key, part):
    key = jax.random.fold_in(key, 7)
    candidates = KB * MB
    blocks = KEPT // KEEP_DEV
    block_keys = jax.random.split(key, blocks)

    def select_block(block_key):
        order = jax.random.permutation(block_key, candidates)
        return jnp.sort(order[:KEEP_DEV]).astype(jnp.int32)
    return jax.vmap(select_block)(block_keys).reshape(KEPT).astype(jnp.int32)


def levels(own_key, extent, shards, low, top_value):
    level, own = 1.0, jax.random.fold_in(own_key, 6)
    for position, blocks in shards:
        steps = jnp.exp(jax.random.uniform(jax.random.fold_in(own, position), (blocks,), jnp.float32, low / len(shards), top_value / len(shards)))
        level = level * jnp.repeat(steps, extent[position] // blocks).reshape([-1 if axis == position else 1 for axis in range(len(extent))])
    return level


def scatter_about(stream_key, extent, spread, bound, cuts=(), held_as=jnp.bfloat16):
    entries = spread * jax.random.normal(stream_key, extent, jnp.float32)
    if cuts:
        entries = entries * levels(stream_key, extent, cuts, -0.22, 0.18)
    return jnp.clip(entries, -bound, bound).astype(held_as)


def setup_inputs(seed: int = 0) -> dict:
    key_of = jax.random.split(jax.random.key(seed), 7)
    in_field = scatter_about(key_of[0], (NLAT, NLON, C), 1.0, 6.0, ((0, 4), (1, 32)))
    out_grad = scatter_about(key_of[1], (NLAT, NLON, C), 1.0, 6.0, ((0, 4), (1, 32)))
    spec_weight = scatter_about(key_of[2], (KEPT, 2, NB, BS * BS), (2 * BS) ** -0.5, 1.0, ((0, 128),))
    inner_weight = scatter_about(key_of[3], (C, HID), C ** -0.5, 0.375)
    output_projection_weight = scatter_about(key_of[4], (HID, C), HID ** -0.5, 0.1875)
    kept_modes = draw_kept_modes(jax.random.fold_in(key_of[6], 71), 0)
    return dict(in_field=in_field, out_grad=out_grad, spec_weight=spec_weight, inner_weight=inner_weight, output_projection_weight=output_projection_weight, kept_modes=kept_modes)


def make_lon_basis():
    lon_ids = jnp.arange(NLON, dtype=jnp.int32)
    mode_ids = jnp.arange(KM, dtype=jnp.int32)
    phases = lon_ids[:, None] * mode_ids[None, :] % NLON
    angles = phases.astype(jnp.float32) * (2.0 * math.pi / NLON)
    return jnp.stack([jnp.cos(angles), -jnp.sin(angles)], axis=1).astype(jnp.bfloat16)

def lat_basis(doubled_rows, wave_ids):
    wavenum = wave_ids - KLAT // 2
    phases = jnp.mod(wavenum[:, None] * doubled_rows[None, :], 2 * NLAT)
    angles = phases.astype(jnp.float32) * (math.pi / NLAT)
    return (jnp.cos(angles).astype(jnp.bfloat16), jnp.sin(angles).astype(jnp.bfloat16))

def row_blocks(grid_point_values):
    block_rows = math.gcd(grid_point_values.shape[0], 32)
    return grid_point_values.reshape((grid_point_values.shape[0] // block_rows, block_rows) + grid_point_values.shape[1:])

def unblock(stacked):
    return stacked.reshape((-1,) + stacked.shape[2:])

def lon_spectrum(grid_point_values, longitude_basis):

    def one_block(tile_row_slice):
        return jnp.einsum('qny,nbd->qbdy', tile_row_slice.astype(jnp.float32), longitude_basis.astype(jnp.float32)).astype(jnp.bfloat16)
    return unblock(lax.map(one_block, row_blocks(grid_point_values)))

def lon_synthesis(lat_vals, longitude_basis, scale):

    def one_block(tile_row_slice):
        reduced_total = jnp.einsum('belv,wel->bwv', tile_row_slice.astype(jnp.float32), longitude_basis.astype(jnp.float32))
        return (reduced_total * scale).astype(jnp.bfloat16)
    return unblock(lax.map(one_block, row_blocks(lat_vals)))

def lat_analysis(lon_vals, doubled_rows):
    cos_tab, sin_tab = lat_basis(doubled_rows, jnp.arange(KLAT, dtype=jnp.int32))
    values = lon_vals.astype(jnp.float32)
    with_cos = jnp.einsum('ki,ipmc->kpmc', cos_tab.astype(jnp.float32), values)
    with_sin = jnp.einsum('ki,ipmc->kpmc', sin_tab.astype(jnp.float32), values)
    return jnp.stack([with_cos[:, 0] + with_sin[:, 1], with_cos[:, 1] - with_sin[:, 0]], axis=1)

def lat_synthesis(placed, doubled_rows):
    cos_tab, sin_tab = lat_basis(doubled_rows, jnp.arange(KLAT, dtype=jnp.int32))
    values = placed.astype(jnp.float32)
    with_cos = jnp.einsum('ki,kpmc->ipmc', cos_tab.astype(jnp.float32), values)
    with_sin = jnp.einsum('ki,kpmc->ipmc', sin_tab.astype(jnp.float32), values)
    return jnp.stack([with_cos[:, 0] - with_sin[:, 1], with_sin[:, 0] + with_cos[:, 1]], axis=1).astype(jnp.bfloat16)

def mix_forward(modes, weights):
    parts = modes.reshape(KEPT, 2, NB, BS)
    hp = lax.Precision.HIGHEST
    real_part = jnp.einsum('qbi,qbio->qbo', parts[:, 0], weights[:, 0], precision=hp) - jnp.einsum('qbi,qbio->qbo', parts[:, 1], weights[:, 1], precision=hp)
    imag_part = jnp.einsum('qbi,qbio->qbo', parts[:, 0], weights[:, 1], precision=hp) + jnp.einsum('qbi,qbio->qbo', parts[:, 1], weights[:, 0], precision=hp)
    return jnp.stack([real_part, imag_part], axis=1).reshape(KEPT, 2, C)

def mix_backward(grads, weights):
    parts = grads.reshape(KEPT, 2, NB, BS)
    hp = lax.Precision.HIGHEST
    real_part = jnp.einsum('qbo,qbio->qbi', parts[:, 0], weights[:, 0], precision=hp) + jnp.einsum('qbo,qbio->qbi', parts[:, 1], weights[:, 1], precision=hp)
    imag_part = jnp.einsum('qbo,qbio->qbi', parts[:, 1], weights[:, 0], precision=hp) - jnp.einsum('qbo,qbio->qbi', parts[:, 0], weights[:, 1], precision=hp)
    return jnp.stack([real_part, imag_part], axis=1).reshape(KEPT, 2, C)

def weight_gradient(modes, grads):
    left_part = modes.reshape(KEPT, 2, NB, BS)
    right_part = grads.reshape(KEPT, 2, NB, BS)
    hp = lax.Precision.HIGHEST
    real_part = jnp.einsum('qbi,qbo->qbio', left_part[:, 0], right_part[:, 0], precision=hp) + jnp.einsum('qbi,qbo->qbio', left_part[:, 1], right_part[:, 1], precision=hp)
    imag_part = jnp.einsum('qbi,qbo->qbio', left_part[:, 0], right_part[:, 1], precision=hp) - jnp.einsum('qbi,qbo->qbio', left_part[:, 1], right_part[:, 0], precision=hp)
    return jnp.stack([real_part, imag_part], axis=1).reshape(KEPT, 2, NB, BS * BS)

def mlp_backward(grid_out, out_grad, inner_weight, output_projection_weight):

    def one_block(tiles):
        tile_out, tile_grad = tiles
        pre_act = jnp.dot(tile_out.reshape(-1, C), inner_weight, preferred_element_type=jnp.float32)
        unused, pullback = jax.vjp(jax.nn.gelu, pre_act)
        hidden_grad = jnp.dot(tile_grad.reshape(-1, C), output_projection_weight.T, preferred_element_type=jnp.float32)
        pre_grad = pullback(hidden_grad)[0].astype(jnp.bfloat16)
        back = jnp.dot(pre_grad, inner_weight.T, preferred_element_type=jnp.float32).astype(jnp.bfloat16)
        return back.reshape(tile_out.shape)
    return unblock(lax.map(one_block, (row_blocks(grid_out), row_blocks(out_grad))))

def reference(in_field, out_grad, spec_weight, inner_weight, output_projection_weight, kept_modes):
    longitude_basis = make_lon_basis()
    top_rows = jnp.arange(NLAT, dtype=jnp.int32)
    lower_half_rows = 2 * NLAT - 1 - top_rows
    fwd_scale = 1.0 / math.sqrt(2 * NLAT * NLON)
    syn_scale = 1.0 / math.sqrt(KEPT)
    owner = jnp.arange(KEPT, dtype=jnp.int32) // KEEP_DEV
    wave_pos = owner // N_LON * KB + kept_modes // MB
    mode_pos = owner % N_LON * MB + kept_modes % MB
    turned = jnp.roll(in_field, -(NLON // 2), axis=1)
    spectrum = lat_analysis(lon_spectrum(in_field, longitude_basis), top_rows) + lat_analysis(lon_spectrum(turned, longitude_basis), lower_half_rows)
    spectrum = spectrum * fwd_scale
    modes_in = spectrum[wave_pos, :, mode_pos]
    weights = spec_weight.astype(jnp.float32).reshape(KEPT, 2, NB, BS, BS)
    mixed_modes = mix_forward(modes_in, weights).astype(jnp.bfloat16)
    placed = jnp.zeros((KLAT, 2, KM, C), jnp.bfloat16).at[wave_pos, :, mode_pos].set(mixed_modes)
    grid_out = lon_synthesis(lat_synthesis(placed, top_rows), longitude_basis, syn_scale)
    grid_grad = mlp_backward(grid_out, out_grad, inner_weight, output_projection_weight)
    back_spectrum = lat_analysis(lon_spectrum(grid_grad, longitude_basis), top_rows) * syn_scale
    modes_grad = back_spectrum[wave_pos, :, mode_pos]
    spectral_grad = weight_gradient(modes_in, modes_grad)
    mode_back = mix_backward(modes_grad, weights).astype(jnp.bfloat16)
    placed_back = jnp.zeros((KLAT, 2, KM, C), jnp.bfloat16).at[wave_pos, :, mode_pos].set(mode_back)
    upper_grid = lon_synthesis(lat_synthesis(placed_back, top_rows), longitude_basis, fwd_scale)
    lower_grid = lon_synthesis(lat_synthesis(placed_back, lower_half_rows), longitude_basis, fwd_scale)
    lower_turned = jnp.roll(lower_grid, -(NLON // 2), axis=1)
    spectral_part = (upper_grid.astype(jnp.float32) + lower_turned.astype(jnp.float32)).astype(jnp.bfloat16)
    input_grad = (out_grad.astype(jnp.float32) + spectral_part.astype(jnp.float32)).astype(jnp.bfloat16)
    return (input_grad, spectral_grad)
```

```python
import functools
import math

import jax
import jax.numpy as jnp
from jax import lax
from jax.experimental import pallas as pl
from jax.experimental.pallas import tpu as pltpu
from jax.sharding import PartitionSpec as P

BS = 16
KM = 64
KLAT = 128
RING = 4
STEPS = (2, 1, 3)
ROWS, LONS, CH, HID = 64, 45, 256, 1024
LONS_PAD = 48
LON_BLOCKS = 32
KEEP = 32
PIECES = ((48, "xyz"), (48, "yzx"), (32, "zxy"))
MESH = pl.DeviceIdType.MESH
F32, BF16 = jnp.float32, jnp.bfloat16
VMEM = pl.BlockSpec(memory_space=pltpu.VMEM)
LIMIT = 56 << 20
ROW_SPECTRA = [pltpu.VMEM((8192, 128), F32)] * 2


def matmul(a, b, contract=(1, 0)):
    dims = (((contract[0],), (contract[1],)), ((), ()))
    return lax.dot_general(a, b, dims, preferred_element_type=F32)


def own_place():
    lat, lon = lax.axis_index("lat"), lax.axis_index("lon")
    return {
        "x": lax.div(lon, 8),
        "y": lax.rem(lon, 4),
        "z": lax.rem(lax.div(lon, 4), 2) * 2 + lax.div(lat, 2),
        "core": lax.rem(lat, 2),
    }


def moved(at, axis, step):
    return {**at, axis: lax.rem(at[axis] + step, 2 if axis == "core" else RING)}


def device_of(at):
    return (lax.rem(at["z"], 2) * 2 + at["core"], at["x"] * 8 + lax.div(at["z"], 2) * 4 + at["y"])


def greet(at):
    partners = [moved(at, axis, step) for axis in "xyz" for step in STEPS] + [moved(at, "core", 1)]
    barrier = pltpu.get_barrier_semaphore()
    for partner in partners:
        pl.semaphore_signal(barrier, inc=1, device_id=device_of(partner), device_id_type=MESH)
    pl.semaphore_wait(barrier, len(partners))


def send(src, dst, sems, target):
    copy = pltpu.make_async_remote_copy(
        src_ref=src,
        dst_ref=dst,
        send_sem=sems[0],
        recv_sem=sems[1],
        device_id=device_of(target),
        device_id_type=MESH,
    )
    copy.start()
    return copy


def rows(start, size):
    return pl.ds(pl.multiple_of(start, math.gcd(size, 16)), size)


def gather_scratch(pieces):
    n = len(pieces)
    dma = pltpu.SemaphoreType.DMA
    return [dma((n, 3, 3)), dma((n, 3, 3)), dma((n, 4)), dma((n, 4))]


def gather(at, pieces, full, sems):
    ring_send, ring_recv, core_send, core_recv = sems
    bases = [at["core"] * (64 * size) for size, _ in pieces]
    pending = []
    sent = [None] * len(pieces)
    for phase in range(3):
        for i, (size, order) in enumerate(pieces):
            if sent[i]:
                for copy in sent[i]:
                    copy.wait_recv()
            axis = order[2 - phase]
            block = size * RING**phase
            index = 0
            for name in order[: 3 - phase]:
                index = index * RING + at[name]
            here = full[i].at[rows(bases[i] + index * block, block)]
            sent[i] = [
                send(
                    here,
                    here,
                    (ring_send.at[i, phase, s], ring_recv.at[i, phase, s]),
                    moved(at, axis, step),
                )
                for s, step in enumerate(STEPS)
            ]
            pending += sent[i]
    sibling = moved(at, "core", 1)
    across = []
    for s in range(4):
        for i, (size, order) in enumerate(pieces):
            if s:
                sent[i][(1, 2, 0)[s - 1]].wait_recv()
            step = (0, 3, 1, 2)[s]
            slab = lax.rem(at[order[0]] + step, RING)
            here = full[i].at[rows(bases[i] + slab * (16 * size), 16 * size)]
            across.append(send(here, here, (core_send.at[i, s], core_recv.at[i, s]), sibling))
    for copy in across:
        copy.wait_recv()
    for copy in pending + across:
        copy.wait_send()


def scatter_scratch():
    dma = pltpu.SemaphoreType.DMA
    scratch = [dma((3, 3, 3)), dma((3, 3, 3)), dma((3, 4)), dma((3, 4))]
    for size, _ in PIECES:
        scratch += [
            pltpu.VMEM((64 * size, 128), BF16),
            pltpu.VMEM((64 * size, 128), BF16),
            pltpu.VMEM((3, 16 * size, 128), BF16),
            pltpu.VMEM((16 * size, 128), BF16),
            pltpu.VMEM((3, 4 * size, 128), BF16),
            pltpu.VMEM((4 * size, 128), BF16),
            pltpu.VMEM((3, size, 128), BF16),
        ]
    return scratch


def reduce_scatter(at, parts, out, scratch):
    ring_send, ring_recv, core_send, core_recv = scratch[:4]
    bufs = [scratch[4 + 7 * i : 11 + 7 * i] for i in range(3)]
    sibling = moved(at, "core", 1)
    pending, across = [], {}
    for s, step in enumerate(STEPS + (0,)):
        for i, (size, order) in enumerate(PIECES):
            slab = lax.rem(at[order[0]] + step, RING) * (16 * size)
            across[s, i] = send(
                parts[i].at[rows((1 - at["core"]) * (64 * size) + slab, 16 * size)],
                bufs[i][0].at[rows(slab, 16 * size)],
                (core_send.at[i, s], core_recv.at[i, s]),
                sibling,
            )
    sent = [[], [], []]
    for s, step in enumerate(STEPS + (0,)):
        for i, (size, order) in enumerate(PIECES):
            slab = lax.rem(at[order[0]] + step, RING) * (16 * size)
            across[s, i].wait_recv()
            here = rows(slab, 16 * size)
            own = parts[i][rows(at["core"] * (64 * size) + slab, 16 * size), :]
            bufs[i][1][here, :] = (own.astype(F32) + bufs[i][0][here, :].astype(F32)).astype(BF16)
            if step:
                sent[i].append(
                    send(
                        bufs[i][1].at[here],
                        bufs[i][2].at[s],
                        (ring_send.at[i, 0, s], ring_recv.at[i, 0, s]),
                        moved(at, order[0], step),
                    )
                )
    for phase in range(3):
        for i, (size, order) in enumerate(PIECES):
            block = size * RING ** (2 - phase)
            mine, landed = bufs[i][1 + 2 * phase], bufs[i][2 + 2 * phase]
            total = mine[rows(at[order[phase]] * block, block), :].astype(F32)
            for s, copy in enumerate(sent[i]):
                copy.wait_recv()
                total = total + landed[s].astype(F32)
            pending += sent[i]
            if phase == 2:
                if i < 2:
                    out[0:48, 128 * i : 128 * i + 128] = total
                else:
                    out[48:64, 0:128] = total[0:16]
                    out[48:64, 128:256] = total[16:32]
                continue
            after = bufs[i][3 + 2 * phase]
            after[...] = total.astype(BF16)
            small = block // RING
            axis = order[phase + 1]
            sent[i] = [
                send(
                    after.at[rows(lax.rem(at[axis] + step, RING) * small, small)],
                    bufs[i][4 + 2 * phase].at[s],
                    (ring_send.at[i, phase + 1, s], ring_recv.at[i, phase + 1, s]),
                    moved(at, axis, step),
                )
                for s, step in enumerate(STEPS)
            ]
    for copy in pending + list(across.values()):
        copy.wait_send()


def piece_shapes():
    return [jax.ShapeDtypeStruct((128 * size, 128), BF16) for size, _ in PIECES]


def scatter_kernel(px, py, pz, out, *scratch):
    at = own_place()
    greet(at)
    reduce_scatter(at, (px, py, pz), out, scratch)


def scatter_call(parts):
    return pl.pallas_call(
        scatter_kernel,
        out_shape=jax.ShapeDtypeStruct((64, CH), F32),
        in_specs=[VMEM] * 3,
        out_specs=VMEM,
        scratch_shapes=scatter_scratch(),
        compiler_params=pltpu.CompilerParams(
            collective_id=0, has_side_effects=True, vmem_limit_bytes=LIMIT
        ),
        name="reduce_scatter",
    )(*parts)


def own_rows(at, size, order):
    index = 0
    for name in order:
        index = index * RING + at[name]
    return rows((at["core"] * 64 + index) * size, size)


def put_own(at, modes, full):
    for i, (size, order) in enumerate(PIECES):
        if i < 2:
            full[i][own_rows(at, size, order), :] = modes[0:48, 128 * i : 128 * i + 128]
        else:
            both = jnp.concatenate([modes[48:64, 0:128], modes[48:64, 128:256]], axis=0)
            full[i][own_rows(at, size, order), :] = both


def gather_kernel(modes, fx, fy, fz, *sems):
    at = own_place()
    put_own(at, modes, (fx, fy, fz))
    greet(at)
    gather(at, PIECES, (fx, fy, fz), sems)


def gather_call(modes):
    return pl.pallas_call(
        gather_kernel,
        out_shape=piece_shapes(),
        in_specs=[VMEM],
        out_specs=[VMEM] * 3,
        scratch_shapes=gather_scratch(PIECES),
        compiler_params=pltpu.CompilerParams(
            collective_id=1, has_side_effects=True, vmem_limit_bytes=LIMIT
        ),
        name="all_gather",
    )(modes)


KEPT_PIECE = ((8, "xyz"),)


def kept_kernel(kept, full, *sems):
    at = own_place()
    full[pl.ds(pl.multiple_of((at["core"] * 64 + (at["x"] * 4 + at["y"]) * 4 + at["z"]) * 8, 8), 8), :] = (
        jnp.broadcast_to(kept[...], (8, 128))
    )
    greet(at)
    gather(at, KEPT_PIECE, (full,), sems)


def kept_call(kept):
    return pl.pallas_call(
        kept_kernel,
        out_shape=jax.ShapeDtypeStruct((1024, 128), jnp.int32),
        in_specs=[VMEM],
        out_specs=VMEM,
        scratch_shapes=gather_scratch(KEPT_PIECE),
        compiler_params=pltpu.CompilerParams(collective_id=2, has_side_effects=True),
        name="gather_kept",
    )(kept)


def split_block(b):
    return {"x": lax.div(b, 8), "zhi": lax.rem(lax.div(b, 4), 2), "y": lax.rem(b, 4)}


def piece_start(b, lat, size, order):
    place = split_block(b)
    place["z"] = place["zhi"] * 2 + lat // 2
    index = 0
    for name in order:
        index = index * RING + place[name]
    return rows((lat % 2 * 64 + index) * size, size)


def one_hot(slots, b):
    ids = lax.broadcasted_iota(jnp.int32, (256, 128), 0)
    return jnp.where(ids == slots[pl.ds(b, 1), :], 1.0, 0.0).astype(BF16)


def put_row(halves, g, value):
    for i, half in enumerate(halves):
        half[pl.ds(g, 128, stride=ROWS), :] = value[:, 128 * i : 128 * i + 128]


def get_row(halves, g):
    return jnp.concatenate([half[pl.ds(g, 128, stride=ROWS), :] for half in halves], axis=1)


def put_block(halves, start, value):
    for i, half in enumerate(halves):
        half[pl.ds(start, 128), :] = value[:, 128 * i : 128 * i + 128]


def get_block(halves, start):
    return jnp.concatenate([half[pl.ds(start, 128), :] for half in halves], axis=1)


def analyse_latitude(rows_spec, slots, table, parts):
    def block(b, carry):
        start = pl.multiple_of(b * 256, 256)
        hot = one_hot(slots, b)
        dense = [
            matmul(table[mode], get_block(rows_spec, start + 128 * mode).astype(BF16)).astype(BF16)
            for mode in range(2)
        ]
        for part in range(2):
            both = jnp.concatenate([d[128 * part : 128 * part + 128] for d in dense], axis=0)
            modes = matmul(hot, both, (0, 0)).astype(BF16)
            for lat in range(4):
                tile = modes[32 * lat : 32 * lat + 32]
                px = parts[0].at[piece_start(b, lat, 48, "xyz")]
                py = parts[1].at[piece_start(b, lat, 48, "yzx")]
                pz = parts[2].at[piece_start(b, lat, 32, "zxy")]
                if part == 0:
                    px[0:32, :] = tile[:, 0:128]
                    py[0:32, :] = tile[:, 128:256]
                else:
                    px[32:48, :] = tile[0:16, 0:128]
                    py[32:48, :] = tile[0:16, 128:256]
                    pz[0:16, :] = tile[16:32, 0:128]
                    pz[16:32, :] = tile[16:32, 128:256]
        return carry

    lax.fori_loop(0, LON_BLOCKS, block, 0)


def synthesise_latitude(full, slots, table, rows_spec):
    def block(b, carry):
        start = pl.multiple_of(b * 256, 256)
        hot = one_hot(slots, b)
        tiles = [[], []]
        for lat in range(4):
            px = full[0][piece_start(b, lat, 48, "xyz"), :]
            py = full[1][piece_start(b, lat, 48, "yzx"), :]
            pz = full[2][piece_start(b, lat, 32, "zxy"), :]
            tiles[0].append(jnp.concatenate([px[0:32], py[0:32]], axis=1))
            tiles[1].append(
                jnp.concatenate(
                    [
                        jnp.concatenate([px[32:48], py[32:48]], axis=1),
                        jnp.concatenate([pz[0:16], pz[16:32]], axis=1),
                    ],
                    axis=0,
                )
            )
        placed = [
            matmul(hot, jnp.concatenate(tiles[part], axis=0)).astype(BF16) for part in range(2)
        ]
        for mode in range(2):
            both = jnp.concatenate([p[128 * mode : 128 * mode + 128] for p in placed], axis=0)
            put_block(rows_spec, start + 128 * mode, matmul(table[mode], both))
        return carry

    lax.fori_loop(0, LON_BLOCKS, block, 0)


def forward_kernel(field, slots, table, basis, px, py, pz, *rows_spec):
    def row(g, carry):
        put_row(rows_spec, g, matmul(basis[:, 0:LONS], field[g]))
        return carry

    lax.fori_loop(0, ROWS, row, 0)
    analyse_latitude(rows_spec, slots, table, (px, py, pz))


def forward_call(field, slots, table, basis):
    return pl.pallas_call(
        forward_kernel,
        out_shape=piece_shapes(),
        in_specs=[VMEM] * 4,
        out_specs=[VMEM] * 3,
        scratch_shapes=ROW_SPECTRA,
        compiler_params=pltpu.CompilerParams(vmem_limit_bytes=LIMIT),
        name="forward",
    )(field, slots, table, basis)


def gelu_slope(x):
    c, a = math.sqrt(2.0 / math.pi), 0.044715
    square = x * x
    t = jnp.tanh(x * (c + (c * a) * square))
    half = 0.5 + 0.5 * t
    return half + x * (half * (1.0 - t)) * (c + (3.0 * c * a) * square)


GROUP = 8


def middle_kernel(
    fx, fy, fz, out_grad, slots, table, table_back, basis, basis_back, w1, w2, px, py, pz, grads, grid, *rows_spec
):
    grads[:, LONS:LONS_PAD, :] = jnp.zeros((ROWS, LONS_PAD - LONS, CH), BF16)
    grads[:, 0:LONS, :] = out_grad[...]
    synthesise_latitude((fx, fy, fz), slots, table_back, rows_spec)

    def row(g, carry):
        spec = get_row(rows_spec, g).astype(BF16)
        grid[g] = matmul(basis_back[...], spec).astype(BF16)
        return carry

    lax.fori_loop(0, ROWS, row, 0)

    def points(i, carry):
        here = pl.ds(i * GROUP, GROUP)
        value = grid[here].reshape(GROUP * LONS_PAD, CH)
        grad = grads[here].reshape(GROUP * LONS_PAD, CH)
        total = jnp.zeros((GROUP * LONS_PAD, CH), F32)
        for k in range(HID // 256):
            cols = slice(256 * k, 256 * k + 256)
            pre = matmul(value, w1[:, cols])
            hidden = matmul(grad, w2[cols, :], (1, 1))
            pre_grad = (gelu_slope(pre) * hidden).astype(BF16)
            total = total + matmul(pre_grad, w1[:, cols], (1, 1))
        grid[here] = total.astype(BF16).reshape(GROUP, LONS_PAD, CH)
        return carry

    lax.fori_loop(0, ROWS // GROUP, points, 0)

    def back(g, carry):
        put_row(rows_spec, g, matmul(basis[...], grid[g]))
        return carry

    lax.fori_loop(0, ROWS, back, 0)
    analyse_latitude(rows_spec, slots, table, (px, py, pz))


def middle_call(full, out_grad, slots, table, table_back, basis, basis_back, w1, w2):
    return pl.pallas_call(
        middle_kernel,
        out_shape=piece_shapes(),
        in_specs=[VMEM] * 11,
        out_specs=[VMEM] * 3,
        scratch_shapes=[
            pltpu.VMEM((ROWS, LONS_PAD, CH), BF16),
            pltpu.VMEM((ROWS, LONS_PAD, CH), BF16),
            *ROW_SPECTRA,
        ],
        compiler_params=pltpu.CompilerParams(vmem_limit_bytes=LIMIT),
        name="middle",
    )(*full, out_grad, slots, table, table_back, basis, basis_back, w1, w2)


def last_kernel(scale, fx, fy, fz, out_grad, slots, table_back, basis_back, out, *rows_spec):
    synthesise_latitude((fx, fy, fz), slots, table_back, rows_spec)

    def row(g, carry):
        spec = get_row(rows_spec, g).astype(BF16)
        part = (matmul(basis_back[...], spec) * scale)[0:LONS]
        out[g] = (out_grad[g].astype(F32) + part).astype(BF16)
        return carry

    lax.fori_loop(0, ROWS, row, 0)


def last_call(scale, full, out_grad, slots, table_back, basis_back):
    return pl.pallas_call(
        functools.partial(last_kernel, scale),
        out_shape=jax.ShapeDtypeStruct((ROWS, LONS, CH), BF16),
        in_specs=[VMEM] * 7,
        out_specs=VMEM,
        scratch_shapes=ROW_SPECTRA,
        compiler_params=pltpu.CompilerParams(vmem_limit_bytes=LIMIT),
        name="last",
    )(*full, out_grad, slots, table_back, basis_back)


def longitude_tables(lon_rank, lon_total):
    lon_ids = lon_rank * LONS + jnp.arange(LONS_PAD, dtype=jnp.int32)
    q = jnp.arange(2 * KM, dtype=jnp.int32)
    mode, part = q // 2, q % 2
    phases = lon_ids[None, :] * mode[:, None] % lon_total
    angles = phases.astype(F32) * (2.0 * math.pi / lon_total)
    basis = jnp.where(part[:, None] == 0, jnp.cos(angles), -jnp.sin(angles))
    basis = jnp.where(jnp.arange(LONS_PAD)[None, :] < LONS, basis, 0.0).astype(BF16)
    return basis, basis.T


def latitude_tables(row_ids, lat_total):
    wave = jnp.arange(KLAT, dtype=jnp.int32) - KLAT // 2

    def angles(ids):
        phases = jnp.mod(wave[:, None] * ids[None, :], 2 * lat_total)
        return phases.astype(F32) * (math.pi / lat_total)

    upper, lower = angles(row_ids), angles(2 * lat_total - 1 - row_ids)
    cu, su, cl, sl = jnp.cos(upper), jnp.sin(upper), jnp.cos(lower), jnp.sin(lower)

    def table(c, s):
        return jnp.concatenate(
            [jnp.concatenate([c, s], axis=1), jnp.concatenate([-s, c], axis=1)], axis=0
        )

    plain = table(cu, su)
    doubled = jnp.stack([table(cu + cl, su + sl), table(cu - cl, su - sl)])
    return jnp.stack([plain, plain]).astype(BF16), doubled.astype(BF16)


def body(in_field, out_grad, spec_weight, inner_weight, output_projection_weight, kept_modes):
    lat_parts, lon_parts = lax.axis_size("lat"), lax.axis_size("lon")
    lat_total, lon_total = ROWS * lat_parts, LONS * lon_parts
    fwd_scale = 1.0 / math.sqrt(2 * lat_total * lon_total)
    syn_scale = 1.0 / math.sqrt(KEEP * lat_parts * lon_parts)
    highest = lax.Precision.HIGHEST
    lat_rank, lon_rank = lax.axis_index("lat"), lax.axis_index("lon")

    kept = kept_call(jnp.pad(kept_modes, (0, 128 - KEEP)).reshape(1, 128))
    kept = kept.reshape(2, 4, 4, 2, 2, 8, 128)[..., 0, :KEEP]
    kept = jnp.transpose(kept, (1, 3, 2, 4, 0, 5)).reshape(LON_BLOCKS, 4, KEEP)
    lat_base = jnp.arange(4, dtype=jnp.int32)[None, :, None] * 32
    slots = (kept % 2 * KLAT + lat_base + kept // 2).reshape(LON_BLOCKS, 4 * KEEP)

    basis, basis_back = longitude_tables(lon_rank, lon_total)
    plain, doubled = latitude_tables(
        lat_rank * ROWS + jnp.arange(ROWS, dtype=jnp.int32), lat_total
    )
    plain_back, doubled_back = jnp.swapaxes(plain, 1, 2), jnp.swapaxes(doubled, 1, 2)

    modes_in = scatter_call(forward_call(in_field, slots, doubled, basis)) * fwd_scale
    xr, xi = modes_in.reshape(2, KEEP, CH // BS, BS)
    weights = spec_weight.astype(F32).reshape(KEEP, 2, CH // BS, BS, BS)
    wr, wi = weights[:, 0], weights[:, 1]

    def mix(a, b):
        return jnp.einsum("qbi,qbio->qbo", a, b, precision=highest)

    mixed = jnp.stack([mix(xr, wr) - mix(xi, wi), mix(xr, wi) + mix(xi, wr)])
    mixed = mixed.reshape(2 * KEEP, CH).astype(BF16)

    scaled_back = (basis_back.astype(F32) * syn_scale).astype(BF16)
    parts = middle_call(
        gather_call(mixed),
        out_grad,
        slots,
        plain,
        plain_back,
        basis,
        scaled_back,
        inner_weight,
        output_projection_weight,
    )
    modes_grad = scatter_call(parts) * syn_scale
    gr, gi = modes_grad.reshape(2, KEEP, CH // BS, BS)

    def mix_back(a, b):
        return jnp.einsum("qbo,qbio->qbi", a, b, precision=highest)

    back = jnp.stack([mix_back(gr, wr) + mix_back(gi, wi), mix_back(gi, wr) - mix_back(gr, wi)])
    back = back.reshape(2 * KEEP, CH).astype(BF16)
    input_grad = last_call(
        fwd_scale, gather_call(back), out_grad, slots, doubled_back, basis_back
    )

    def outer(a, b):
        return a[:, :, :, None] * b[:, :, None, :]

    spectral_grad = jnp.stack(
        [outer(xr, gr) + outer(xi, gi), outer(xr, gi) - outer(xi, gr)], axis=1
    ).reshape(KEEP, 2, CH // BS, BS * BS)
    return input_grad, spectral_grad


def solution(mesh):
    return jax.shard_map(
        body,
        mesh=mesh,
        in_specs=(
            P("lat", "lon", None),
            P("lat", "lon", None),
            P(("lat", "lon"), None, None, None),
            P(),
            P(),
            P(("lat", "lon")),
        ),
        out_specs=(P("lat", "lon", None), P(("lat", "lon"), None, None, None)),
        check_vma=False,
    )
```

```python
import functools
import math

import jax
import jax.numpy as jnp
import numpy as np
from jax import lax
from jax.experimental import pallas as pl
from jax.experimental.pallas import tpu as pltpu
from jax.sharding import PartitionSpec as P

BS = 16
KM = 64
KLAT = 128
RING = 4
STEPS = (2, 1, 3)
ROWS, LONS, CH, HID = 64, 45, 256, 1024
LONS_PAD = 48
LON_BLOCKS = 32
KEEP = 32
PIECES = ((48, "xyz"), (48, "yzx"), (32, "zxy"))
MESH = pl.DeviceIdType.MESH
F32, BF16 = jnp.float32, jnp.bfloat16
VMEM = pl.BlockSpec(memory_space=pltpu.VMEM)
LIMIT = 60 << 20
U_FILL, U_ROW, U_BLK, GROUP, CHUNK = 5, 16, 8, 9, 256


def matmul(a, b, contract=(1, 0)):
    dims = (((contract[0],), (contract[1],)), ((), ()))
    return lax.dot_general(a, b, dims, preferred_element_type=F32)


def own_place():
    lat, lon = lax.axis_index("lat"), lax.axis_index("lon")
    return {
        "x": lax.div(lon, 8),
        "y": lax.rem(lon, 4),
        "z": lax.rem(lax.div(lon, 4), 2) * 2 + lax.div(lat, 2),
        "core": lax.rem(lat, 2),
    }


def moved(at, axis, step):
    return {**at, axis: lax.rem(at[axis] + step, 2 if axis == "core" else RING)}


def device_of(at):
    return (lax.rem(at["z"], 2) * 2 + at["core"], at["x"] * 8 + lax.div(at["z"], 2) * 4 + at["y"])


def greet(at):
    partners = [moved(at, axis, step) for axis in "xyz" for step in STEPS] + [moved(at, "core", 1)]
    for partner in partners:
        pl.semaphore_signal(
            pltpu.get_barrier_semaphore(),
            inc=1,
            device_id=device_of(partner),
            device_id_type=MESH,
        )
    return len(partners)


def send(src, dst, sems, target):
    copy = pltpu.make_async_remote_copy(
        src_ref=src,
        dst_ref=dst,
        send_sem=sems[0],
        recv_sem=sems[1],
        device_id=device_of(target),
        device_id_type=MESH,
    )
    copy.start()
    return copy


def rows(start, size):
    return pl.ds(pl.multiple_of(start, math.gcd(size, 16)), size)


def index_of(at, order):
    index = 0
    for name in order:
        index = index * RING + at[name]
    return index


def gather_sems(pieces):
    n, dma = len(pieces), pltpu.SemaphoreType.DMA
    return [dma((n, 3, 3)), dma((n, 3, 3)), dma((n, 4)), dma((n, 4))]


def gather(at, pieces, full, sems):
    ring_send, ring_recv, core_send, core_recv = sems
    bases = [at["core"] * (64 * size) for size, _ in pieces]
    sibling = moved(at, "core", 1)
    pending, across = [], []
    sent = [[] for _ in pieces]

    def across_core(i, s, step):
        size, order = pieces[i]
        slab = lax.rem(at[order[0]] + step, RING)
        here = full[i].at[rows(bases[i] + slab * (16 * size), 16 * size)]
        across.append(send(here, here, (core_send.at[i, s], core_recv.at[i, s]), sibling))

    for phase in range(3):
        for i, (size, order) in enumerate(pieces):
            for copy in sent[i]:
                copy.wait_recv()
            block = size * RING**phase
            index = index_of(at, order[: 3 - phase])
            here = full[i].at[rows(bases[i] + index * block, block)]
            sent[i] = [
                send(
                    here,
                    here,
                    (ring_send.at[i, phase, s], ring_recv.at[i, phase, s]),
                    moved(at, order[2 - phase], step),
                )
                for s, step in enumerate(STEPS)
            ]
            pending += sent[i]
            if phase == 2:
                across_core(i, 0, 0)
        yield
    for s in (1, 2, 0):
        for i in range(len(pieces)):
            sent[i][s].wait_recv()
            across_core(i, s + 1, RING - STEPS[s])
    for copy in across:
        copy.wait_recv()
    for copy in pending + across:
        copy.wait_send()


def scatter_scratch():
    dma = pltpu.SemaphoreType.DMA
    scratch = [dma((3, 3, 3)), dma((3, 3, 3)), dma((3, 4)), dma((3, 4))]
    for size, _ in PIECES:
        scratch += [
            pltpu.VMEM((64 * size, 128), BF16),
            pltpu.VMEM((64 * size, 128), BF16),
            pltpu.VMEM((3, 16 * size, 128), BF16),
            pltpu.VMEM((16 * size, 128), BF16),
            pltpu.VMEM((3, 4 * size, 128), BF16),
            pltpu.VMEM((4 * size, 128), BF16),
            pltpu.VMEM((3, size, 128), BF16),
        ]
    return scratch


def reduce_scatter(at, parts, scale, out, scratch):
    ring_send, ring_recv, core_send, core_recv = scratch[:4]
    bufs = [scratch[4 + 7 * i : 11 + 7 * i] for i in range(3)]
    sibling = moved(at, "core", 1)
    pending, across = [], {}
    for s, step in enumerate(STEPS + (0,)):
        for i, (size, order) in enumerate(PIECES):
            slab = lax.rem(at[order[0]] + step, RING) * (16 * size)
            across[s, i] = send(
                parts[i].at[rows((1 - at["core"]) * (64 * size) + slab, 16 * size)],
                bufs[i][0].at[rows(slab, 16 * size)],
                (core_send.at[i, s], core_recv.at[i, s]),
                sibling,
            )
    sent = [[], [], []]
    for s, step in enumerate(STEPS + (0,)):
        for i, (size, order) in enumerate(PIECES):
            slab = lax.rem(at[order[0]] + step, RING) * (16 * size)
            across[s, i].wait_recv()
            here = rows(slab, 16 * size)
            own = parts[i][rows(at["core"] * (64 * size) + slab, 16 * size), :]
            bufs[i][1][here, :] = (own.astype(F32) + bufs[i][0][here, :].astype(F32)).astype(BF16)
            if step:
                sent[i].append(
                    send(
                        bufs[i][1].at[here],
                        bufs[i][2].at[s],
                        (ring_send.at[i, 0, s], ring_recv.at[i, 0, s]),
                        moved(at, order[0], step),
                    )
                )
    yield
    for phase in range(3):
        for i, (size, order) in enumerate(PIECES):
            block = size * RING ** (2 - phase)
            mine, landed = bufs[i][1 + 2 * phase], bufs[i][2 + 2 * phase]
            total = mine[rows(at[order[phase]] * block, block), :].astype(F32)
            for s, copy in enumerate(sent[i]):
                copy.wait_recv()
                total = total + landed[s].astype(F32)
            pending += sent[i]
            if phase == 2:
                total = total * scale
                if i < 2:
                    out[0:48, 128 * i : 128 * i + 128] = total
                else:
                    out[48:64, 0:128] = total[0:16]
                    out[48:64, 128:256] = total[16:32]
                continue
            after = bufs[i][3 + 2 * phase]
            after[...] = total.astype(BF16)
            small = block // RING
            axis = order[phase + 1]
            sent[i] = [
                send(
                    after.at[rows(lax.rem(at[axis] + step, RING) * small, small)],
                    bufs[i][4 + 2 * phase].at[s],
                    (ring_send.at[i, phase + 1, s], ring_recv.at[i, phase + 1, s]),
                    moved(at, axis, step),
                )
                for s, step in enumerate(STEPS)
            ]
        if phase < 2:
            yield
    for copy in pending + list(across.values()):
        copy.wait_send()


def run(steps, *between):
    work = list(between)
    for _ in steps:
        if work:
            work.pop(0)()


def put_own(at, modes, full):
    for i, (size, order) in enumerate(PIECES):
        here = rows((at["core"] * 64 + index_of(at, order)) * size, size)
        if i < 2:
            full[i][here, :] = modes[0:48, 128 * i : 128 * i + 128]
        else:
            full[i][here, :] = jnp.concatenate(
                [modes[48:64, 0:128], modes[48:64, 128:256]], axis=0
            )


def split_block(b):
    return {"x": lax.div(b, 8), "zhi": lax.rem(lax.div(b, 4), 2), "y": lax.rem(b, 4)}


def piece_start(b, lat, size, order):
    place = split_block(b)
    place["z"] = place["zhi"] * 2 + lat // 2
    index = 0
    for name in order:
        index = index * RING + place[name]
    return rows((lat % 2 * 64 + index) * size, size)


def put(halves, where, value):
    for i, half in enumerate(halves):
        half[where, :] = value[:, 128 * i : 128 * i + 128]


def get(halves, where):
    return jnp.concatenate([half[where, :] for half in halves], axis=1)


def one_hot(slots, b):
    ids = lax.broadcasted_iota(jnp.int32, (256, 128), 0).astype(F32)
    return jnp.where(ids == slots[pl.ds(b, 1), :], 1.0, 0.0).astype(BF16)


def one_hot_turned(slots, b):
    columns = jnp.transpose(jnp.broadcast_to(slots[pl.ds(b, 1), :], (128, 128)))
    ids = lax.broadcasted_iota(jnp.int32, (128, 128), 1).astype(F32)
    hot = [jnp.where(ids == columns - 128.0 * mode, 1.0, 0.0).astype(BF16) for mode in range(2)]
    return jnp.concatenate(hot, axis=1)


def fill_points(field, points):
    def one(j, carry):
        put(points, pl.ds(pl.multiple_of(j * ROWS, ROWS), ROWS), field[j].astype(F32))
        return carry

    lax.fori_loop(0, LONS, one, 0, unroll=U_FILL)
    tail = pl.ds(LONS * ROWS, (LONS_PAD - LONS) * ROWS)
    put(points, tail, jnp.zeros(((LONS_PAD - LONS) * ROWS, CH), F32))


def analyse_longitude(points, basis, rows_spec):
    def one(g, carry):
        value = get(points, pl.ds(g, LONS_PAD, stride=ROWS)).astype(BF16)
        put(rows_spec, pl.ds(g, 2 * KM, stride=ROWS), matmul(basis[...], value))
        return carry

    lax.fori_loop(0, ROWS, one, 0, unroll=U_ROW)


def synthesise_longitude(rows_spec, basis_back, points, scale):
    def one(g, carry):
        spec = get(rows_spec, pl.ds(g, 2 * KM, stride=ROWS)).astype(BF16)
        put(points, pl.ds(g, LONS_PAD, stride=ROWS), matmul(basis_back[...], spec) * scale)
        return carry

    lax.fori_loop(0, ROWS, one, 0, unroll=U_ROW)


def spec_block(b, size=256):
    return pl.ds(pl.multiple_of(b * size, size), size)


def analyse_dense(rows_spec, table, dense):
    def one(b, carry):
        value = get(rows_spec, spec_block(b)).astype(BF16)
        for mode in range(2):
            full = matmul(table[mode], value[128 * mode : 128 * mode + 128]).astype(BF16)
            for part in range(2):
                start = pl.multiple_of(b * 512 + part * 256 + mode * 128, 128)
                dense[pl.ds(start, 128), :] = full[128 * part : 128 * part + 128]
        return carry

    lax.fori_loop(0, LON_BLOCKS, one, 0, unroll=U_BLK)


def store_modes(b, part, modes, parts):
    for lat in range(4):
        tile = modes[32 * lat : 32 * lat + 32]
        px = parts[0].at[piece_start(b, lat, 48, "xyz")]
        py = parts[1].at[piece_start(b, lat, 48, "yzx")]
        pz = parts[2].at[piece_start(b, lat, 32, "zxy")]
        if part == 0:
            px[0:32, :] = tile[:, 0:128]
            py[0:32, :] = tile[:, 128:256]
        else:
            px[32:48, :] = tile[0:16, 0:128]
            py[32:48, :] = tile[0:16, 128:256]
            pz[0:16, :] = tile[16:32, 0:128]
            pz[16:32, :] = tile[16:32, 128:256]


def load_modes(b, full):
    tiles = [[], []]
    for lat in range(4):
        px = full[0][piece_start(b, lat, 48, "xyz"), :]
        py = full[1][piece_start(b, lat, 48, "yzx"), :]
        pz = full[2][piece_start(b, lat, 32, "zxy"), :]
        tiles[0].append(jnp.concatenate([px[0:32], py[0:32]], axis=1))
        tiles[1].append(jnp.concatenate([px[32:48], py[32:48]], axis=1))
        tiles[1].append(jnp.concatenate([pz[0:16], pz[16:32]], axis=1))
    return jnp.concatenate(tiles[0] + tiles[1], axis=0)


def select_modes(dense, slots, parts):
    def one(b, carry):
        hot = one_hot_turned(slots, b)
        for part in range(2):
            modes = matmul(hot, dense[pl.ds(pl.multiple_of(b * 512 + part * 256, 256), 256), :])
            store_modes(b, part, modes.astype(BF16), parts)
        return carry

    lax.fori_loop(0, LON_BLOCKS, one, 0, unroll=U_BLK)


def build_analysis(slots, table, out, low, high):
    def one(b, carry):
        hot = one_hot_turned(slots, b)
        for part in range(2):
            for mode in range(2):
                value = matmul(
                    hot[:, 128 * mode : 128 * mode + 128],
                    table[mode, 128 * part : 128 * part + 128, :],
                )
                start = pl.multiple_of(b * 256 + part * 128, 128)
                out[pl.ds(start, 128), 128 * mode : 128 * mode + 128] = value.astype(BF16)
        return carry

    lax.fori_loop(low, high, one, 0, unroll=U_BLK)


def build_synthesis(slots, table, out, low, high):
    def one(b, carry):
        hot = one_hot(slots, b)
        for part in range(2):
            for mode in range(2):
                value = matmul(
                    table[mode, :, 128 * part : 128 * part + 128],
                    hot[128 * mode : 128 * mode + 128],
                )
                start = pl.multiple_of(b * 256 + mode * 128, 128)
                out[pl.ds(start, 128), 128 * part : 128 * part + 128] = value.astype(BF16)
        return carry

    lax.fori_loop(low, high, one, 0, unroll=U_BLK)


def analyse_latitude(rows_spec, table, parts):
    def one(b, carry):
        value = get(rows_spec, spec_block(b)).astype(BF16)
        modes = matmul(table[spec_block(b), :], value).astype(BF16)
        for part in range(2):
            store_modes(b, part, modes[128 * part : 128 * part + 128], parts)
        return carry

    lax.fori_loop(0, LON_BLOCKS, one, 0, unroll=U_BLK)


def synthesise_latitude(full, table, rows_spec):
    def one(b, carry):
        put(rows_spec, spec_block(b), matmul(table[spec_block(b), :], load_modes(b, full)))
        return carry

    lax.fori_loop(0, LON_BLOCKS, one, 0, unroll=U_BLK)


def gelu_slope(x):
    c, a = math.sqrt(2.0 / math.pi), 0.044715
    square = x * x
    t = jnp.tanh(x * (c + (c * a) * square))
    half = 0.5 + 0.5 * t
    return half + x * (half * (1.0 - t)) * (c + (3.0 * c * a) * square)


def hidden_gradient(out_grad, w2, hidden, low, high):
    def one(i, carry):
        grad = out_grad[pl.ds(i * GROUP, GROUP)].reshape(GROUP * ROWS, CH)
        here = pl.ds(pl.multiple_of(i * (GROUP * ROWS), GROUP * ROWS), GROUP * ROWS)
        for k in range(HID // CHUNK):
            cols = slice(CHUNK * k, CHUNK * k + CHUNK)
            hidden[here, cols] = matmul(grad, w2[cols, :], (1, 1)).astype(BF16)
        return carry

    lax.fori_loop(low, high, one, 0)


def pointwise(points, hidden, w1, low, high):
    def one(i, carry):
        here = pl.ds(pl.multiple_of(i * (GROUP * ROWS), GROUP * ROWS), GROUP * ROWS)
        value = get(points, here).astype(BF16)
        total = None
        for k in range(HID // CHUNK):
            cols = slice(CHUNK * k, CHUNK * k + CHUNK)
            pre = matmul(value, w1[:, cols])
            pre_grad = (gelu_slope(pre) * hidden[here, cols].astype(F32)).astype(BF16)
            term = matmul(pre_grad, w1[:, cols], (1, 1))
            total = term if total is None else total + term
        put(points, here, total)
        return carry

    lax.fori_loop(low, high, one, 0)


def lane_match(spread_high):
    channel = lax.broadcasted_iota(jnp.int32, (CH, CH), 0) & (BS - 1)
    lane = lax.broadcasted_iota(jnp.int32, (CH, CH), 1)
    half = lax.shift_right_logical(lane, 4) if spread_high else lane & (BS - 1)
    return jnp.where(channel == half, 1.0, 0.0).astype(BF16)


def lane_sum(over_low):
    lane = lax.broadcasted_iota(jnp.int32, (CH, CH), 0)
    channel = lax.broadcasted_iota(jnp.int32, (CH, CH), 1) & (BS - 1)
    half = lax.shift_right_logical(lane, 4) if over_low else lane & (BS - 1)
    return jnp.where(channel == half, 1.0, 0.0).astype(BF16)


def block_mask():
    beta = lax.broadcasted_iota(jnp.int32, (CH // BS, CH), 0)
    channel = lax.broadcasted_iota(jnp.int32, (CH // BS, CH), 1)
    return jnp.where(beta == lax.shift_right_logical(channel, 4), 1.0, 0.0)


def exact(value, ones):
    high = value.astype(BF16)
    low = (value - high.astype(F32)).astype(BF16)
    return matmul(high, ones) + matmul(low, ones)


MIX = 8


def spread(modes, match, out):
    mask = block_mask()[None]

    def one(i, carry):
        value = modes[pl.ds(pl.multiple_of(i * MIX, MIX), MIX), :]
        wide = (value[:, None, :] * mask).reshape(MIX * BS, CH)
        out[pl.ds(pl.multiple_of(i * (MIX * BS), MIX * BS), MIX * BS), :] = exact(wide, match)
        return carry

    lax.fori_loop(0, 2 * KEEP // MIX, one, 0, unroll=2)


def spread_rows(i, part):
    return pl.ds(pl.multiple_of(part * (KEEP * BS) + i * (MIX * BS), MIX * BS), MIX * BS)


def mix(wide, weight, conjugate, sums, out):
    mask = block_mask()[None]

    def one(i, carry):
        re, im = wide[spread_rows(i, 0), :], wide[spread_rows(i, 1), :]
        wr, wi = (
            weight[pl.ds(i * MIX, MIX), part].astype(F32).reshape(MIX * BS, CH) for part in range(2)
        )
        if conjugate:
            terms = re * wr + im * wi, im * wr - re * wi
        else:
            terms = re * wr - im * wi, re * wi + im * wr
        for part, term in enumerate(terms):
            total = exact(term, sums).reshape(MIX, BS, CH) * mask
            start = pl.multiple_of(part * KEEP + i * MIX, MIX)
            out[pl.ds(start, MIX), :] = jnp.sum(total, axis=1)
        return carry

    lax.fori_loop(0, KEEP // MIX, one, 0, unroll=2)


def weight_gradient(wide_in, wide_grad, out):
    def one(i, carry):
        ar, ai = wide_in[spread_rows(i, 0), :], wide_in[spread_rows(i, 1), :]
        br, bi = wide_grad[spread_rows(i, 0), :], wide_grad[spread_rows(i, 1), :]
        here = pl.ds(i * MIX, MIX)
        out[here, 0] = (ar * br + ai * bi).reshape(MIX, BS, CH)
        out[here, 1] = (ar * bi - ai * br).reshape(MIX, BS, CH)
        return carry

    lax.fori_loop(0, KEEP // MIX, one, 0)


KEPT_PIECE = ((8, "xyz"),)


def own_slots(at, kept):
    lat = lax.rem(at["z"], 2) * 2 + at["core"]
    value = jnp.concatenate([kept[...]] * 4, axis=1)
    slot = (value & 1) * KLAT + lat * KEEP + lax.shift_right_logical(value, 1)
    lane = lax.broadcasted_iota(jnp.int32, (1, 128), 1)
    return jnp.where(lax.shift_right_logical(lane, 5) == lat, slot.astype(F32), 0.0)


def collect_slots(full, slots):
    for b in range(LON_BLOCKS):
        x, zhi, y = b // 8, b // 4 % 2, b % 4
        first = ((x * 4 + y) * 4 + zhi * 2) * 8
        total = full[first : first + 8, :]
        for start in (first + 8, first + 512, first + 520):
            total = total + full[start : start + 8, :]
        slots[b : b + 1, :] = total[0:1]


def kernel(
    fwd_scale,
    syn_scale,
    field,
    out_grad_hbm,
    weight_hbm,
    w1_hbm,
    w2_hbm,
    kept,
    basis_hbm,
    back_hbm,
    plain_hbm,
    doubled_hbm,
    plain_back_hbm,
    doubled_back_hbm,
    input_grad,
    spectral_grad,
    *scratch,
):
    scratch = list(scratch)

    def take(n):
        taken = scratch[:n]
        del scratch[:n]
        return taken

    out_grad, weight, w1, w2, basis, basis_back, plain, doubled, plain_back, doubled_back = take(10)
    (load_sems,) = take(1)
    points, rows_spec, parts, full = take(2), take(2), take(3), take(3)
    tables, hidden, slots, kept_full, modes, mixed, wide_in, wide_grad = take(8)
    kept_sems, full_sems, scatter = take(4), take(4), scratch
    analysis, synthesis = tables.at[0:8192], tables.at[8192:16384]

    at = own_place()
    lat, lon = lax.axis_index("lat"), lax.axis_index("lon")
    greeted = greet(at)
    loads = []
    for i, (src, dst) in enumerate(
        [
            (basis_hbm.at[lon], basis),
            (doubled_hbm.at[lat], doubled),
            (plain_hbm.at[lat], plain),
            (plain_back_hbm.at[lat], plain_back),
            (weight_hbm, weight),
            (w2_hbm, w2),
            (out_grad_hbm, out_grad),
            (back_hbm.at[lon], basis_back),
            (w1_hbm, w1),
            (doubled_back_hbm.at[lat], doubled_back),
        ]
    ):
        copy = pltpu.make_async_copy(src, dst, load_sems.at[i])
        copy.start()
        loads.append(copy)
    here = rows((at["core"] * 64 + index_of(at, "xyz")) * 8, 8)
    kept_full[here, :] = jnp.broadcast_to(own_slots(at, kept), (8, 128))
    fill_points(field, points)
    pl.semaphore_wait(pltpu.get_barrier_semaphore(), greeted)

    def first_longitude():
        loads[0].wait()
        analyse_longitude(points, basis, rows_spec)

    def first_dense():
        loads[1].wait()
        analyse_dense(rows_spec, doubled, tables)

    run(gather(at, KEPT_PIECE, (kept_full,), kept_sems), first_longitude, first_dense)
    collect_slots(kept_full, slots)
    select_modes(tables, slots, parts)

    def wait_tables():
        for copy in loads[2:]:
            copy.wait()

    def build(table, turned, out, low, high):
        (build_analysis if turned else build_synthesis)(slots, table, out, low, high)

    def work_a():
        wait_tables()
        build(plain, True, analysis, 0, LON_BLOCKS)

    run(
        reduce_scatter(at, parts, fwd_scale, modes, scatter),
        work_a,
        lambda: build(plain_back, False, synthesis, 0, LON_BLOCKS // 2),
        lambda: build(plain_back, False, synthesis, LON_BLOCKS // 2, LON_BLOCKS),
    )
    spread(modes, lane_match(True), wide_in)
    mix(wide_in, weight, False, lane_sum(False), mixed)
    put_own(at, mixed[...].astype(BF16), full)
    groups = LONS // GROUP
    run(
        gather(at, PIECES, full, full_sems),
        lambda: hidden_gradient(out_grad, w2, hidden, 0, groups // 3),
        lambda: hidden_gradient(out_grad, w2, hidden, groups // 3, 2 * groups // 3),
        lambda: hidden_gradient(out_grad, w2, hidden, 2 * groups // 3, groups),
    )
    synthesise_latitude(full, synthesis, rows_spec)
    synthesise_longitude(rows_spec, basis_back, points, syn_scale)
    pointwise(points, hidden, w1, 0, groups)
    analyse_longitude(points, basis, rows_spec)
    analyse_latitude(rows_spec, analysis, parts)
    run(
        reduce_scatter(at, parts, syn_scale, modes, scatter),
        lambda: build(doubled_back, False, synthesis, 0, LON_BLOCKS),
    )
    spread(modes, lane_match(False), wide_grad)
    mix(wide_grad, weight, True, lane_sum(True), mixed)
    put_own(at, mixed[...].astype(BF16), full)
    run(
        gather(at, PIECES, full, full_sems),
        lambda: weight_gradient(wide_in, wide_grad, spectral_grad),
    )
    synthesise_latitude(full, synthesis, rows_spec)
    synthesise_longitude(rows_spec, basis_back, points, fwd_scale)

    def finish(j, carry):
        part = get(points, spec_block(j, ROWS))
        input_grad[j] = (out_grad[j].astype(F32) + part).astype(BF16)
        return carry

    lax.fori_loop(0, LONS, finish, 0, unroll=U_FILL)


def kernel_scratch():
    v, dma = pltpu.VMEM, pltpu.SemaphoreType.DMA
    return [
        v((LONS, ROWS, CH), BF16),
        v((KEEP, 2, CH // BS, BS * BS), BF16),
        v((CH, HID), BF16),
        v((HID, CH), BF16),
        v((2 * KM, LONS_PAD), BF16),
        v((LONS_PAD, 2 * KM), BF16),
        v((2, 2 * KLAT, 2 * ROWS), BF16),
        v((2, 2 * KLAT, 2 * ROWS), BF16),
        v((2, 2 * ROWS, 2 * KLAT), BF16),
        v((2, 2 * ROWS, 2 * KLAT), BF16),
        dma((10,)),
        *[v((LONS_PAD * ROWS, 128), F32)] * 2,
        *[v((LON_BLOCKS * 4 * ROWS, 128), F32)] * 2,
        *[v((128 * size, 128), BF16) for size, _ in PIECES] * 2,
        v((16384, CH), BF16),
        v((LONS * ROWS, HID), BF16),
        v((LON_BLOCKS, 128), F32),
        v((1024, 128), F32),
        v((2 * KEEP, CH), F32),
        v((2 * KEEP, CH), F32),
        v((2 * KEEP * BS, CH), F32),
        v((2 * KEEP * BS, CH), F32),
        *gather_sems(KEPT_PIECE),
        *gather_sems(PIECES),
        *scatter_scratch(),
    ]


def longitude_tables(lon_total):
    j = np.arange(lon_total).reshape(-1, LONS)
    j = np.pad(j, ((0, 0), (0, LONS_PAD - LONS)))
    q = np.arange(2 * KM)
    angles = (j[:, None, :] * (q // 2)[None, :, None] % lon_total) * (2.0 * math.pi / lon_total)
    basis = np.where((q % 2)[None, :, None] == 0, np.cos(angles), -np.sin(angles))
    basis[:, :, LONS:] = 0.0
    basis = basis.astype(np.float32)
    return jnp.asarray(basis, BF16), jnp.asarray(np.swapaxes(basis, 1, 2), BF16)


def latitude_tables(lat_total):
    wave = np.arange(KLAT) - KLAT // 2

    def angles(ids):
        return (wave[None, :, None] * ids[:, None, :] % (2 * lat_total)) * (math.pi / lat_total)

    ids = np.arange(lat_total).reshape(-1, ROWS)
    upper, lower = angles(ids), angles(2 * lat_total - 1 - ids)
    cu, su, cl, sl = np.cos(upper), np.sin(upper), np.cos(lower), np.sin(lower)

    def table(c, s):
        top, bottom = np.concatenate([c, s], axis=2), np.concatenate([-s, c], axis=2)
        return np.concatenate([top, bottom], axis=1)

    plain = np.stack([table(cu, su)] * 2, axis=1)
    doubled = np.stack([table(cu + cl, su + sl), table(cu - cl, su - sl)], axis=1)
    tables = []
    for value in (plain, doubled, np.swapaxes(plain, 2, 3), np.swapaxes(doubled, 2, 3)):
        tables.append(jnp.asarray(value.astype(np.float32), BF16))
    return tables


def body(in_field, out_grad, spec_weight, inner_weight, output_projection_weight, kept_modes):
    lat_parts, lon_parts = lax.axis_size("lat"), lax.axis_size("lon")
    lat_total, lon_total = ROWS * lat_parts, LONS * lon_parts
    fwd_scale = 1.0 / math.sqrt(2 * lat_total * lon_total)
    syn_scale = 1.0 / math.sqrt(KEEP * lat_parts * lon_parts)
    hbm = pl.BlockSpec(memory_space=pl.ANY)
    input_grad, spectral_grad = pl.pallas_call(
        functools.partial(kernel, fwd_scale, syn_scale),
        out_shape=(
            jax.ShapeDtypeStruct((LONS, ROWS, CH), BF16),
            jax.ShapeDtypeStruct((KEEP, 2, CH // BS, BS * BS), F32),
        ),
        in_specs=[VMEM] + [hbm] * 4 + [VMEM] + [hbm] * 6,
        out_specs=(VMEM, VMEM),
        scratch_shapes=kernel_scratch(),
        compiler_params=pltpu.CompilerParams(
            collective_id=0, has_side_effects=True, vmem_limit_bytes=LIMIT
        ),
        name="layer_gradients",
    )(
        jnp.swapaxes(in_field, 0, 1),
        jnp.swapaxes(out_grad, 0, 1),
        spec_weight,
        inner_weight,
        output_projection_weight,
        kept_modes.reshape(1, KEEP),
        *longitude_tables(lon_total),
        *latitude_tables(lat_total),
    )
    return jnp.swapaxes(input_grad, 0, 1), spectral_grad


def solution(mesh):
    return jax.shard_map(
        body,
        mesh=mesh,
        in_specs=(
            P("lat", "lon", None),
            P("lat", "lon", None),
            P(("lat", "lon"), None, None, None),
            P(),
            P(),
            P(("lat", "lon")),
        ),
        out_specs=(P("lat", "lon", None), P(("lat", "lon"), None, None, None)),
        check_vma=False,
    )
```

```python
import functools
import math

import jax
import jax.numpy as jnp
import numpy as np
from jax import lax
from jax.experimental import pallas as pl
from jax.experimental.pallas import tpu as pltpu
from jax.sharding import PartitionSpec as P

BS = 16
KM = 64
KLAT = 128
RING = 4
STEPS = (2, 1, 3)
ROWS, LONS, CH, HID = 64, 45, 256, 1024
LONS_PAD = 48
LON_BLOCKS = 32
KEEP = 32
HALVES = (
    ((32, "xyz"), (16, "yzx"), (16, "zxy")),
    ((32, "yzx"), (16, "xyz"), (16, "zxy")),
)
HALF = 128
STRIDE = 72
MESH = pl.DeviceIdType.MESH
F32, BF16 = jnp.float32, jnp.bfloat16
VMEM = pl.BlockSpec(memory_space=pltpu.VMEM)
LIMIT = 60 << 20
U_FILL, U_ROW, U_BLK, U_BUILD, GROUP, CHUNK, WORK = 5, 16, 8, 4, 9, 256, 3


def matmul(a, b, contract=(1, 0)):
    dims = (((contract[0],), (contract[1],)), ((), ()))
    return lax.dot_general(a, b, dims, preferred_element_type=F32)


def own_place():
    lat, lon = lax.axis_index("lat"), lax.axis_index("lon")
    return {
        "x": lax.div(lon, 8),
        "y": lax.rem(lon, 4),
        "z": lax.rem(lax.div(lon, 4), 2) * 2 + lax.div(lat, 2),
        "core": lax.rem(lat, 2),
    }


def moved(at, axis, step):
    return {**at, axis: lax.rem(at[axis] + step, 2 if axis == "core" else RING)}


def device_of(at):
    return (lax.rem(at["z"], 2) * 2 + at["core"], at["x"] * 8 + lax.div(at["z"], 2) * 4 + at["y"])


def greet(at):
    partners = [moved(at, axis, step) for axis in "xyz" for step in STEPS] + [moved(at, "core", 1)]
    partners += [moved(moved(at, "y", dy), "z", dz) for dy in STEPS for dz in STEPS]
    for partner in partners:
        pl.semaphore_signal(
            pltpu.get_barrier_semaphore(),
            inc=1,
            device_id=device_of(partner),
            device_id_type=MESH,
        )
    return len(partners)


def send(src, dst, sems, target):
    copy = pltpu.make_async_remote_copy(
        src_ref=src,
        dst_ref=dst,
        send_sem=sems[0],
        recv_sem=sems[1],
        device_id=device_of(target),
        device_id_type=MESH,
    )
    copy.start()
    return copy


def rows(start, size):
    return pl.ds(pl.multiple_of(start, math.gcd(size, 16)), size)


def index_of(at, order):
    index = 0
    for name in order:
        index = index * RING + at[name]
    return index


def pair_of_sems(*shape):
    return [pltpu.SemaphoreType.DMA(shape)] * 2


def gather(at, pieces, full, sems):
    ring_send, ring_recv, core_send, core_recv = sems
    bases = [at["core"] * (64 * size) for size, _ in pieces]
    sibling = moved(at, "core", 1)
    pending, across = [], []
    sent = [[] for _ in pieces]

    def across_core(i, s, step):
        size, order = pieces[i]
        slab = lax.rem(at[order[0]] + step, RING)
        here = full[i].at[rows(bases[i] + slab * (16 * size), 16 * size)]
        across.append(send(here, here, (core_send.at[i, s], core_recv.at[i, s]), sibling))

    for phase in range(3):
        for i, (size, order) in enumerate(pieces):
            for copy in sent[i]:
                copy.wait_recv()
            block = size * RING**phase
            index = index_of(at, order[: 3 - phase])
            here = full[i].at[rows(bases[i] + index * block, block)]
            sent[i] = [
                send(
                    here,
                    here,
                    (ring_send.at[i, phase, s], ring_recv.at[i, phase, s]),
                    moved(at, order[2 - phase], step),
                )
                for s, step in enumerate(STEPS)
            ]
            pending += sent[i]
        if phase == 2:
            for i in range(len(pieces)):
                across_core(i, 0, 0)
        yield
    for s in (1, 2, 0):
        for i in range(len(pieces)):
            sent[i][s].wait_recv()
            across_core(i, s + 1, RING - STEPS[s])
    yield
    for copy in across:
        copy.wait_recv()
    for copy in pending + across:
        copy.wait_send()


def scatter_scratch(pieces):
    scratch = [*pair_of_sems(3, 3, 3), *pair_of_sems(3, 4)]
    for size, _ in pieces:
        scratch += [
            pltpu.VMEM((64 * size, HALF), BF16),
            pltpu.VMEM((64 * size, HALF), BF16),
            pltpu.VMEM((3, 16 * size, HALF), BF16),
            pltpu.VMEM((16 * size, HALF), BF16),
            pltpu.VMEM((3, 4 * size, HALF), BF16),
            pltpu.VMEM((4 * size, HALF), BF16),
            pltpu.VMEM((3, size, HALF), BF16),
        ]
    return scratch


def reduce_scatter(at, pieces, parts, scale, out, scratch):
    ring_send, ring_recv, core_send, core_recv = scratch[:4]
    bufs = [scratch[4 + 7 * i : 11 + 7 * i] for i in range(3)]
    sibling = moved(at, "core", 1)
    pending, across = [], {}
    for s, step in enumerate(STEPS + (0,)):
        for i, (size, order) in enumerate(pieces):
            slab = lax.rem(at[order[0]] + step, RING) * (16 * size)
            across[s, i] = send(
                parts[i].at[rows((1 - at["core"]) * (64 * size) + slab, 16 * size)],
                bufs[i][0].at[rows(slab, 16 * size)],
                (core_send.at[i, s], core_recv.at[i, s]),
                sibling,
            )
    yield
    sent = [[], [], []]
    for s, step in enumerate(STEPS + (0,)):
        for i, (size, order) in enumerate(pieces):
            slab = lax.rem(at[order[0]] + step, RING) * (16 * size)
            across[s, i].wait_recv()
            here = rows(slab, 16 * size)
            own = parts[i][rows(at["core"] * (64 * size) + slab, 16 * size), :]
            bufs[i][1][here, :] = (own.astype(F32) + bufs[i][0][here, :].astype(F32)).astype(BF16)
            if step:
                sent[i].append(
                    send(
                        bufs[i][1].at[here],
                        bufs[i][2].at[s],
                        (ring_send.at[i, 0, s], ring_recv.at[i, 0, s]),
                        moved(at, order[0], step),
                    )
                )
    yield
    first = 0
    for phase in range(3):
        first = 0
        for i, (size, order) in enumerate(pieces):
            block = size * RING ** (2 - phase)
            mine, landed = bufs[i][1 + 2 * phase], bufs[i][2 + 2 * phase]
            total = mine[rows(at[order[phase]] * block, block), :].astype(F32)
            for s in (1, 2, 0):
                sent[i][s].wait_recv()
                total = total + landed[s].astype(F32)
            pending += sent[i]
            if phase == 2:
                out[first : first + size, :] = total * scale
                first += size
                continue
            after = bufs[i][3 + 2 * phase]
            after[...] = total.astype(BF16)
            small = block // RING
            axis = order[phase + 1]
            sent[i] = [
                send(
                    after.at[rows(lax.rem(at[axis] + step, RING) * small, small)],
                    bufs[i][4 + 2 * phase].at[s],
                    (ring_send.at[i, phase + 1, s], ring_recv.at[i, phase + 1, s]),
                    moved(at, axis, step),
                )
                for s, step in enumerate(STEPS)
            ]
        if phase < 2:
            yield
    for copy in pending + list(across.values()):
        copy.wait_send()


def put_own(at, pieces, modes, full):
    first = 0
    for i, (size, order) in enumerate(pieces):
        here = rows((at["core"] * 64 + index_of(at, order)) * size, size)
        full[i][here, :] = modes[first : first + size]
        first += size


def own_slots(at, kept):
    lat = lax.rem(at["z"], 2) * 2 + at["core"]
    value = jnp.concatenate([kept[...]] * 4, axis=1)
    slot = (value & 1) * KLAT + lat * KEEP + lax.shift_right_logical(value, 1)
    lane = lax.broadcasted_iota(jnp.int32, (1, 128), 1)
    own = jnp.where(lax.shift_right_logical(lane, 5) == lat, slot.astype(F32), 0.0)
    return jnp.broadcast_to(own, (8, 128))


def gather_slots(at, own, other, full, sems):
    core_send, core_recv, line_send, line_recv, plane_send, plane_recv = sems
    copies = [send(own, other, (core_send.at[0], core_recv.at[0]), moved(at, "core", 1))]
    copies[0].wait_recv()
    mine = rows(index_of(at, "yzx") * 8, 8)
    full[mine, :] = own[...] + other[...]
    line = [
        send(full.at[mine], full.at[mine], (line_send.at[s], line_recv.at[s]), moved(at, "x", step))
        for s, step in enumerate(STEPS)
    ]
    yield
    for copy in line:
        copy.wait_recv()
    here = full.at[rows(index_of(at, "yz") * 32, 32)]
    plane = []
    for dy, dz in ((2, 2), (2, 1), (2, 3), (1, 2), (3, 2), (1, 1), (1, 3), (3, 1), (3, 3)):
        plane.append((dy, dz))
    for step in STEPS:
        plane += [(step, 0), (0, step)]
    plane = [
        send(
            here,
            here,
            (plane_send.at[dy, dz], plane_recv.at[dy, dz]),
            moved(moved(at, "y", dy), "z", dz),
        )
        for dy, dz in plane
    ]
    yield
    for copy in plane:
        copy.wait_recv()
    for copy in copies + line + plane:
        copy.wait_send()


def collect_slots(full, slots):
    for b in range(LON_BLOCKS):
        x, zhi, y = b // 8, b // 4 % 2, b % 4
        first = ((y * 4 + zhi * 2) * 4 + x) * 8
        total = full[first : first + 8, :] + full[first + 32 : first + 40, :]
        slots[b : b + 1, :] = total[0:1]


def piece_start(b, lat, size, order):
    place = {"x": lax.div(b, 8), "z": lax.rem(lax.div(b, 4), 2) * 2 + lat // 2, "y": lax.rem(b, 4)}
    return rows((lat % 2 * 64 + index_of(place, order)) * size, size)


def group(i):
    return pl.ds(pl.multiple_of(i * STRIDE, 8), ROWS)


def one_hot(slots, b):
    ids = lax.broadcasted_iota(jnp.int32, (256, 128), 0).astype(F32)
    return jnp.where(ids == slots[pl.ds(b, 1), :], 1.0, 0.0).astype(BF16)


def one_hot_turned(slots, b):
    columns = jnp.transpose(jnp.broadcast_to(slots[pl.ds(b, 1), :], (128, 128)))
    ids = lax.broadcasted_iota(jnp.int32, (128, 128), 1).astype(F32)
    hot = [jnp.where(ids == columns - 128.0 * mode, 1.0, 0.0).astype(BF16) for mode in range(2)]
    return jnp.concatenate(hot, axis=1)


def both(halves, where):
    return jnp.concatenate([half[where, :] for half in halves], axis=1)


def fill_points(field, points):
    def one(j, carry):
        value = field[j].astype(F32)
        for h in range(2):
            points[h][group(j), :] = value[:, HALF * h : HALF * h + HALF]
        return carry

    lax.fori_loop(0, LONS, one, 0, unroll=U_FILL)
    for j in range(LONS, LONS_PAD):
        for h in range(2):
            points[h][group(j), :] = jnp.zeros((ROWS, HALF), F32)


def analyse_longitude(points, basis, rows_spec):
    def one(g, carry):
        value = both(points, pl.ds(g, LONS_PAD, stride=STRIDE)).astype(BF16)
        spec = matmul(basis[...], value)
        for h, half in enumerate(rows_spec):
            half[pl.ds(g, 2 * KM, stride=STRIDE), :] = spec[:, HALF * h : HALF * h + HALF]
        return carry

    lax.fori_loop(0, ROWS, one, 0, unroll=U_ROW)


def synthesise_longitude(rows_spec, basis_back, points, scale):
    def one(g, carry):
        spec = rows_spec[pl.ds(g, 2 * KM, stride=STRIDE), :].astype(BF16)
        points[pl.ds(g, LONS_PAD, stride=STRIDE), :] = matmul(basis_back[...], spec) * scale
        return carry

    lax.fori_loop(0, ROWS, one, 0, unroll=U_ROW)


def spec_block(b, size=256):
    return pl.ds(pl.multiple_of(b * size, size), size)


def analyse_dense(rows_spec, table, dense):
    def one(b, carry):
        for mode in range(2):
            value = jnp.concatenate(
                [both(rows_spec, group(b * 4 + mode * 2 + part)) for part in range(2)], axis=0
            )
            full = matmul(table[mode], value.astype(BF16)).astype(BF16)
            for part in range(2):
                start = pl.multiple_of(b * 512 + part * 256 + mode * 128, 128)
                dense[pl.ds(start, 128), :] = full[128 * part : 128 * part + 128]
        return carry

    lax.fori_loop(0, LON_BLOCKS, one, 0, unroll=U_BLK)


def store_modes(b, part, modes, pieces, parts):
    for lat in range(4):
        tile = modes[32 * lat : 32 * lat + 32]
        starts = [piece_start(b, lat, *piece) for piece in pieces]
        if part == 0:
            parts[0][starts[0], :] = tile
        else:
            parts[1][starts[1], :] = tile[0:16]
            parts[2][starts[2], :] = tile[16:32]


def load_modes(b, pieces, full):
    tiles = [[], []]
    for lat in range(4):
        values = [full[i][piece_start(b, lat, *piece), :] for i, piece in enumerate(pieces)]
        tiles[0].append(values[0])
        tiles[1] += values[1:]
    return jnp.concatenate(tiles[0] + tiles[1], axis=0)


def select_modes(dense, slots, parts):
    def one(b, carry):
        hot = one_hot_turned(slots, b)
        for part in range(2):
            modes = matmul(hot, dense[spec_block(b * 2 + part), :]).astype(BF16)
            for h in range(2):
                here = modes[:, HALF * h : HALF * h + HALF]
                store_modes(b, part, here, HALVES[h], parts[h])
        return carry

    lax.fori_loop(0, LON_BLOCKS, one, 0, unroll=U_BLK)


def build_analysis(slots, table, out, low, high):
    def one(b, carry):
        hot = one_hot_turned(slots, b)
        for part in range(2):
            for mode in range(2):
                value = matmul(
                    hot[:, 128 * mode : 128 * mode + 128],
                    table[mode, 128 * part : 128 * part + 128, :],
                )
                start = pl.multiple_of(b * 256 + part * 128, 128)
                out[pl.ds(start, 128), 128 * mode : 128 * mode + 128] = value.astype(BF16)
        return carry

    lax.fori_loop(low, high, one, 0, unroll=U_BUILD)


def build_synthesis(slots, table, out, low, high):
    def one(b, carry):
        hot = one_hot(slots, b)
        for part in range(2):
            for mode in range(2):
                value = matmul(
                    table[mode, :, 128 * part : 128 * part + 128],
                    hot[128 * mode : 128 * mode + 128],
                )
                start = pl.multiple_of(b * 256 + mode * 128, 128)
                out[pl.ds(start, 128), 128 * part : 128 * part + 128] = value.astype(BF16)
        return carry

    lax.fori_loop(low, high, one, 0, unroll=U_BUILD)


def analyse_latitude(rows_spec, table, pieces, parts):
    def one(b, carry):
        value = jnp.concatenate([rows_spec[group(b * 4 + q), :] for q in range(4)], axis=0)
        modes = matmul(table[spec_block(b), :], value.astype(BF16)).astype(BF16)
        for part in range(2):
            store_modes(b, part, modes[128 * part : 128 * part + 128], pieces, parts)
        return carry

    lax.fori_loop(0, LON_BLOCKS, one, 0, unroll=U_BLK)


def synthesise_latitude(pieces, full, table, rows_spec):
    def one(b, carry):
        value = matmul(table[spec_block(b), :], load_modes(b, pieces, full))
        for q in range(4):
            rows_spec[group(b * 4 + q), :] = value[ROWS * q : ROWS * q + ROWS]
        return carry

    lax.fori_loop(0, LON_BLOCKS, one, 0, unroll=U_BLK)


def gelu_slope(x):
    c, a = math.sqrt(2.0 / math.pi), 0.044715
    square = x * x
    t = jnp.tanh(x * (c + (c * a) * square))
    half = 0.5 + 0.5 * t
    return half + x * (half * (1.0 - t)) * (c + (3.0 * c * a) * square)


def hidden_gradient(out_grad, w2, hidden, low, high):
    def one(i, carry):
        grad = out_grad[pl.ds(i * GROUP, GROUP)].reshape(GROUP * ROWS, CH)
        here = pl.ds(pl.multiple_of(i * (GROUP * ROWS), GROUP * ROWS), GROUP * ROWS)
        for k in range(HID // CHUNK):
            cols = slice(CHUNK * k, CHUNK * k + CHUNK)
            hidden[here, cols] = matmul(grad, w2[cols, :], (1, 1)).astype(BF16)
        return carry

    lax.fori_loop(low, high, one, 0)


def pointwise(points, hidden, w1, low, high):
    def one(i, carry):
        here = pl.ds(pl.multiple_of(i * (GROUP * ROWS), GROUP * ROWS), GROUP * ROWS)
        value = [both(points, group(i * GROUP + j)).astype(BF16) for j in range(GROUP)]
        value = jnp.concatenate(value, axis=0)
        total = None
        for k in range(HID // CHUNK):
            cols = slice(CHUNK * k, CHUNK * k + CHUNK)
            pre = matmul(value, w1[:, cols])
            pre_grad = (gelu_slope(pre) * hidden[here, cols].astype(F32)).astype(BF16)
            term = matmul(pre_grad, w1[:, cols], (1, 1))
            total = term if total is None else total + term
        for j in range(GROUP):
            for h in range(2):
                points[h][group(i * GROUP + j), :] = total[
                    ROWS * j : ROWS * j + ROWS, HALF * h : HALF * h + HALF
                ]
        return carry

    lax.fori_loop(low, high, one, 0)


BETAS = HALF // BS
MIX = 16


def match_lanes(high, lane_first):
    shape = (CH, HALF) if lane_first else (HALF, CH)
    lane = lax.broadcasted_iota(jnp.int32, shape, 0 if lane_first else 1)
    channel = lax.broadcasted_iota(jnp.int32, shape, 1 if lane_first else 0) & (BS - 1)
    half = lax.shift_right_logical(lane, 4) if high else lane & (BS - 1)
    return jnp.where(channel == half, 1.0, 0.0).astype(BF16)


def block_mask():
    beta = lax.broadcasted_iota(jnp.int32, (BETAS, HALF), 0)
    channel = lax.broadcasted_iota(jnp.int32, (BETAS, HALF), 1)
    return jnp.where(beta == lax.shift_right_logical(channel, 4), 1.0, 0.0)[None]


def exact(value, ones):
    high = value.astype(BF16)
    low = (value - high.astype(F32)).astype(BF16)
    return matmul(high, ones) + matmul(low, ones)


def widen_weight(weight, wide):
    def one(e, carry):
        for part in range(2):
            value = weight[e, part].astype(F32)
            for h in range(2):
                start = pl.multiple_of((part * KEEP + e) * BETAS, BETAS)
                wide[h][pl.ds(start, BETAS), :] = value[BETAS * h : BETAS * h + BETAS]
        return carry

    lax.fori_loop(0, KEEP, one, 0, unroll=4)


def spread(modes, high, out):
    mask, match = block_mask(), match_lanes(high, False)
    for i in range(2 * KEEP // MIX):
        value = modes[MIX * i : MIX * i + MIX, :]
        wide = (value[:, None, :] * mask).reshape(MIX * BETAS, HALF)
        out[MIX * BETAS * i : MIX * BETAS * (i + 1), :] = exact(wide, match)


def mixing_rows(i):
    return [
        slice((part * KEEP + MIX * i) * BETAS, (part * KEEP + MIX * (i + 1)) * BETAS)
        for part in range(2)
    ]


def mix(wide, weight, backward):
    mask, sums = block_mask(), match_lanes(backward, True)
    out = [[], []]
    for i in range(KEEP // MIX):
        first, second = mixing_rows(i)
        re, im, wr, wi = wide[first, :], wide[second, :], weight[first, :], weight[second, :]
        if backward:
            terms = re * wr + im * wi, im * wr - re * wi
        else:
            terms = re * wr - im * wi, re * wi + im * wr
        for part, term in enumerate(terms):
            total = exact(term, sums).reshape(MIX, BETAS, HALF) * mask
            out[part].append(jnp.sum(total, axis=1))
    return jnp.concatenate(out[0] + out[1], axis=0).astype(BF16)


def weight_gradient(h, wide_in, wide_grad, out):
    for i in range(KEEP // MIX):
        first, second = mixing_rows(i)
        ar, ai, br, bi = wide_in[first, :], wide_in[second, :], wide_grad[first, :], wide_grad[second, :]
        here, betas = slice(MIX * i, MIX * i + MIX), slice(BETAS * h, BETAS * h + BETAS)
        out[here, 0, betas, :] = (ar * br + ai * bi).reshape(MIX, BETAS, CH)
        out[here, 1, betas, :] = (ar * bi - ai * br).reshape(MIX, BETAS, CH)


def kernel(fwd_scale, syn_scale, *refs):
    refs = list(refs)

    def take(n):
        taken = refs[:n]
        del refs[:n]
        return taken

    field_hbm, out_grad_hbm, weight_hbm, w1_hbm, w2_hbm, kept = take(6)
    basis_hbm, back_hbm, plain_hbm, doubled_hbm, plain_back_hbm, doubled_back_hbm = take(6)
    spectral_part, spectral_grad = take(2)
    field, out_grad, weight, w1, w2 = take(5)
    basis, basis_back, plain, doubled, plain_back, doubled_back = take(6)
    (load_sems,) = take(1)
    points, rows_spec = take(2), take(2)
    parts, full = [take(3), take(3)], [take(3), take(3)]
    tables, hidden, slots, own, other, slots_full = take(6)
    modes, weights, wide_in, wide_grad = take(2), take(2), take(2), take(2)
    slot_sems = take(6)
    gather_sems = [take(4), take(4)]
    scatter = [take(25), take(25)]
    analysis, synthesis = tables.at[0:8192], tables.at[8192:16384]

    at = own_place()
    lat, lon = lax.axis_index("lat"), lax.axis_index("lon")
    greeted = greet(at)
    loads = []
    for i, (src, dst) in enumerate(
        [
            (field_hbm, field),
            (basis_hbm.at[lon], basis),
            (doubled_hbm.at[lat], doubled),
            (plain_hbm.at[lat], plain),
            (plain_back_hbm.at[lat], plain_back),
            (weight_hbm, weight),
            (w2_hbm, w2),
            (out_grad_hbm, out_grad),
            (back_hbm.at[lon], basis_back),
            (w1_hbm, w1),
            (doubled_back_hbm.at[lat], doubled_back),
        ]
    ):
        copy = pltpu.make_async_copy(src, dst, load_sems.at[i])
        copy.start()
        loads.append(copy)
    own[...] = own_slots(at, kept)
    loads[0].wait()
    fill_points(field, points)
    pl.semaphore_wait(pltpu.get_barrier_semaphore(), greeted)

    collecting = gather_slots(at, own, other, slots_full, slot_sems)
    next(collecting)
    loads[1].wait()
    analyse_longitude(points, basis, rows_spec)
    next(collecting)
    loads[2].wait()
    analyse_dense(rows_spec, doubled, tables)
    next(collecting, None)
    collect_slots(slots_full, slots)
    select_modes(tables, slots, parts)

    def exchange(h, scale, backward, synthesised):
        wide = (wide_grad if backward else wide_in)[h]
        yield from reduce_scatter(at, HALVES[h], parts[h], scale, modes[h], scatter[h])
        spread(modes[h], not backward, wide)
        put_own(at, HALVES[h], mix(wide, weights[h], backward), full[h])
        yield from gather(at, HALVES[h], full[h], gather_sems[h])
        synthesise_latitude(HALVES[h], full[h], synthesis, rows_spec[h])
        synthesise_longitude(rows_spec[h], basis_back, points[h], synthesised)

    def drive(first, second, work, before=lambda: None):
        next(first)
        before()
        next(second)
        for _ in range(6):
            for task in work[:WORK]:
                task()
            del work[:WORK]
            next(first)
            next(second)
        for task in work:
            task()
        next(first)
        next(first, None)
        next(second)
        next(second, None)

    quarter = LON_BLOCKS // 4
    work = [lambda: [copy.wait() for copy in loads[3:]]]
    for low in range(0, LON_BLOCKS, quarter):
        span = (low, low + quarter)
        work += [
            functools.partial(build_analysis, slots, plain, analysis, *span),
            functools.partial(build_synthesis, slots, plain_back, synthesis, *span),
        ]
    work.insert(1, functools.partial(widen_weight, weight, weights))
    for i in range(LONS // GROUP):
        work.append(functools.partial(hidden_gradient, out_grad, w2, hidden, i, i + 1))
    drive(*[exchange(h, fwd_scale, False, syn_scale) for h in range(2)], work)

    pointwise(points, hidden, w1, 0, LONS // GROUP)

    def analyse(h):
        analyse_longitude(points[h : h + 1], basis, rows_spec[h : h + 1])
        analyse_latitude(rows_spec[h], analysis, HALVES[h], parts[h])

    analyse(0)
    work = []
    for low in range(0, LON_BLOCKS, quarter):
        work.append(
            functools.partial(
                build_synthesis, slots, doubled_back, synthesis, low, low + quarter
            )
        )
        work += [lambda: None] * (WORK - 1)
    for h in range(2):
        work.append(
            functools.partial(weight_gradient, h, wide_in[h], wide_grad[h], spectral_grad)
        )
    drive(
        *[exchange(h, syn_scale, True, fwd_scale) for h in range(2)],
        work,
        lambda: analyse(1),
    )

    def finish(j, carry):
        spectral_part[j] = both(points, group(j)).astype(BF16)
        return carry

    lax.fori_loop(0, LONS, finish, 0, unroll=U_FILL)


def kernel_scratch():
    v = pltpu.VMEM
    pieces = [v((128 * size, HALF), BF16) for half in HALVES for size, _ in half]
    return [
        v((LONS, ROWS, CH), BF16),
        v((LONS, ROWS, CH), BF16),
        v((KEEP, 2, CH // BS, BS * BS), BF16),
        v((CH, HID), BF16),
        v((HID, CH), BF16),
        v((2 * KM, LONS_PAD), BF16),
        v((LONS_PAD, 2 * KM), BF16),
        v((2, 2 * KLAT, 2 * ROWS), BF16),
        v((2, 2 * KLAT, 2 * ROWS), BF16),
        v((2, 2 * ROWS, 2 * KLAT), BF16),
        v((2, 2 * ROWS, 2 * KLAT), BF16),
        pltpu.SemaphoreType.DMA((11,)),
        *[v((LONS_PAD * STRIDE, HALF), F32)] * 2,
        *[v((2 * KM * STRIDE, HALF), F32)] * 2,
        *pieces,
        *pieces,
        v((16384, CH), BF16),
        v((LONS * ROWS, HID), BF16),
        v((LON_BLOCKS, 128), F32),
        v((8, 128), F32),
        v((8, 128), F32),
        v((512, 128), F32),
        *[v((2 * KEEP, HALF), F32)] * 2,
        *[v((2 * KEEP * BETAS, CH), F32)] * 6,
        *pair_of_sems(1),
        *pair_of_sems(3),
        *pair_of_sems(4, 4),
        *[*pair_of_sems(3, 3, 3), *pair_of_sems(3, 4)] * 2,
        *scatter_scratch(HALVES[0]),
        *scatter_scratch(HALVES[1]),
    ]


def longitude_tables(lon_total):
    j = np.arange(lon_total).reshape(-1, LONS)
    j = np.pad(j, ((0, 0), (0, LONS_PAD - LONS)))
    q = np.arange(2 * KM)
    angles = (j[:, None, :] * (q // 2)[None, :, None] % lon_total) * (2.0 * math.pi / lon_total)
    basis = np.where((q % 2)[None, :, None] == 0, np.cos(angles), -np.sin(angles))
    basis[:, :, LONS:] = 0.0
    basis = basis.astype(np.float32)
    return jnp.asarray(basis, BF16), jnp.asarray(np.swapaxes(basis, 1, 2), BF16)


def latitude_tables(lat_total):
    wave = np.arange(KLAT) - KLAT // 2

    def angles(ids):
        return (wave[None, :, None] * ids[:, None, :] % (2 * lat_total)) * (math.pi / lat_total)

    ids = np.arange(lat_total).reshape(-1, ROWS)
    upper, lower = angles(ids), angles(2 * lat_total - 1 - ids)
    cu, su, cl, sl = np.cos(upper), np.sin(upper), np.cos(lower), np.sin(lower)

    def table(c, s):
        top, bottom = np.concatenate([c, s], axis=2), np.concatenate([-s, c], axis=2)
        return np.concatenate([top, bottom], axis=1)

    plain = np.stack([table(cu, su)] * 2, axis=1)
    doubled = np.stack([table(cu + cl, su + sl), table(cu - cl, su - sl)], axis=1)
    tables = []
    for value in (plain, doubled, np.swapaxes(plain, 2, 3), np.swapaxes(doubled, 2, 3)):
        tables.append(jnp.asarray(value.astype(np.float32), BF16))
    return tables


def body(in_field, out_grad, spec_weight, inner_weight, output_projection_weight, kept_modes):
    lat_parts, lon_parts = lax.axis_size("lat"), lax.axis_size("lon")
    lat_total, lon_total = ROWS * lat_parts, LONS * lon_parts
    fwd_scale = 1.0 / math.sqrt(2 * lat_total * lon_total)
    syn_scale = 1.0 / math.sqrt(KEEP * lat_parts * lon_parts)
    hbm = pl.BlockSpec(memory_space=pl.ANY)
    spectral_part, spectral_grad = pl.pallas_call(
        functools.partial(kernel, fwd_scale, syn_scale),
        out_shape=(
            jax.ShapeDtypeStruct((LONS, ROWS, CH), BF16),
            jax.ShapeDtypeStruct((KEEP, 2, CH // BS, BS * BS), F32),
        ),
        in_specs=[hbm] * 5 + [VMEM] + [hbm] * 6,
        out_specs=(VMEM, VMEM),
        scratch_shapes=kernel_scratch(),
        compiler_params=pltpu.CompilerParams(
            collective_id=0, has_side_effects=True, vmem_limit_bytes=LIMIT
        ),
        name="layer_gradients",
    )(
        jnp.swapaxes(in_field, 0, 1),
        jnp.swapaxes(out_grad, 0, 1),
        spec_weight,
        inner_weight,
        output_projection_weight,
        kept_modes.reshape(1, KEEP),
        *longitude_tables(lon_total),
        *latitude_tables(lat_total),
    )
    part = jnp.swapaxes(spectral_part, 0, 1)
    input_grad = (out_grad.astype(F32) + part.astype(F32)).astype(BF16)
    return input_grad, spectral_grad


def solution(mesh):
    return jax.shard_map(
        body,
        mesh=mesh,
        in_specs=(
            P("lat", "lon", None),
            P("lat", "lon", None),
            P(("lat", "lon"), None, None, None),
            P(),
            P(),
            P(("lat", "lon")),
        ),
        out_specs=(P("lat", "lon", None), P(("lat", "lon"), None, None, None)),
        check_vma=False,
    )
```

```python
import functools
import math

import jax
import jax.numpy as jnp
import numpy as np
from jax import lax
from jax.experimental import pallas as pl
from jax.experimental.pallas import tpu as pltpu
from jax.sharding import PartitionSpec as P

BS = 16
KM = 64
KLAT = 128
RING = 4
STEPS = (2, 1, 3)
ROWS, LONS, CH, HID = 64, 45, 256, 1024
LONS_PAD = 48
LON_BLOCKS = 32
KEEP = 32
HALVES = (
    ((32, "xyz"), (16, "yzx"), (16, "zxy")),
    ((32, "yzx"), (16, "xyz"), (16, "zxy")),
)
HALF = 128
STRIDE = 72
MESH = pl.DeviceIdType.MESH
F32, BF16 = jnp.float32, jnp.bfloat16
VMEM = pl.BlockSpec(memory_space=pltpu.VMEM)
LIMIT = 60 << 20
U_FILL, U_ROW, U_BLK, U_BUILD, GROUP, CHUNK, WORK = 5, 16, 8, 4, 9, 256, 3


def matmul(a, b, contract=(1, 0)):
    dims = (((contract[0],), (contract[1],)), ((), ()))
    return lax.dot_general(a, b, dims, preferred_element_type=F32)


def own_place():
    lat, lon = lax.axis_index("lat"), lax.axis_index("lon")
    return {
        "x": lax.div(lon, 8),
        "y": lax.rem(lon, 4),
        "z": lax.rem(lax.div(lon, 4), 2) * 2 + lax.div(lat, 2),
        "core": lax.rem(lat, 2),
    }


def moved(at, axis, step):
    return {**at, axis: lax.rem(at[axis] + step, 2 if axis == "core" else RING)}


def device_of(at):
    return (lax.rem(at["z"], 2) * 2 + at["core"], at["x"] * 8 + lax.div(at["z"], 2) * 4 + at["y"])


def greet(at):
    partners = [moved(at, axis, step) for axis in "xyz" for step in STEPS] + [moved(at, "core", 1)]
    for partner in partners:
        pl.semaphore_signal(
            pltpu.get_barrier_semaphore(),
            inc=1,
            device_id=device_of(partner),
            device_id_type=MESH,
        )
    return len(partners)


def send(src, dst, sems, target):
    copy = pltpu.make_async_remote_copy(
        src_ref=src,
        dst_ref=dst,
        send_sem=sems[0],
        recv_sem=sems[1],
        device_id=device_of(target),
        device_id_type=MESH,
    )
    copy.start()
    return copy


def rows(start, size):
    return pl.ds(pl.multiple_of(start, math.gcd(size, 16)), size)


def index_of(at, order):
    index = 0
    for name in order:
        index = index * RING + at[name]
    return index


def pair_of_sems(*shape):
    return [pltpu.SemaphoreType.DMA(shape)] * 2


def gather(at, pieces, full, sems):
    ring_send, ring_recv, core_send, core_recv = sems
    bases = [at["core"] * (64 * size) for size, _ in pieces]
    sibling = moved(at, "core", 1)
    pending, across = [], []
    sent = [[] for _ in pieces]

    def across_core(i, s, step):
        size, order = pieces[i]
        slab = lax.rem(at[order[0]] + step, RING)
        here = full[i].at[rows(bases[i] + slab * (16 * size), 16 * size)]
        across.append(send(here, here, (core_send.at[i, s], core_recv.at[i, s]), sibling))

    for phase in range(3):
        for i, (size, order) in enumerate(pieces):
            for copy in sent[i]:
                copy.wait_recv()
            block = size * RING**phase
            index = index_of(at, order[: 3 - phase])
            here = full[i].at[rows(bases[i] + index * block, block)]
            sent[i] = [
                send(
                    here,
                    here,
                    (ring_send.at[i, phase, s], ring_recv.at[i, phase, s]),
                    moved(at, order[2 - phase], step),
                )
                for s, step in enumerate(STEPS)
            ]
            pending += sent[i]
        if phase == 2:
            for i in range(len(pieces)):
                across_core(i, 0, 0)
        yield
    for s in (1, 2, 0):
        for i in range(len(pieces)):
            sent[i][s].wait_recv()
            across_core(i, s + 1, RING - STEPS[s])
    yield
    for copy in across:
        copy.wait_recv()
    for copy in pending + across:
        copy.wait_send()


def scatter_scratch(pieces):
    scratch = [*pair_of_sems(3, 3, 3), *pair_of_sems(3, 4)]
    for size, _ in pieces:
        scratch += [
            pltpu.VMEM((64 * size, HALF), BF16),
            pltpu.VMEM((64 * size, HALF), BF16),
            pltpu.VMEM((3, 16 * size, HALF), BF16),
            pltpu.VMEM((16 * size, HALF), BF16),
            pltpu.VMEM((3, 4 * size, HALF), BF16),
            pltpu.VMEM((4 * size, HALF), BF16),
            pltpu.VMEM((3, size, HALF), BF16),
        ]
    return scratch


def reduce_scatter(at, pieces, parts, scale, out, scratch):
    ring_send, ring_recv, core_send, core_recv = scratch[:4]
    bufs = [scratch[4 + 7 * i : 11 + 7 * i] for i in range(3)]
    sibling = moved(at, "core", 1)
    pending, across = [], {}
    for s, step in enumerate(STEPS + (0,)):
        for i, (size, order) in enumerate(pieces):
            slab = lax.rem(at[order[0]] + step, RING) * (16 * size)
            across[s, i] = send(
                parts[i].at[rows((1 - at["core"]) * (64 * size) + slab, 16 * size)],
                bufs[i][0].at[rows(slab, 16 * size)],
                (core_send.at[i, s], core_recv.at[i, s]),
                sibling,
            )
    yield
    sent = [[], [], []]
    for s, step in enumerate(STEPS + (0,)):
        for i, (size, order) in enumerate(pieces):
            slab = lax.rem(at[order[0]] + step, RING) * (16 * size)
            across[s, i].wait_recv()
            here = rows(slab, 16 * size)
            own = parts[i][rows(at["core"] * (64 * size) + slab, 16 * size), :]
            bufs[i][1][here, :] = (own.astype(F32) + bufs[i][0][here, :].astype(F32)).astype(BF16)
            if step:
                sent[i].append(
                    send(
                        bufs[i][1].at[here],
                        bufs[i][2].at[s],
                        (ring_send.at[i, 0, s], ring_recv.at[i, 0, s]),
                        moved(at, order[0], step),
                    )
                )
    yield
    first = 0
    for phase in range(3):
        first = 0
        for i, (size, order) in enumerate(pieces):
            block = size * RING ** (2 - phase)
            mine, landed = bufs[i][1 + 2 * phase], bufs[i][2 + 2 * phase]
            total = mine[rows(at[order[phase]] * block, block), :].astype(F32)
            for s in (1, 2, 0):
                sent[i][s].wait_recv()
                total = total + landed[s].astype(F32)
            pending += sent[i]
            if phase == 2:
                out[first : first + size, :] = total * scale
                first += size
                continue
            after = bufs[i][3 + 2 * phase]
            after[...] = total.astype(BF16)
            small = block // RING
            axis = order[phase + 1]
            sent[i] = [
                send(
                    after.at[rows(lax.rem(at[axis] + step, RING) * small, small)],
                    bufs[i][4 + 2 * phase].at[s],
                    (ring_send.at[i, phase + 1, s], ring_recv.at[i, phase + 1, s]),
                    moved(at, axis, step),
                )
                for s, step in enumerate(STEPS)
            ]
        if phase < 2:
            yield
    for copy in pending + list(across.values()):
        copy.wait_send()


def put_own(at, pieces, modes, full):
    first = 0
    for i, (size, order) in enumerate(pieces):
        here = rows((at["core"] * 64 + index_of(at, order)) * size, size)
        full[i][here, :] = modes[first : first + size]
        first += size


def own_slots(at, kept):
    lat = lax.rem(at["z"], 2) * 2 + at["core"]
    value = jnp.concatenate([kept[...]] * 4, axis=1)
    slot = (value & 1) * KLAT + lat * KEEP + lax.shift_right_logical(value, 1)
    lane = lax.broadcasted_iota(jnp.int32, (1, 128), 1)
    own = jnp.where(lax.shift_right_logical(lane, 5) == lat, slot.astype(F32), 0.0)
    return jnp.broadcast_to(own, (8, 128))


def gather_slots(at, own, other, full, sems):
    core_send, core_recv, line_send, line_recv, plane_send, plane_recv, past = sems
    copies = [send(own, other, (core_send.at[0], core_recv.at[0]), moved(at, "core", 1))]
    for step in STEPS:
        pl.semaphore_signal(
            past, inc=1, device_id=device_of(moved(at, "y", step)), device_id_type=MESH
        )
    copies[0].wait_recv()
    mine = rows(index_of(at, "yzx") * 8, 8)
    full[mine, :] = own[...] + other[...]
    line = [
        send(full.at[mine], full.at[mine], (line_send.at[s], line_recv.at[s]), moved(at, "x", step))
        for s, step in enumerate(STEPS)
    ]
    yield
    for copy in line:
        copy.wait_recv()
    pl.semaphore_wait(past, len(STEPS))
    here = full.at[rows(index_of(at, "yz") * 32, 32)]
    plane = []
    for dy, dz in ((2, 2), (2, 1), (2, 3), (1, 2), (3, 2), (1, 1), (1, 3), (3, 1), (3, 3)):
        plane.append((dy, dz))
    for step in STEPS:
        plane += [(step, 0), (0, step)]
    plane = [
        send(
            here,
            here,
            (plane_send.at[dy, dz], plane_recv.at[dy, dz]),
            moved(moved(at, "y", dy), "z", dz),
        )
        for dy, dz in plane
    ]
    yield
    for copy in plane:
        copy.wait_recv()
    for copy in copies + line + plane:
        copy.wait_send()


def collect_slots(full, slots):
    for b in range(LON_BLOCKS):
        x, zhi, y = b // 8, b // 4 % 2, b % 4
        first = ((y * 4 + zhi * 2) * 4 + x) * 8
        total = full[first : first + 8, :] + full[first + 32 : first + 40, :]
        slots[b : b + 1, :] = total[0:1]


def piece_start(b, lat, size, order):
    place = {"x": lax.div(b, 8), "z": lax.rem(lax.div(b, 4), 2) * 2 + lat // 2, "y": lax.rem(b, 4)}
    return rows((lat % 2 * 64 + index_of(place, order)) * size, size)


def group(i):
    return pl.ds(pl.multiple_of(i * STRIDE, 8), ROWS)


def one_hot(slots, b):
    ids = lax.broadcasted_iota(jnp.int32, (256, 128), 0).astype(F32)
    return jnp.where(ids == slots[pl.ds(b, 1), :], 1.0, 0.0).astype(BF16)


def one_hot_turned(slots, b):
    columns = jnp.transpose(jnp.broadcast_to(slots[pl.ds(b, 1), :], (128, 128)))
    ids = lax.broadcasted_iota(jnp.int32, (128, 128), 1).astype(F32)
    hot = [jnp.where(ids == columns - 128.0 * mode, 1.0, 0.0).astype(BF16) for mode in range(2)]
    return jnp.concatenate(hot, axis=1)


def both(halves, where):
    return jnp.concatenate([half[where, :] for half in halves], axis=1)


def fill_points(field, points):
    def one(j, carry):
        value = field[j].astype(F32)
        for h in range(2):
            points[h][group(j), :] = value[:, HALF * h : HALF * h + HALF]
        return carry

    lax.fori_loop(0, LONS, one, 0, unroll=U_FILL)
    for j in range(LONS, LONS_PAD):
        for h in range(2):
            points[h][group(j), :] = jnp.zeros((ROWS, HALF), F32)


def analyse_longitude(points, basis, rows_spec):
    def one(g, carry):
        value = both(points, pl.ds(g, LONS_PAD, stride=STRIDE)).astype(BF16)
        spec = matmul(basis[...], value)
        for h, half in enumerate(rows_spec):
            half[pl.ds(g, 2 * KM, stride=STRIDE), :] = spec[:, HALF * h : HALF * h + HALF]
        return carry

    lax.fori_loop(0, ROWS, one, 0, unroll=U_ROW)


def synthesise_longitude(rows_spec, basis_back, points, scale):
    def one(g, carry):
        spec = rows_spec[pl.ds(g, 2 * KM, stride=STRIDE), :].astype(BF16)
        points[pl.ds(g, LONS_PAD, stride=STRIDE), :] = matmul(basis_back[...], spec) * scale
        return carry

    lax.fori_loop(0, ROWS, one, 0, unroll=U_ROW)


def spec_block(b, size=256):
    return pl.ds(pl.multiple_of(b * size, size), size)


def analyse_dense(rows_spec, table, dense):
    def one(b, carry):
        for mode in range(2):
            value = jnp.concatenate(
                [both(rows_spec, group(b * 4 + mode * 2 + part)) for part in range(2)], axis=0
            )
            full = matmul(table[mode], value.astype(BF16)).astype(BF16)
            for part in range(2):
                start = pl.multiple_of(b * 512 + part * 256 + mode * 128, 128)
                dense[pl.ds(start, 128), :] = full[128 * part : 128 * part + 128]
        return carry

    lax.fori_loop(0, LON_BLOCKS, one, 0, unroll=U_BLK)


def store_modes(b, part, modes, pieces, parts):
    for lat in range(4):
        tile = modes[32 * lat : 32 * lat + 32]
        starts = [piece_start(b, lat, *piece) for piece in pieces]
        if part == 0:
            parts[0][starts[0], :] = tile
        else:
            parts[1][starts[1], :] = tile[0:16]
            parts[2][starts[2], :] = tile[16:32]


def load_modes(b, pieces, full):
    tiles = [[], []]
    for lat in range(4):
        values = [full[i][piece_start(b, lat, *piece), :] for i, piece in enumerate(pieces)]
        tiles[0].append(values[0])
        tiles[1] += values[1:]
    return jnp.concatenate(tiles[0] + tiles[1], axis=0)


def select_modes(dense, slots, parts):
    def one(b, carry):
        hot = one_hot_turned(slots, b)
        for part in range(2):
            modes = matmul(hot, dense[spec_block(b * 2 + part), :]).astype(BF16)
            for h in range(2):
                here = modes[:, HALF * h : HALF * h + HALF]
                store_modes(b, part, here, HALVES[h], parts[h])
        return carry

    lax.fori_loop(0, LON_BLOCKS, one, 0, unroll=U_BLK)


def build_analysis(slots, table, out, low, high):
    def one(b, carry):
        hot = one_hot_turned(slots, b)
        for part in range(2):
            for mode in range(2):
                value = matmul(
                    hot[:, 128 * mode : 128 * mode + 128],
                    table[mode, 128 * part : 128 * part + 128, :],
                )
                start = pl.multiple_of(b * 256 + part * 128, 128)
                out[pl.ds(start, 128), 128 * mode : 128 * mode + 128] = value.astype(BF16)
        return carry

    lax.fori_loop(low, high, one, 0, unroll=U_BUILD)


def build_synthesis(slots, table, out, low, high):
    def one(b, carry):
        hot = one_hot(slots, b)
        for part in range(2):
            for mode in range(2):
                value = matmul(
                    table[mode, :, 128 * part : 128 * part + 128],
                    hot[128 * mode : 128 * mode + 128],
                )
                start = pl.multiple_of(b * 256 + mode * 128, 128)
                out[pl.ds(start, 128), 128 * part : 128 * part + 128] = value.astype(BF16)
        return carry

    lax.fori_loop(low, high, one, 0, unroll=U_BUILD)


def analyse_latitude(rows_spec, table, pieces, parts):
    def one(b, carry):
        value = jnp.concatenate([rows_spec[group(b * 4 + q), :] for q in range(4)], axis=0)
        modes = matmul(table[spec_block(b), :], value.astype(BF16)).astype(BF16)
        for part in range(2):
            store_modes(b, part, modes[128 * part : 128 * part + 128], pieces, parts)
        return carry

    lax.fori_loop(0, LON_BLOCKS, one, 0, unroll=U_BLK)


def synthesise_latitude(pieces, full, table, rows_spec):
    def one(b, carry):
        value = matmul(table[spec_block(b), :], load_modes(b, pieces, full))
        for q in range(4):
            rows_spec[group(b * 4 + q), :] = value[ROWS * q : ROWS * q + ROWS]
        return carry

    lax.fori_loop(0, LON_BLOCKS, one, 0, unroll=U_BLK)


def gelu_slope(x):
    c, a = math.sqrt(2.0 / math.pi), 0.044715
    square = x * x
    t = jnp.tanh(x * (c + (c * a) * square))
    half = 0.5 + 0.5 * t
    return half + x * (half * (1.0 - t)) * (c + (3.0 * c * a) * square)


def hidden_gradient(out_grad, w2, hidden, low, high):
    def one(i, carry):
        grad = out_grad[pl.ds(i * GROUP, GROUP)].reshape(GROUP * ROWS, CH)
        here = pl.ds(pl.multiple_of(i * (GROUP * ROWS), GROUP * ROWS), GROUP * ROWS)
        for k in range(HID // CHUNK):
            cols = slice(CHUNK * k, CHUNK * k + CHUNK)
            hidden[here, cols] = matmul(grad, w2[cols, :], (1, 1)).astype(BF16)
        return carry

    lax.fori_loop(low, high, one, 0)


def pointwise(points, hidden, w1, low, high):
    def one(i, carry):
        here = pl.ds(pl.multiple_of(i * (GROUP * ROWS), GROUP * ROWS), GROUP * ROWS)
        value = [both(points, group(i * GROUP + j)).astype(BF16) for j in range(GROUP)]
        value = jnp.concatenate(value, axis=0)
        total = None
        for k in range(HID // CHUNK):
            cols = slice(CHUNK * k, CHUNK * k + CHUNK)
            pre = matmul(value, w1[:, cols])
            pre_grad = (gelu_slope(pre) * hidden[here, cols].astype(F32)).astype(BF16)
            term = matmul(pre_grad, w1[:, cols], (1, 1))
            total = term if total is None else total + term
        for j in range(GROUP):
            for h in range(2):
                points[h][group(i * GROUP + j), :] = total[
                    ROWS * j : ROWS * j + ROWS, HALF * h : HALF * h + HALF
                ]
        return carry

    lax.fori_loop(low, high, one, 0)


BETAS = HALF // BS
MIX = 16


def match_lanes(high, lane_first):
    shape = (CH, HALF) if lane_first else (HALF, CH)
    lane = lax.broadcasted_iota(jnp.int32, shape, 0 if lane_first else 1)
    channel = lax.broadcasted_iota(jnp.int32, shape, 1 if lane_first else 0) & (BS - 1)
    half = lax.shift_right_logical(lane, 4) if high else lane & (BS - 1)
    return jnp.where(channel == half, 1.0, 0.0).astype(BF16)


def block_mask():
    beta = lax.broadcasted_iota(jnp.int32, (BETAS, HALF), 0)
    channel = lax.broadcasted_iota(jnp.int32, (BETAS, HALF), 1)
    return jnp.where(beta == lax.shift_right_logical(channel, 4), 1.0, 0.0)[None]


def exact(value, ones):
    high = value.astype(BF16)
    low = (value - high.astype(F32)).astype(BF16)
    return matmul(high, ones) + matmul(low, ones)


def widen_weight(weight, wide):
    def one(e, carry):
        for part in range(2):
            value = weight[e, part].astype(F32)
            for h in range(2):
                start = pl.multiple_of((part * KEEP + e) * BETAS, BETAS)
                wide[h][pl.ds(start, BETAS), :] = value[BETAS * h : BETAS * h + BETAS]
        return carry

    lax.fori_loop(0, KEEP, one, 0, unroll=4)


def spread(modes, high, out):
    mask, match = block_mask(), match_lanes(high, False)
    for i in range(2 * KEEP // MIX):
        value = modes[MIX * i : MIX * i + MIX, :]
        wide = (value[:, None, :] * mask).reshape(MIX * BETAS, HALF)
        out[MIX * BETAS * i : MIX * BETAS * (i + 1), :] = exact(wide, match)


def mixing_rows(i):
    return [
        slice((part * KEEP + MIX * i) * BETAS, (part * KEEP + MIX * (i + 1)) * BETAS)
        for part in range(2)
    ]


def mix(wide, weight, backward):
    mask, sums = block_mask(), match_lanes(backward, True)
    out = [[], []]
    for i in range(KEEP // MIX):
        first, second = mixing_rows(i)
        re, im, wr, wi = wide[first, :], wide[second, :], weight[first, :], weight[second, :]
        if backward:
            terms = re * wr + im * wi, im * wr - re * wi
        else:
            terms = re * wr - im * wi, re * wi + im * wr
        for part, term in enumerate(terms):
            total = exact(term, sums).reshape(MIX, BETAS, HALF) * mask
            out[part].append(jnp.sum(total, axis=1))
    return jnp.concatenate(out[0] + out[1], axis=0).astype(BF16)


def weight_gradient(h, wide_in, wide_grad, out):
    for i in range(KEEP // MIX):
        first, second = mixing_rows(i)
        ar, ai, br, bi = wide_in[first, :], wide_in[second, :], wide_grad[first, :], wide_grad[second, :]
        here, betas = slice(MIX * i, MIX * i + MIX), slice(BETAS * h, BETAS * h + BETAS)
        out[here, 0, betas, :] = (ar * br + ai * bi).reshape(MIX, BETAS, CH)
        out[here, 1, betas, :] = (ar * bi - ai * br).reshape(MIX, BETAS, CH)


def kernel(fwd_scale, syn_scale, *refs):
    refs = list(refs)

    def take(n):
        taken = refs[:n]
        del refs[:n]
        return taken

    field_hbm, out_grad_hbm, weight_hbm, w1_hbm, w2_hbm, kept = take(6)
    basis_hbm, back_hbm, plain_hbm, doubled_hbm, plain_back_hbm, doubled_back_hbm = take(6)
    part_hbm, grad_hbm = take(2)
    field, out_grad, weight, w1, w2 = take(5)
    basis, basis_back, plain, doubled, plain_back, doubled_back = take(6)
    load_sems, store_sems = take(2)
    (spectral_grad,) = take(1)
    points, rows_spec = take(2), take(2)
    parts, full = [take(3), take(3)], [take(3), take(3)]
    tables, hidden, slots, own, other, slots_full = take(6)
    modes, weights, wide_in, wide_grad = take(2), take(2), take(2), take(2)
    slot_sems = take(7)
    gather_sems = [take(4), take(4)]
    scatter = [take(25), take(25)]
    analysis, synthesis = tables.at[0:8192], tables.at[8192:16384]

    at = own_place()
    lat, lon = lax.axis_index("lat"), lax.axis_index("lon")
    greeted = greet(at)
    loads = []
    for i, (src, dst) in enumerate(
        [
            (field_hbm, field),
            (basis_hbm.at[lon], basis),
            (doubled_hbm.at[lat], doubled),
            (plain_hbm.at[lat], plain),
            (plain_back_hbm.at[lat], plain_back),
            (weight_hbm, weight),
            (w2_hbm, w2),
            (out_grad_hbm, out_grad),
            (back_hbm.at[lon], basis_back),
            (w1_hbm, w1),
            (doubled_back_hbm.at[lat], doubled_back),
        ]
    ):
        copy = pltpu.make_async_copy(src, dst, load_sems.at[i])
        copy.start()
        loads.append(copy)
    own[...] = own_slots(at, kept)
    loads[0].wait()
    fill_points(field, points)
    pl.semaphore_wait(pltpu.get_barrier_semaphore(), greeted)

    collecting = gather_slots(at, own, other, slots_full, slot_sems)
    next(collecting)
    loads[1].wait()
    analyse_longitude(points, basis, rows_spec)
    next(collecting)
    loads[2].wait()
    analyse_dense(rows_spec, doubled, tables)
    next(collecting, None)
    collect_slots(slots_full, slots)
    select_modes(tables, slots, parts)

    stores = []

    def store(src, dst):
        stores.append(pltpu.make_async_copy(src, dst, store_sems.at[len(stores)]))
        stores[-1].start()

    def finish(h):
        lanes = slice(HALF * h, HALF * h + HALF)

        def one(j, carry):
            field[j, :, lanes] = points[h][group(j), :].astype(BF16)
            return carry

        lax.fori_loop(0, LONS, one, 0, unroll=U_FILL)
        store(field.at[:, :, lanes], part_hbm.at[:, :, lanes])

    def exchange(h, scale, backward, synthesised):
        wide = (wide_grad if backward else wide_in)[h]
        yield from reduce_scatter(at, HALVES[h], parts[h], scale, modes[h], scatter[h])
        spread(modes[h], not backward, wide)
        put_own(at, HALVES[h], mix(wide, weights[h], backward), full[h])
        yield from gather(at, HALVES[h], full[h], gather_sems[h])
        synthesise_latitude(HALVES[h], full[h], synthesis, rows_spec[h])
        synthesise_longitude(rows_spec[h], basis_back, points[h], synthesised)
        if backward:
            finish(h)

    def drive(first, second, work, before=lambda: None):
        next(first)
        before()
        next(second)
        for _ in range(6):
            for task in work[:WORK]:
                task()
            del work[:WORK]
            next(first)
            next(second)
        for task in work:
            task()
        next(first)
        next(first, None)
        next(second)
        next(second, None)

    quarter = LON_BLOCKS // 4
    work = [lambda: [copy.wait() for copy in loads[3:]]]
    for low in range(0, LON_BLOCKS, quarter):
        span = (low, low + quarter)
        work += [
            functools.partial(build_analysis, slots, plain, analysis, *span),
            functools.partial(build_synthesis, slots, plain_back, synthesis, *span),
        ]
    work.insert(1, functools.partial(widen_weight, weight, weights))
    for i in range(LONS // GROUP):
        work.append(functools.partial(hidden_gradient, out_grad, w2, hidden, i, i + 1))
    drive(*[exchange(h, fwd_scale, False, syn_scale) for h in range(2)], work)

    pointwise(points, hidden, w1, 0, LONS // GROUP)

    def analyse(h):
        analyse_longitude(points[h : h + 1], basis, rows_spec[h : h + 1])
        analyse_latitude(rows_spec[h], analysis, HALVES[h], parts[h])

    analyse(0)
    work = []
    for low in range(0, LON_BLOCKS, quarter):
        work.append(
            functools.partial(
                build_synthesis, slots, doubled_back, synthesis, low, low + quarter
            )
        )
        work += [lambda: None] * (WORK - 1)
    for h in range(2):
        work.append(
            functools.partial(weight_gradient, h, wide_in[h], wide_grad[h], spectral_grad)
        )
    work.append(lambda: store(spectral_grad, grad_hbm))
    drive(
        *[exchange(h, syn_scale, True, fwd_scale) for h in range(2)],
        work,
        lambda: analyse(1),
    )

    for copy in stores:
        copy.wait()


def kernel_scratch():
    v = pltpu.VMEM
    pieces = [v((128 * size, HALF), BF16) for half in HALVES for size, _ in half]
    return [
        v((LONS, ROWS, CH), BF16),
        v((LONS, ROWS, CH), BF16),
        v((KEEP, 2, CH // BS, BS * BS), BF16),
        v((CH, HID), BF16),
        v((HID, CH), BF16),
        v((2 * KM, LONS_PAD), BF16),
        v((LONS_PAD, 2 * KM), BF16),
        v((2, 2 * KLAT, 2 * ROWS), BF16),
        v((2, 2 * KLAT, 2 * ROWS), BF16),
        v((2, 2 * ROWS, 2 * KLAT), BF16),
        v((2, 2 * ROWS, 2 * KLAT), BF16),
        pltpu.SemaphoreType.DMA((11,)),
        pltpu.SemaphoreType.DMA((3,)),
        v((KEEP, 2, CH // BS, BS * BS), F32),
        *[v((LONS_PAD * STRIDE, HALF), F32)] * 2,
        *[v((2 * KM * STRIDE, HALF), F32)] * 2,
        *pieces,
        *pieces,
        v((16384, CH), BF16),
        v((LONS * ROWS, HID), BF16),
        v((LON_BLOCKS, 128), F32),
        v((8, 128), F32),
        v((8, 128), F32),
        v((512, 128), F32),
        *[v((2 * KEEP, HALF), F32)] * 2,
        *[v((2 * KEEP * BETAS, CH), F32)] * 6,
        *pair_of_sems(1),
        *pair_of_sems(3),
        *pair_of_sems(4, 4),
        pltpu.SemaphoreType.REGULAR,
        *[*pair_of_sems(3, 3, 3), *pair_of_sems(3, 4)] * 2,
        *scatter_scratch(HALVES[0]),
        *scatter_scratch(HALVES[1]),
    ]


def result_kernel(out_grad, part, grad, out, grad_out):
    out[...] = (out_grad[...].astype(F32) + part[...].astype(F32)).astype(BF16)
    grad_out[...] = grad[...]


def result_call(out_grad, part, grad):
    blocks = 4
    point = pl.BlockSpec((LONS * ROWS // blocks, CH), lambda i: (i, 0))
    mode = pl.BlockSpec((2 * KEEP * CH // BS // blocks, BS * BS), lambda i: (i, 0))
    return pl.pallas_call(
        result_kernel,
        grid=(blocks,),
        out_shape=(
            jax.ShapeDtypeStruct(out_grad.shape, BF16),
            jax.ShapeDtypeStruct(grad.shape, F32),
        ),
        in_specs=[point, point, mode],
        out_specs=(point, mode),
        compiler_params=pltpu.CompilerParams(vmem_limit_bytes=LIMIT),
        name="results",
    )(out_grad, part, grad)


def longitude_tables(lon_total):
    j = np.arange(lon_total).reshape(-1, LONS)
    j = np.pad(j, ((0, 0), (0, LONS_PAD - LONS)))
    q = np.arange(2 * KM)
    angles = (j[:, None, :] * (q // 2)[None, :, None] % lon_total) * (2.0 * math.pi / lon_total)
    basis = np.where((q % 2)[None, :, None] == 0, np.cos(angles), -np.sin(angles))
    basis[:, :, LONS:] = 0.0
    basis = basis.astype(np.float32)
    return jnp.asarray(basis, BF16), jnp.asarray(np.swapaxes(basis, 1, 2), BF16)


def latitude_tables(lat_total):
    wave = np.arange(KLAT) - KLAT // 2

    def angles(ids):
        return (wave[None, :, None] * ids[:, None, :] % (2 * lat_total)) * (math.pi / lat_total)

    ids = np.arange(lat_total).reshape(-1, ROWS)
    upper, lower = angles(ids), angles(2 * lat_total - 1 - ids)
    cu, su, cl, sl = np.cos(upper), np.sin(upper), np.cos(lower), np.sin(lower)

    def table(c, s):
        top, bottom = np.concatenate([c, s], axis=2), np.concatenate([-s, c], axis=2)
        return np.concatenate([top, bottom], axis=1)

    plain = np.stack([table(cu, su)] * 2, axis=1)
    doubled = np.stack([table(cu + cl, su + sl), table(cu - cl, su - sl)], axis=1)
    tables = []
    for value in (plain, doubled, np.swapaxes(plain, 2, 3), np.swapaxes(doubled, 2, 3)):
        tables.append(jnp.asarray(value.astype(np.float32), BF16))
    return tables


def body(in_field, out_grad, spec_weight, inner_weight, output_projection_weight, kept_modes):
    lat_parts, lon_parts = lax.axis_size("lat"), lax.axis_size("lon")
    lat_total, lon_total = ROWS * lat_parts, LONS * lon_parts
    fwd_scale = 1.0 / math.sqrt(2 * lat_total * lon_total)
    syn_scale = 1.0 / math.sqrt(KEEP * lat_parts * lon_parts)
    hbm = pl.BlockSpec(memory_space=pl.ANY)
    spectral_part, spectral_grad = pl.pallas_call(
        functools.partial(kernel, fwd_scale, syn_scale),
        out_shape=(
            jax.ShapeDtypeStruct((LONS, ROWS, CH), BF16),
            jax.ShapeDtypeStruct((KEEP, 2, CH // BS, BS * BS), F32),
        ),
        in_specs=[hbm] * 5 + [VMEM] + [hbm] * 6,
        out_specs=(hbm, hbm),
        scratch_shapes=kernel_scratch(),
        compiler_params=pltpu.CompilerParams(
            collective_id=0, has_side_effects=True, vmem_limit_bytes=LIMIT
        ),
        name="layer_gradients",
    )(
        jnp.swapaxes(in_field, 0, 1),
        jnp.swapaxes(out_grad, 0, 1),
        spec_weight,
        inner_weight,
        output_projection_weight,
        kept_modes.reshape(1, KEEP),
        *longitude_tables(lon_total),
        *latitude_tables(lat_total),
    )
    input_grad, spectral_grad = result_call(
        jnp.swapaxes(out_grad, 0, 1).reshape(LONS * ROWS, CH),
        spectral_part.reshape(LONS * ROWS, CH),
        spectral_grad.reshape(2 * KEEP * CH // BS, BS * BS),
    )
    return (
        jnp.swapaxes(input_grad.reshape(LONS, ROWS, CH), 0, 1),
        spectral_grad.reshape(KEEP, 2, CH // BS, BS * BS),
    )


def solution(mesh):
    return jax.shard_map(
        body,
        mesh=mesh,
        in_specs=(
            P("lat", "lon", None),
            P("lat", "lon", None),
            P(("lat", "lon"), None, None, None),
            P(),
            P(),
            P(("lat", "lon")),
        ),
        out_specs=(P("lat", "lon", None), P(("lat", "lon"), None, None, None)),
        check_vma=False,
    )
```

```python
import functools
import math

import jax
import jax.numpy as jnp
import numpy as np
from jax import lax
from jax.experimental import pallas as pl
from jax.experimental.pallas import tpu as pltpu
from jax.sharding import PartitionSpec as P

BS = 16
KM = 64
KLAT = 128
RING = 4
STEPS = (2, 1, 3)
ROWS, LONS, CH, HID = 64, 45, 256, 1024
LONS_PAD = 48
LON_BLOCKS = 32
KEEP = 32
ORDERS = (("xyz", "yzx"), ("yzx", "zxy"), ("zxy", "xyz"))
HALVES = (
    ((32, ORDERS[0]), (16, ORDERS[1]), (16, ORDERS[2])),
    ((32, ORDERS[1]), (16, ORDERS[2]), (16, ORDERS[0])),
)
HALF = 128
STRIDE = 72
MESH = pl.DeviceIdType.MESH
F32, BF16 = jnp.float32, jnp.bfloat16
VMEM = pl.BlockSpec(memory_space=pltpu.VMEM)
LIMIT = 60 << 20
U_FILL, U_ROW, U_BLK, U_BUILD, GROUP, CHUNK, WORK = 5, 16, 8, 4, 9, 256, 2


def matmul(a, b, contract=(1, 0)):
    dims = (((contract[0],), (contract[1],)), ((), ()))
    return lax.dot_general(a, b, dims, preferred_element_type=F32)


def own_place():
    lat, lon = lax.axis_index("lat"), lax.axis_index("lon")
    return {
        "x": lax.div(lon, 8),
        "y": lax.rem(lon, 4),
        "z": lax.rem(lax.div(lon, 4), 2) * 2 + lax.div(lat, 2),
        "core": lax.rem(lat, 2),
    }


def moved(at, axis, step):
    return {**at, axis: lax.rem(at[axis] + step, 2 if axis == "core" else RING)}


def device_of(at):
    return (lax.rem(at["z"], 2) * 2 + at["core"], at["x"] * 8 + lax.div(at["z"], 2) * 4 + at["y"])


def greet(at):
    partners = [moved(at, axis, step) for axis in "xyz" for step in STEPS] + [moved(at, "core", 1)]
    for partner in partners:
        pl.semaphore_signal(
            pltpu.get_barrier_semaphore(),
            inc=1,
            device_id=device_of(partner),
            device_id_type=MESH,
        )
    return len(partners)


def send(src, dst, sems, target):
    copy = pltpu.make_async_remote_copy(
        src_ref=src,
        dst_ref=dst,
        send_sem=sems[0],
        recv_sem=sems[1],
        device_id=device_of(target),
        device_id_type=MESH,
    )
    copy.start()
    return copy


def rows(start, size):
    return pl.ds(pl.multiple_of(start, math.gcd(size, 16)), size)


def index_of(at, order):
    index = 0
    for name in order:
        index = index * RING + at[name]
    return index


def by_core(core, values):
    return values[0] + (values[1] - values[0]) * core


def piece_index(at, core, orders, depth=3):
    return by_core(core, [index_of(at, order[:depth]) for order in orders])


def along(at, orders, depth, step):
    moves = [moved(at, order[depth], step) for order in orders]
    there = {name: by_core(at["core"], [move[name] for move in moves]) for name in "xyz"}
    return {**there, "core": at["core"]}


def wait_bytes(ref, sem):
    pltpu.make_async_copy(ref, ref, sem).wait()


def dma(*shape):
    return pltpu.SemaphoreType.DMA(shape)


def gather_sems():
    return [dma(3), dma(3, 2), dma(3, 3), dma(3)]


def gather(at, pieces, full, sems):
    sent, recv, far_recv, core_recv = sems
    core = at["core"]
    sibling = moved(at, "core", 1)

    def slab(i, step, first, count):
        size, orders = pieces[i]
        place = lax.rem(piece_index(at, core, orders, 1) + step, RING)
        start = core * (64 * size) + place * (16 * size) + first * (8 * size)
        return full[i].at[rows(start, count * (8 * size))]

    def give(i, here, sem, target):
        send(here, here, (sent.at[i], sem), target)

    for phase in range(2):
        for i in (1, 2, 0):
            size, orders = pieces[i]
            if phase:
                wait_bytes(full[i].at[0 : 3 * size], recv.at[i, 0])
            block = size * RING**phase
            index = piece_index(at, core, orders, 3 - phase)
            here = full[i].at[rows(core * (64 * size) + index * block, block)]
            for step in STEPS:
                give(i, here, recv.at[i, phase], along(at, orders, 2 - phase, step))
        yield
    for i in (1, 2, 0):
        size, orders = pieces[i]
        wait_bytes(full[i].at[0 : 12 * size], recv.at[i, 1])
        right, left = along(at, orders, 0, 1), along(at, orders, 0, 3)
        give(i, slab(i, 0, 0, 1), far_recv.at[i, 0], right)
        give(i, slab(i, 0, 1, 1), far_recv.at[i, 0], left)
        give(i, slab(i, 0, 1, 1), far_recv.at[i, 1], right)
        give(i, slab(i, 0, 0, 1), far_recv.at[i, 1], left)
    for i in range(3):
        give(i, slab(i, 0, 0, 2), core_recv.at[i], sibling)
    yield
    for i in (1, 2, 0):
        size, orders = pieces[i]
        wait_bytes(full[i].at[0 : 16 * size], far_recv.at[i, 0])
        give(i, slab(i, 3, 0, 1), far_recv.at[i, 2], along(at, orders, 0, 1))
        give(i, slab(i, 1, 1, 1), far_recv.at[i, 2], along(at, orders, 0, 3))
    yield
    for kind, steps in ((1, (1, 3)), (2, (2,))):
        for i in (1, 2, 0):
            size, _ = pieces[i]
            wait_bytes(full[i].at[0 : 16 * size], far_recv.at[i, kind])
            for step in steps:
                give(i, slab(i, step, 0, 2), core_recv.at[i], sibling)
    yield
    for i, (size, _) in enumerate(pieces):
        wait_bytes(full[i].at[0 : 64 * size], core_recv.at[i])
        wait_bytes(full[i].at[0 : 127 * size], sent.at[i])


def scatter_scratch(pieces):
    scratch = [dma(3), dma(3, 4), dma(3, 4)]
    for size, _ in pieces:
        scratch += [
            pltpu.VMEM((64 * size, HALF), BF16),
            pltpu.VMEM((64 * size, HALF), BF16),
            pltpu.VMEM((2, 8 * size, HALF), BF16),
            pltpu.VMEM((2, 16 * size, HALF), BF16),
            pltpu.VMEM((16 * size, HALF), BF16),
            pltpu.VMEM((3, 4 * size, HALF), BF16),
            pltpu.VMEM((4 * size, HALF), BF16),
            pltpu.VMEM((3, size, HALF), BF16),
        ]
    return scratch


def reduce_scatter(at, pieces, parts, scale, out, scratch):
    sent, core_recv, recv = scratch[:3]
    bufs = [scratch[3 + 8 * i : 11 + 8 * i] for i in range(3)]
    core = at["core"]
    sibling = moved(at, "core", 1)

    def slab(i, owner, step):
        size, orders = pieces[i]
        return lax.rem(piece_index(at, owner, orders, 1) + step, RING) * (16 * size)

    for s, step in enumerate((2, 1, 3, 0)):
        for i, (size, orders) in enumerate(pieces):
            start = slab(i, 1 - core, step)
            send(
                parts[i].at[rows((1 - core) * (64 * size) + start, 16 * size)],
                bufs[i][0].at[rows(start, 16 * size)],
                (sent.at[i], core_recv.at[i, s]),
                sibling,
            )
    yield

    def give(i, step, first, kind, dst, target):
        size, _ = pieces[i]
        here = rows(slab(i, core, step) + first * (8 * size), 8 * size)
        send(bufs[i][1].at[here], dst, (sent.at[i], recv.at[i, kind]), target)

    for s, step in enumerate((2, 1, 3, 0)):
        for i, (size, orders) in enumerate(pieces):
            sib, total, onward, landed = bufs[i][:4]
            right, left = along(at, orders, 0, 1), along(at, orders, 0, 3)
            start = slab(i, core, step)
            here = rows(start, 16 * size)
            wait_bytes(sib.at[here], core_recv.at[i, s])
            mine = parts[i][rows(core * (64 * size) + start, 16 * size), :]
            total[here, :] = (mine.astype(F32) + sib[here, :].astype(F32)).astype(BF16)
            if step == 2:
                give(i, 2, 0, 0, onward.at[0], right)
                give(i, 2, 1, 0, onward.at[1], left)
            elif step == 1:
                give(i, 1, 1, 1, landed.at[0, 8 * size : 16 * size], right)
            elif step == 3:
                give(i, 3, 0, 1, landed.at[1, 0 : 8 * size], left)
    yield
    for i in (1, 2, 0):
        size, orders = pieces[i]
        _, total, onward, landed = bufs[i][:4]
        wait_bytes(onward, recv.at[i, 0])
        for way, (step, first) in enumerate(((1, 0), (3, 1))):
            here = rows(slab(i, core, step) + first * (8 * size), 8 * size)
            total[here, :] = (total[here, :].astype(F32) + onward[way].astype(F32)).astype(BF16)
            dst = landed.at[way, first * (8 * size) : (first + 1) * (8 * size)]
            give(i, step, first, 1, dst, along(at, orders, 0, step))
    yield
    for phase in range(3):
        for i in (1, 2, 0):
            size, orders = pieces[i]
            mine, landed = ((1, 3), (4, 5), (6, 7))[phase]
            mine, landed = bufs[i][mine], bufs[i][landed]
            block = size * RING ** (2 - phase)
            place = by_core(core, [at[order[phase]] for order in orders])
            total = mine[rows(place * block, block), :].astype(F32)
            wait_bytes(landed, recv.at[i, phase + 1])
            for s in range(landed.shape[0]):
                total = total + landed[s].astype(F32)
            if phase == 2:
                first = sum(before for before, _ in pieces[:i])
                out[first : first + size, :] = total * scale
                continue
            after, there = bufs[i][4 + 2 * phase], bufs[i][5 + 2 * phase]
            after[...] = total.astype(BF16)
            small = block // RING
            place = by_core(core, [at[order[phase + 1]] for order in orders])
            for s, step in enumerate(STEPS):
                send(
                    after.at[rows(lax.rem(place + step, RING) * small, small)],
                    there.at[s],
                    (sent.at[i], recv.at[i, phase + 2]),
                    along(at, orders, phase + 1, step),
                )
        if phase < 2:
            yield
    for i, (size, _) in enumerate(pieces):
        wait_bytes(parts[i].at[0 : 127 * size], sent.at[i])


def put_own(at, pieces, modes, full):
    first = 0
    for i, (size, orders) in enumerate(pieces):
        here = rows((at["core"] * 64 + piece_index(at, at["core"], orders)) * size, size)
        full[i][here, :] = modes[first : first + size]
        first += size


def own_slots(at, kept):
    lat = lax.rem(at["z"], 2) * 2 + at["core"]
    value = jnp.concatenate([kept[...]] * 4, axis=1)
    slot = (value & 1) * KLAT + lat * KEEP + lax.shift_right_logical(value, 1)
    lane = lax.broadcasted_iota(jnp.int32, (1, 128), 1)
    own = jnp.where(lax.shift_right_logical(lane, 5) == lat, slot.astype(F32), 0.0)
    return jnp.broadcast_to(own, (8, 128))


def gather_slots(at, own, other, full, sems):
    sems, past = sems
    copy = send(own, other, (sems.at[0], sems.at[1]), moved(at, "core", 1))
    for step in STEPS:
        pl.semaphore_signal(
            past, inc=1, device_id=device_of(moved(at, "y", step)), device_id_type=MESH
        )
    copy.wait_recv()
    mine = rows(index_of(at, "yzx") * 8, 8)
    full[mine, :] = own[...] + other[...]
    for step in STEPS:
        send(full.at[mine], full.at[mine], (sems.at[2], sems.at[3]), moved(at, "x", step))
    yield
    wait_bytes(full.at[0:24], sems.at[3])
    pl.semaphore_wait(past, len(STEPS))
    here = full.at[rows(index_of(at, "yz") * 32, 32)]
    ways = [(dy, dz) for dy in STEPS for dz in STEPS]
    for step in STEPS:
        ways += [(step, 0), (0, step)]
    for dy, dz in ways:
        send(here, here, (sems.at[4], sems.at[5]), moved(moved(at, "y", dy), "z", dz))
    yield
    wait_bytes(full.at[0:480], sems.at[5])
    copy.wait_send()
    wait_bytes(full.at[0:24], sems.at[2])
    wait_bytes(full.at[0:480], sems.at[4])


def collect_slots(full, slots):
    for b in range(LON_BLOCKS):
        x, zhi, y = b // 8, b // 4 % 2, b % 4
        first = ((y * 4 + zhi * 2) * 4 + x) * 8
        total = full[first : first + 8, :] + full[first + 32 : first + 40, :]
        slots[b : b + 1, :] = total[0:1]


def piece_start(b, lat, size, orders):
    order = orders[lat % 2]
    place = {"x": lax.div(b, 8), "z": lax.rem(lax.div(b, 4), 2) * 2 + lat // 2, "y": lax.rem(b, 4)}
    return rows((lat % 2 * 64 + index_of(place, order)) * size, size)


def group(i):
    return pl.ds(pl.multiple_of(i * STRIDE, 8), ROWS)


def one_hot(slots, b):
    ids = lax.broadcasted_iota(jnp.int32, (256, 128), 0).astype(F32)
    return jnp.where(ids == slots[pl.ds(b, 1), :], 1.0, 0.0).astype(BF16)


def one_hot_turned(slots, b):
    columns = jnp.transpose(jnp.broadcast_to(slots[pl.ds(b, 1), :], (128, 128)))
    ids = lax.broadcasted_iota(jnp.int32, (128, 128), 1).astype(F32)
    hot = [jnp.where(ids == columns - 128.0 * mode, 1.0, 0.0).astype(BF16) for mode in range(2)]
    return jnp.concatenate(hot, axis=1)


def both(halves, where):
    return jnp.concatenate([half[where, :] for half in halves], axis=1)


def fill_points(field, points):
    def one(j, carry):
        value = field[j].astype(F32)
        for h in range(2):
            points[h][group(j), :] = value[:, HALF * h : HALF * h + HALF]
        return carry

    lax.fori_loop(0, LONS, one, 0, unroll=U_FILL)
    for j in range(LONS, LONS_PAD):
        for h in range(2):
            points[h][group(j), :] = jnp.zeros((ROWS, HALF), F32)


def analyse_longitude(points, basis, rows_spec):
    def one(g, carry):
        value = both(points, pl.ds(g, LONS_PAD, stride=STRIDE)).astype(BF16)
        spec = matmul(basis[...], value)
        for h, half in enumerate(rows_spec):
            half[pl.ds(g, 2 * KM, stride=STRIDE), :] = spec[:, HALF * h : HALF * h + HALF]
        return carry

    lax.fori_loop(0, ROWS, one, 0, unroll=U_ROW)


def synthesise_longitude(rows_spec, basis_back, points, scale):
    def one(g, carry):
        spec = rows_spec[pl.ds(g, 2 * KM, stride=STRIDE), :].astype(BF16)
        points[pl.ds(g, LONS_PAD, stride=STRIDE), :] = matmul(basis_back[...], spec) * scale
        return carry

    lax.fori_loop(0, ROWS, one, 0, unroll=U_ROW)


def spec_block(b, size=256):
    return pl.ds(pl.multiple_of(b * size, size), size)


def analyse_dense(rows_spec, table, dense):
    def one(b, carry):
        for mode in range(2):
            value = jnp.concatenate(
                [both(rows_spec, group(b * 4 + mode * 2 + part)) for part in range(2)], axis=0
            )
            full = matmul(table[mode], value.astype(BF16)).astype(BF16)
            for part in range(2):
                start = pl.multiple_of(b * 512 + part * 256 + mode * 128, 128)
                dense[pl.ds(start, 128), :] = full[128 * part : 128 * part + 128]
        return carry

    lax.fori_loop(0, LON_BLOCKS, one, 0, unroll=U_BLK)


def store_modes(b, part, modes, pieces, parts):
    for lat in range(4):
        tile = modes[32 * lat : 32 * lat + 32]
        starts = [piece_start(b, lat, *piece) for piece in pieces]
        if part == 0:
            parts[0][starts[0], :] = tile
        else:
            parts[1][starts[1], :] = tile[0:16]
            parts[2][starts[2], :] = tile[16:32]


def load_modes(b, pieces, full):
    tiles = [[], []]
    for lat in range(4):
        values = [full[i][piece_start(b, lat, *piece), :] for i, piece in enumerate(pieces)]
        tiles[0].append(values[0])
        tiles[1] += values[1:]
    return jnp.concatenate(tiles[0] + tiles[1], axis=0)


def select_modes(dense, slots, parts):
    def one(b, carry):
        hot = one_hot_turned(slots, b)
        for part in range(2):
            modes = matmul(hot, dense[spec_block(b * 2 + part), :]).astype(BF16)
            for h in range(2):
                here = modes[:, HALF * h : HALF * h + HALF]
                store_modes(b, part, here, HALVES[h], parts[h])
        return carry

    lax.fori_loop(0, LON_BLOCKS, one, 0, unroll=U_BLK)


def build_analysis(slots, table, out, low, high):
    def one(b, carry):
        hot = one_hot_turned(slots, b)
        for part in range(2):
            for mode in range(2):
                value = matmul(
                    hot[:, 128 * mode : 128 * mode + 128],
                    table[mode, 128 * part : 128 * part + 128, :],
                )
                start = pl.multiple_of(b * 256 + part * 128, 128)
                out[pl.ds(start, 128), 128 * mode : 128 * mode + 128] = value.astype(BF16)
        return carry

    lax.fori_loop(low, high, one, 0, unroll=U_BUILD)


def build_synthesis(slots, table, out, low, high):
    def one(b, carry):
        hot = one_hot(slots, b)
        for part in range(2):
            for mode in range(2):
                value = matmul(
                    table[mode, :, 128 * part : 128 * part + 128],
                    hot[128 * mode : 128 * mode + 128],
                )
                start = pl.multiple_of(b * 256 + mode * 128, 128)
                out[pl.ds(start, 128), 128 * part : 128 * part + 128] = value.astype(BF16)
        return carry

    lax.fori_loop(low, high, one, 0, unroll=U_BUILD)


def analyse_latitude(rows_spec, table, pieces, parts):
    def one(b, carry):
        value = jnp.concatenate([rows_spec[group(b * 4 + q), :] for q in range(4)], axis=0)
        modes = matmul(table[spec_block(b), :], value.astype(BF16)).astype(BF16)
        for part in range(2):
            store_modes(b, part, modes[128 * part : 128 * part + 128], pieces, parts)
        return carry

    lax.fori_loop(0, LON_BLOCKS, one, 0, unroll=U_BLK)


def synthesise_latitude(pieces, full, table, rows_spec):
    def one(b, carry):
        value = matmul(table[spec_block(b), :], load_modes(b, pieces, full))
        for q in range(4):
            rows_spec[group(b * 4 + q), :] = value[ROWS * q : ROWS * q + ROWS]
        return carry

    lax.fori_loop(0, LON_BLOCKS, one, 0, unroll=U_BLK)


def gelu_slope(x):
    c, a = math.sqrt(2.0 / math.pi), 0.044715
    square = x * x
    t = jnp.tanh(x * (c + (c * a) * square))
    half = 0.5 + 0.5 * t
    return half + x * (half * (1.0 - t)) * (c + (3.0 * c * a) * square)


def hidden_gradient(out_grad, w2, hidden, low, high):
    def one(i, carry):
        grad = out_grad[pl.ds(i * GROUP, GROUP)].reshape(GROUP * ROWS, CH)
        here = pl.ds(pl.multiple_of(i * (GROUP * ROWS), GROUP * ROWS), GROUP * ROWS)
        for k in range(HID // CHUNK):
            cols = slice(CHUNK * k, CHUNK * k + CHUNK)
            hidden[here, cols] = matmul(grad, w2[cols, :], (1, 1)).astype(BF16)
        return carry

    lax.fori_loop(low, high, one, 0)


def pointwise(points, hidden, w1, low, high):
    def one(i, carry):
        here = pl.ds(pl.multiple_of(i * (GROUP * ROWS), GROUP * ROWS), GROUP * ROWS)
        value = [both(points, group(i * GROUP + j)).astype(BF16) for j in range(GROUP)]
        value = jnp.concatenate(value, axis=0)
        total = None
        for k in range(HID // CHUNK):
            cols = slice(CHUNK * k, CHUNK * k + CHUNK)
            pre = matmul(value, w1[:, cols])
            pre_grad = (gelu_slope(pre) * hidden[here, cols].astype(F32)).astype(BF16)
            term = matmul(pre_grad, w1[:, cols], (1, 1))
            total = term if total is None else total + term
        for j in range(GROUP):
            for h in range(2):
                points[h][group(i * GROUP + j), :] = total[
                    ROWS * j : ROWS * j + ROWS, HALF * h : HALF * h + HALF
                ]
        return carry

    lax.fori_loop(low, high, one, 0)


BETAS = HALF // BS
MIX = 16


def match_lanes(high, lane_first):
    shape = (CH, HALF) if lane_first else (HALF, CH)
    lane = lax.broadcasted_iota(jnp.int32, shape, 0 if lane_first else 1)
    channel = lax.broadcasted_iota(jnp.int32, shape, 1 if lane_first else 0) & (BS - 1)
    half = lax.shift_right_logical(lane, 4) if high else lane & (BS - 1)
    return jnp.where(channel == half, 1.0, 0.0).astype(BF16)


def block_mask():
    beta = lax.broadcasted_iota(jnp.int32, (BETAS, HALF), 0)
    channel = lax.broadcasted_iota(jnp.int32, (BETAS, HALF), 1)
    return jnp.where(beta == lax.shift_right_logical(channel, 4), 1.0, 0.0)[None]


def exact(value, ones):
    high = value.astype(BF16)
    low = (value - high.astype(F32)).astype(BF16)
    return matmul(high, ones) + matmul(low, ones)


def widen_weight(weight, wide):
    def one(e, carry):
        for part in range(2):
            value = weight[e, part].astype(F32)
            for h in range(2):
                start = pl.multiple_of((part * KEEP + e) * BETAS, BETAS)
                wide[h][pl.ds(start, BETAS), :] = value[BETAS * h : BETAS * h + BETAS]
        return carry

    lax.fori_loop(0, KEEP, one, 0, unroll=4)


def spread(modes, high, out):
    mask, match = block_mask(), match_lanes(high, False)
    for i in range(2 * KEEP // MIX):
        value = modes[MIX * i : MIX * i + MIX, :]
        wide = (value[:, None, :] * mask).reshape(MIX * BETAS, HALF)
        out[MIX * BETAS * i : MIX * BETAS * (i + 1), :] = exact(wide, match)


def mixing_rows(i):
    return [
        slice((part * KEEP + MIX * i) * BETAS, (part * KEEP + MIX * (i + 1)) * BETAS)
        for part in range(2)
    ]


def mix(wide, weight, backward):
    mask, sums = block_mask(), match_lanes(backward, True)
    out = [[], []]
    for i in range(KEEP // MIX):
        first, second = mixing_rows(i)
        re, im, wr, wi = wide[first, :], wide[second, :], weight[first, :], weight[second, :]
        if backward:
            terms = re * wr + im * wi, im * wr - re * wi
        else:
            terms = re * wr - im * wi, re * wi + im * wr
        for part, term in enumerate(terms):
            total = exact(term, sums).reshape(MIX, BETAS, HALF) * mask
            out[part].append(jnp.sum(total, axis=1))
    return jnp.concatenate(out[0] + out[1], axis=0).astype(BF16)


def weight_gradient(h, wide_in, wide_grad, out):
    for i in range(KEEP // MIX):
        first, second = mixing_rows(i)
        ar, ai, br, bi = wide_in[first, :], wide_in[second, :], wide_grad[first, :], wide_grad[second, :]
        here, betas = slice(MIX * i, MIX * i + MIX), slice(BETAS * h, BETAS * h + BETAS)
        out[here, 0, betas, :] = (ar * br + ai * bi).reshape(MIX, BETAS, CH)
        out[here, 1, betas, :] = (ar * bi - ai * br).reshape(MIX, BETAS, CH)


def kernel(fwd_scale, syn_scale, *refs):
    refs = list(refs)

    def take(n):
        taken = refs[:n]
        del refs[:n]
        return taken

    field_hbm, out_grad_hbm, weight_hbm, w1_hbm, w2_hbm, kept = take(6)
    basis_hbm, back_hbm, plain_hbm, doubled_hbm, plain_back_hbm, doubled_back_hbm = take(6)
    part_hbm, grad_hbm = take(2)
    field, out_grad, weight, w1, w2 = take(5)
    basis, basis_back, plain, doubled, plain_back, doubled_back = take(6)
    load_sems, store_sems = take(2)
    (spectral_grad,) = take(1)
    points, rows_spec = take(2), take(2)
    parts, full = [take(3), take(3)], [take(3), take(3)]
    tables, hidden, slots, own, other, slots_full = take(6)
    modes, weights, wide_in, wide_grad = take(2), take(2), take(2), take(2)
    slot_sems = take(2)
    gather_sems = [take(4), take(4)]
    scatter = [take(27), take(27)]
    analysis, synthesis = tables.at[0:8192], tables.at[8192:16384]

    at = own_place()
    lat, lon = lax.axis_index("lat"), lax.axis_index("lon")
    greeted = greet(at)
    loads = []
    for i, (src, dst) in enumerate(
        [
            (field_hbm, field),
            (basis_hbm.at[lon], basis),
            (doubled_hbm.at[lat], doubled),
            (plain_hbm.at[lat], plain),
            (plain_back_hbm.at[lat], plain_back),
            (weight_hbm, weight),
            (w2_hbm, w2),
            (out_grad_hbm, out_grad),
            (back_hbm.at[lon], basis_back),
            (w1_hbm, w1),
            (doubled_back_hbm.at[lat], doubled_back),
        ]
    ):
        copy = pltpu.make_async_copy(src, dst, load_sems.at[i])
        copy.start()
        loads.append(copy)
    own[...] = own_slots(at, kept)
    loads[0].wait()
    fill_points(field, points)
    pl.semaphore_wait(pltpu.get_barrier_semaphore(), greeted)

    collecting = gather_slots(at, own, other, slots_full, slot_sems)
    next(collecting)
    loads[1].wait()
    analyse_longitude(points, basis, rows_spec)
    next(collecting)
    loads[2].wait()
    analyse_dense(rows_spec, doubled, tables)
    next(collecting, None)
    collect_slots(slots_full, slots)
    select_modes(tables, slots, parts)

    stores = []

    def store(src, dst):
        stores.append(pltpu.make_async_copy(src, dst, store_sems.at[len(stores)]))
        stores[-1].start()

    def finish(h):
        lanes = slice(HALF * h, HALF * h + HALF)

        def one(j, carry):
            field[j, :, lanes] = points[h][group(j), :].astype(BF16)
            return carry

        lax.fori_loop(0, LONS, one, 0, unroll=U_FILL)
        store(field.at[:, :, lanes], part_hbm.at[:, :, lanes])

    def exchange(h, scale, backward, synthesised):
        wide = (wide_grad if backward else wide_in)[h]
        yield from reduce_scatter(at, HALVES[h], parts[h], scale, modes[h], scatter[h])
        spread(modes[h], not backward, wide)
        put_own(at, HALVES[h], mix(wide, weights[h], backward), full[h])
        yield from gather(at, HALVES[h], full[h], gather_sems[h])
        synthesise_latitude(HALVES[h], full[h], synthesis, rows_spec[h])
        synthesise_longitude(rows_spec[h], basis_back, points[h], synthesised)
        if backward:
            finish(h)

    def drive(first, second, work, before=lambda: None):
        next(first)
        before()
        next(second)
        for _ in range(8):
            for task in work[:WORK]:
                task()
            del work[:WORK]
            next(first)
            next(second)
        for task in work:
            task()
        next(first)
        next(first, None)
        next(second)
        next(second, None)

    quarter = LON_BLOCKS // 4
    work = [lambda: [copy.wait() for copy in loads[3:]]]
    for low in range(0, LON_BLOCKS, quarter):
        span = (low, low + quarter)
        work += [
            functools.partial(build_analysis, slots, plain, analysis, *span),
            functools.partial(build_synthesis, slots, plain_back, synthesis, *span),
        ]
    work.insert(1, functools.partial(widen_weight, weight, weights))
    for i in range(LONS // GROUP):
        work.append(functools.partial(hidden_gradient, out_grad, w2, hidden, i, i + 1))
    drive(*[exchange(h, fwd_scale, False, syn_scale) for h in range(2)], work)

    pointwise(points, hidden, w1, 0, LONS // GROUP)

    def analyse(h):
        analyse_longitude(points[h : h + 1], basis, rows_spec[h : h + 1])
        analyse_latitude(rows_spec[h], analysis, HALVES[h], parts[h])

    analyse(0)
    work = []
    for low in range(0, LON_BLOCKS, quarter):
        work.append(
            functools.partial(
                build_synthesis, slots, doubled_back, synthesis, low, low + quarter
            )
        )
        work += [lambda: None] * (WORK - 1)
    work += [lambda: None] * WORK
    for h in range(2):
        work.append(
            functools.partial(weight_gradient, h, wide_in[h], wide_grad[h], spectral_grad)
        )
    work.append(lambda: store(spectral_grad, grad_hbm))
    drive(
        *[exchange(h, syn_scale, True, fwd_scale) for h in range(2)],
        work,
        lambda: analyse(1),
    )

    for copy in stores:
        copy.wait()


def kernel_scratch():
    v = pltpu.VMEM
    pieces = [v((128 * size, HALF), BF16) for half in HALVES for size, _ in half]
    return [
        v((LONS, ROWS, CH), BF16),
        v((LONS, ROWS, CH), BF16),
        v((KEEP, 2, CH // BS, BS * BS), BF16),
        v((CH, HID), BF16),
        v((HID, CH), BF16),
        v((2 * KM, LONS_PAD), BF16),
        v((LONS_PAD, 2 * KM), BF16),
        v((2, 2 * KLAT, 2 * ROWS), BF16),
        v((2, 2 * KLAT, 2 * ROWS), BF16),
        v((2, 2 * ROWS, 2 * KLAT), BF16),
        v((2, 2 * ROWS, 2 * KLAT), BF16),
        dma(11),
        dma(3),
        v((KEEP, 2, CH // BS, BS * BS), F32),
        *[v((LONS_PAD * STRIDE, HALF), F32)] * 2,
        *[v((2 * KM * STRIDE, HALF), F32)] * 2,
        *pieces,
        *pieces,
        v((16384, CH), BF16),
        v((LONS * ROWS, HID), BF16),
        v((LON_BLOCKS, 128), F32),
        v((8, 128), F32),
        v((8, 128), F32),
        v((512, 128), F32),
        *[v((2 * KEEP, HALF), F32)] * 2,
        *[v((2 * KEEP * BETAS, CH), F32)] * 6,
        dma(6),
        pltpu.SemaphoreType.REGULAR,
        *gather_sems(),
        *gather_sems(),
        *scatter_scratch(HALVES[0]),
        *scatter_scratch(HALVES[1]),
    ]


def result_kernel(out_grad, part, grad, out, grad_out):
    out[...] = (out_grad[...].astype(F32) + part[...].astype(F32)).astype(BF16)
    grad_out[...] = grad[...]


def result_call(out_grad, part, grad):
    blocks = 4
    point = pl.BlockSpec((LONS * ROWS // blocks, CH), lambda i: (i, 0))
    mode = pl.BlockSpec((2 * KEEP * CH // BS // blocks, BS * BS), lambda i: (i, 0))
    return pl.pallas_call(
        result_kernel,
        grid=(blocks,),
        out_shape=(
            jax.ShapeDtypeStruct(out_grad.shape, BF16),
            jax.ShapeDtypeStruct(grad.shape, F32),
        ),
        in_specs=[point, point, mode],
        out_specs=(point, mode),
        compiler_params=pltpu.CompilerParams(vmem_limit_bytes=LIMIT),
        name="results",
    )(out_grad, part, grad)


def longitude_tables(lon_total):
    j = np.arange(lon_total).reshape(-1, LONS)
    j = np.pad(j, ((0, 0), (0, LONS_PAD - LONS)))
    q = np.arange(2 * KM)
    angles = (j[:, None, :] * (q // 2)[None, :, None] % lon_total) * (2.0 * math.pi / lon_total)
    basis = np.where((q % 2)[None, :, None] == 0, np.cos(angles), -np.sin(angles))
    basis[:, :, LONS:] = 0.0
    basis = basis.astype(np.float32)
    return jnp.asarray(basis, BF16), jnp.asarray(np.swapaxes(basis, 1, 2), BF16)


def latitude_tables(lat_total):
    wave = np.arange(KLAT) - KLAT // 2

    def angles(ids):
        return (wave[None, :, None] * ids[:, None, :] % (2 * lat_total)) * (math.pi / lat_total)

    ids = np.arange(lat_total).reshape(-1, ROWS)
    upper, lower = angles(ids), angles(2 * lat_total - 1 - ids)
    cu, su, cl, sl = np.cos(upper), np.sin(upper), np.cos(lower), np.sin(lower)

    def table(c, s):
        top, bottom = np.concatenate([c, s], axis=2), np.concatenate([-s, c], axis=2)
        return np.concatenate([top, bottom], axis=1)

    plain = np.stack([table(cu, su)] * 2, axis=1)
    doubled = np.stack([table(cu + cl, su + sl), table(cu - cl, su - sl)], axis=1)
    tables = []
    for value in (plain, doubled, np.swapaxes(plain, 2, 3), np.swapaxes(doubled, 2, 3)):
        tables.append(jnp.asarray(value.astype(np.float32), BF16))
    return tables


def body(in_field, out_grad, spec_weight, inner_weight, output_projection_weight, kept_modes):
    lat_parts, lon_parts = lax.axis_size("lat"), lax.axis_size("lon")
    lat_total, lon_total = ROWS * lat_parts, LONS * lon_parts
    fwd_scale = 1.0 / math.sqrt(2 * lat_total * lon_total)
    syn_scale = 1.0 / math.sqrt(KEEP * lat_parts * lon_parts)
    hbm = pl.BlockSpec(memory_space=pl.ANY)
    spectral_part, spectral_grad = pl.pallas_call(
        functools.partial(kernel, fwd_scale, syn_scale),
        out_shape=(
            jax.ShapeDtypeStruct((LONS, ROWS, CH), BF16),
            jax.ShapeDtypeStruct((KEEP, 2, CH // BS, BS * BS), F32),
        ),
        in_specs=[hbm] * 5 + [VMEM] + [hbm] * 6,
        out_specs=(hbm, hbm),
        scratch_shapes=kernel_scratch(),
        compiler_params=pltpu.CompilerParams(
            collective_id=0, has_side_effects=True, vmem_limit_bytes=LIMIT
        ),
        name="layer_gradients",
    )(
        jnp.swapaxes(in_field, 0, 1),
        jnp.swapaxes(out_grad, 0, 1),
        spec_weight,
        inner_weight,
        output_projection_weight,
        kept_modes.reshape(1, KEEP),
        *longitude_tables(lon_total),
        *latitude_tables(lat_total),
    )
    input_grad, spectral_grad = result_call(
        jnp.swapaxes(out_grad, 0, 1).reshape(LONS * ROWS, CH),
        spectral_part.reshape(LONS * ROWS, CH),
        spectral_grad.reshape(2 * KEEP * CH // BS, BS * BS),
    )
    return (
        jnp.swapaxes(input_grad.reshape(LONS, ROWS, CH), 0, 1),
        spectral_grad.reshape(KEEP, 2, CH // BS, BS * BS),
    )


def solution(mesh):
    return jax.shard_map(
        body,
        mesh=mesh,
        in_specs=(
            P("lat", "lon", None),
            P("lat", "lon", None),
            P(("lat", "lon"), None, None, None),
            P(),
            P(),
            P(("lat", "lon")),
        ),
        out_specs=(P("lat", "lon", None), P(("lat", "lon"), None, None, None)),
        check_vma=False,
    )
```

```python
import functools
import math

import jax
import jax.numpy as jnp
import numpy as np
from jax import lax
from jax.experimental import pallas as pl
from jax.experimental.pallas import tpu as pltpu
from jax.sharding import PartitionSpec as P

BS = 16
KM = 64
KLAT = 128
RING = 4
STEPS = (2, 1, 3)
ROWS, LONS, CH, HID = 64, 45, 256, 1024
LONS_PAD = 48
LON_BLOCKS = 32
KEEP = 32
ORDERS = (("xyz", "yzx"), ("yzx", "zxy"), ("zxy", "xyz"))
HALVES = (
    ((32, ORDERS[0]), (16, ORDERS[1]), (16, ORDERS[2])),
    ((32, ORDERS[1]), (16, ORDERS[2]), (16, ORDERS[0])),
)
HALF = 128
STRIDE = 72
MESH = pl.DeviceIdType.MESH
F32, BF16 = jnp.float32, jnp.bfloat16
VMEM = pl.BlockSpec(memory_space=pltpu.VMEM)
LIMIT = 60 << 20
U_FILL, U_ROW, U_BLK, U_BUILD, GROUP, CHUNK = 5, 16, 8, 4, 9, 256


def matmul(a, b, contract=(1, 0)):
    dims = (((contract[0],), (contract[1],)), ((), ()))
    return lax.dot_general(a, b, dims, preferred_element_type=F32)


def own_place():
    lat, lon = lax.axis_index("lat"), lax.axis_index("lon")
    return {
        "x": lax.div(lon, 8),
        "y": lax.rem(lon, 4),
        "z": lax.rem(lax.div(lon, 4), 2) * 2 + lax.div(lat, 2),
        "core": lax.rem(lat, 2),
    }


def moved(at, axis, step):
    return {**at, axis: lax.rem(at[axis] + step, 2 if axis == "core" else RING)}


def device_of(at):
    return (lax.rem(at["z"], 2) * 2 + at["core"], at["x"] * 8 + lax.div(at["z"], 2) * 4 + at["y"])


def greet(at):
    partners = [moved(at, axis, step) for axis in "xyz" for step in STEPS] + [moved(at, "core", 1)]
    for partner in partners:
        pl.semaphore_signal(
            pltpu.get_barrier_semaphore(),
            inc=1,
            device_id=device_of(partner),
            device_id_type=MESH,
        )
    return len(partners)


def send(src, dst, sems, target):
    copy = pltpu.make_async_remote_copy(
        src_ref=src,
        dst_ref=dst,
        send_sem=sems[0],
        recv_sem=sems[1],
        device_id=device_of(target),
        device_id_type=MESH,
    )
    copy.start()
    return copy


def rows(start, size):
    return pl.ds(pl.multiple_of(start, math.gcd(size, 16)), size)


def index_of(at, order):
    index = 0
    for name in order:
        index = index * RING + at[name]
    return index


def by_core(core, values):
    return values[0] + (values[1] - values[0]) * core


def piece_index(at, core, orders, depth=3):
    return by_core(core, [index_of(at, order[:depth]) for order in orders])


def along(at, orders, depth, step):
    moves = [moved(at, order[depth], step) for order in orders]
    there = {name: by_core(at["core"], [move[name] for move in moves]) for name in "xyz"}
    return {**there, "core": at["core"]}


def wait_bytes(ref, sem):
    pltpu.make_async_copy(ref, ref, sem).wait()


def dma(*shape):
    return pltpu.SemaphoreType.DMA(shape)


def gather_sems():
    return [dma(3), dma(3, 2), dma(3, 3), dma(3)]


def gather(at, pieces, full, sems):
    sent, recv, far_recv, core_recv = sems
    core = at["core"]
    sibling = moved(at, "core", 1)

    def slab(i, step, first, count):
        size, orders = pieces[i]
        place = lax.rem(piece_index(at, core, orders, 1) + step, RING)
        start = core * (64 * size) + place * (16 * size) + first * (8 * size)
        return full[i].at[rows(start, count * (8 * size))]

    def give(i, here, sem, target):
        send(here, here, (sent.at[i], sem), target)

    for phase in range(2):
        for i in (1, 2, 0):
            size, orders = pieces[i]
            if phase:
                wait_bytes(full[i].at[0 : 3 * size], recv.at[i, 0])
            block = size * RING**phase
            index = piece_index(at, core, orders, 3 - phase)
            here = full[i].at[rows(core * (64 * size) + index * block, block)]
            for step in STEPS:
                give(i, here, recv.at[i, phase], along(at, orders, 2 - phase, step))
        yield
    for i in (1, 2, 0):
        size, orders = pieces[i]
        wait_bytes(full[i].at[0 : 12 * size], recv.at[i, 1])
        right, left = along(at, orders, 0, 1), along(at, orders, 0, 3)
        give(i, slab(i, 0, 0, 1), far_recv.at[i, 0], right)
        give(i, slab(i, 0, 1, 1), far_recv.at[i, 0], left)
        give(i, slab(i, 0, 1, 1), far_recv.at[i, 1], right)
        give(i, slab(i, 0, 0, 1), far_recv.at[i, 1], left)
    for i in range(3):
        give(i, slab(i, 0, 0, 2), core_recv.at[i], sibling)
    yield
    for i in (1, 2, 0):
        size, orders = pieces[i]
        wait_bytes(full[i].at[0 : 16 * size], far_recv.at[i, 0])
        give(i, slab(i, 3, 0, 1), far_recv.at[i, 2], along(at, orders, 0, 1))
        give(i, slab(i, 1, 1, 1), far_recv.at[i, 2], along(at, orders, 0, 3))
    yield
    for kind, steps in ((1, (1, 3)), (2, (2,))):
        for i in (1, 2, 0):
            size, _ = pieces[i]
            wait_bytes(full[i].at[0 : 16 * size], far_recv.at[i, kind])
            for step in steps:
                give(i, slab(i, step, 0, 2), core_recv.at[i], sibling)
    yield
    for i, (size, _) in enumerate(pieces):
        wait_bytes(full[i].at[0 : 64 * size], core_recv.at[i])
        wait_bytes(full[i].at[0 : 127 * size], sent.at[i])


def scatter_scratch(pieces):
    scratch = [dma(3), dma(3, 4), dma(3, 4)]
    for size, _ in pieces:
        scratch += [
            pltpu.VMEM((64 * size, HALF), BF16),
            pltpu.VMEM((64 * size, HALF), BF16),
            pltpu.VMEM((2, 8 * size, HALF), BF16),
            pltpu.VMEM((2, 16 * size, HALF), BF16),
            pltpu.VMEM((16 * size, HALF), BF16),
            pltpu.VMEM((3, 4 * size, HALF), BF16),
            pltpu.VMEM((4 * size, HALF), BF16),
            pltpu.VMEM((3, size, HALF), BF16),
        ]
    return scratch


def reduce_scatter(at, pieces, parts, scale, out, scratch):
    sent, core_recv, recv = scratch[:3]
    bufs = [scratch[3 + 8 * i : 11 + 8 * i] for i in range(3)]
    core = at["core"]
    sibling = moved(at, "core", 1)

    def slab(i, owner, step):
        size, orders = pieces[i]
        return lax.rem(piece_index(at, owner, orders, 1) + step, RING) * (16 * size)

    for s, step in enumerate((2, 1, 3, 0)):
        for i, (size, orders) in enumerate(pieces):
            start = slab(i, 1 - core, step)
            send(
                parts[i].at[rows((1 - core) * (64 * size) + start, 16 * size)],
                bufs[i][0].at[rows(start, 16 * size)],
                (sent.at[i], core_recv.at[i, s]),
                sibling,
            )
    yield

    def give(i, step, first, kind, dst, target):
        size, _ = pieces[i]
        here = rows(slab(i, core, step) + first * (8 * size), 8 * size)
        send(bufs[i][1].at[here], dst, (sent.at[i], recv.at[i, kind]), target)

    for s, step in enumerate((2, 1, 3, 0)):
        for i, (size, orders) in enumerate(pieces):
            sib, total, onward, landed = bufs[i][:4]
            right, left = along(at, orders, 0, 1), along(at, orders, 0, 3)
            start = slab(i, core, step)
            here = rows(start, 16 * size)
            wait_bytes(sib.at[here], core_recv.at[i, s])
            mine = parts[i][rows(core * (64 * size) + start, 16 * size), :]
            total[here, :] = mine + sib[here, :]
            if step == 2:
                give(i, 2, 0, 0, onward.at[0], right)
                give(i, 2, 1, 0, onward.at[1], left)
            elif step == 1:
                give(i, 1, 1, 1, landed.at[0, 8 * size : 16 * size], right)
            elif step == 3:
                give(i, 3, 0, 1, landed.at[1, 0 : 8 * size], left)
    yield
    for i in (1, 2, 0):
        size, orders = pieces[i]
        _, total, onward, landed = bufs[i][:4]
        wait_bytes(onward, recv.at[i, 0])
        for way, (step, first) in enumerate(((1, 0), (3, 1))):
            here = rows(slab(i, core, step) + first * (8 * size), 8 * size)
            total[here, :] = total[here, :] + onward[way]
            dst = landed.at[way, first * (8 * size) : (first + 1) * (8 * size)]
            give(i, step, first, 1, dst, along(at, orders, 0, step))
    yield
    for phase in range(3):
        for i in (1, 2, 0):
            size, orders = pieces[i]
            mine, landed = ((1, 3), (4, 5), (6, 7))[phase]
            mine, landed = bufs[i][mine], bufs[i][landed]
            block = size * RING ** (2 - phase)
            place = by_core(core, [at[order[phase]] for order in orders])
            total = mine[rows(place * block, block), :].astype(F32)
            wait_bytes(landed, recv.at[i, phase + 1])
            for s in range(landed.shape[0]):
                total = total + landed[s].astype(F32)
            if phase == 2:
                first = sum(before for before, _ in pieces[:i])
                out[first : first + size, :] = total * scale
                continue
            after, there = bufs[i][4 + 2 * phase], bufs[i][5 + 2 * phase]
            after[...] = total.astype(BF16)
            small = block // RING
            place = by_core(core, [at[order[phase + 1]] for order in orders])
            for s, step in enumerate(STEPS):
                send(
                    after.at[rows(lax.rem(place + step, RING) * small, small)],
                    there.at[s],
                    (sent.at[i], recv.at[i, phase + 2]),
                    along(at, orders, phase + 1, step),
                )
        if phase < 2:
            yield
    for i, (size, _) in enumerate(pieces):
        wait_bytes(parts[i].at[0 : 127 * size], sent.at[i])


def put_own(at, pieces, modes, full):
    first = 0
    for i, (size, orders) in enumerate(pieces):
        here = rows((at["core"] * 64 + piece_index(at, at["core"], orders)) * size, size)
        full[i][here, :] = modes[first : first + size]
        first += size


def own_slots(at, kept):
    lat = lax.rem(at["z"], 2) * 2 + at["core"]
    value = jnp.concatenate([kept[...]] * 4, axis=1)
    slot = (value & 1) * KLAT + lat * KEEP + lax.shift_right_logical(value, 1)
    lane = lax.broadcasted_iota(jnp.int32, (1, 128), 1)
    own = jnp.where(lax.shift_right_logical(lane, 5) == lat, slot.astype(F32), 0.0)
    return jnp.broadcast_to(own, (8, 128))


def gather_slots(at, own, other, full, sems):
    sems, past = sems
    copy = send(own, other, (sems.at[0], sems.at[1]), moved(at, "core", 1))
    for step in STEPS:
        pl.semaphore_signal(
            past, inc=1, device_id=device_of(moved(at, "y", step)), device_id_type=MESH
        )
    copy.wait_recv()
    mine = rows(index_of(at, "yzx") * 8, 8)
    full[mine, :] = own[...] + other[...]
    for step in STEPS:
        send(full.at[mine], full.at[mine], (sems.at[2], sems.at[3]), moved(at, "x", step))
    yield
    wait_bytes(full.at[0:24], sems.at[3])
    pl.semaphore_wait(past, len(STEPS))
    here = full.at[rows(index_of(at, "yz") * 32, 32)]
    ways = [(dy, dz) for dy in STEPS for dz in STEPS]
    for step in STEPS:
        ways += [(step, 0), (0, step)]
    for dy, dz in ways:
        send(here, here, (sems.at[4], sems.at[5]), moved(moved(at, "y", dy), "z", dz))
    yield
    wait_bytes(full.at[0:480], sems.at[5])
    copy.wait_send()
    wait_bytes(full.at[0:24], sems.at[2])
    wait_bytes(full.at[0:480], sems.at[4])


def collect_slots(full, slots):
    for b in range(LON_BLOCKS):
        x, zhi, y = b // 8, b // 4 % 2, b % 4
        first = ((y * 4 + zhi * 2) * 4 + x) * 8
        total = full[first : first + 8, :] + full[first + 32 : first + 40, :]
        slots[b : b + 1, :] = total[0:1]


def piece_start(b, lat, size, orders):
    order = orders[lat % 2]
    place = {"x": lax.div(b, 8), "z": lax.rem(lax.div(b, 4), 2) * 2 + lat // 2, "y": lax.rem(b, 4)}
    return rows((lat % 2 * 64 + index_of(place, order)) * size, size)


def group(i):
    return pl.ds(pl.multiple_of(i * STRIDE, 8), ROWS)


def one_hot(slots, b):
    ids = lax.broadcasted_iota(jnp.int32, (256, 128), 0).astype(F32)
    return jnp.where(ids == slots[pl.ds(b, 1), :], 1.0, 0.0).astype(BF16)


def one_hot_turned(slots, b):
    columns = jnp.transpose(jnp.broadcast_to(slots[pl.ds(b, 1), :], (128, 128)))
    ids = lax.broadcasted_iota(jnp.int32, (128, 128), 1).astype(F32)
    hot = [jnp.where(ids == columns - 128.0 * mode, 1.0, 0.0).astype(BF16) for mode in range(2)]
    return jnp.concatenate(hot, axis=1)


def both(halves, where):
    return jnp.concatenate([half[where, :] for half in halves], axis=1)


def fill_points(field, points):
    def one(j, carry):
        value = field[j].astype(F32)
        for h in range(2):
            points[h][group(j), :] = value[:, HALF * h : HALF * h + HALF]
        return carry

    lax.fori_loop(0, LONS, one, 0, unroll=U_FILL)
    for j in range(LONS, LONS_PAD):
        for h in range(2):
            points[h][group(j), :] = jnp.zeros((ROWS, HALF), F32)


def analyse_longitude(points, basis, rows_spec):
    def one(g, carry):
        value = both(points, pl.ds(g, LONS_PAD, stride=STRIDE)).astype(BF16)
        spec = matmul(basis[...], value)
        for h, half in enumerate(rows_spec):
            half[pl.ds(g, 2 * KM, stride=STRIDE), :] = spec[:, HALF * h : HALF * h + HALF]
        return carry

    lax.fori_loop(0, ROWS, one, 0, unroll=U_ROW)


def synthesise_longitude(rows_spec, basis_back, points, scale):
    def one(g, carry):
        spec = rows_spec[pl.ds(g, 2 * KM, stride=STRIDE), :].astype(BF16)
        points[pl.ds(g, LONS_PAD, stride=STRIDE), :] = matmul(basis_back[...], spec) * scale
        return carry

    lax.fori_loop(0, ROWS, one, 0, unroll=U_ROW)


def spec_block(b, size=256):
    return pl.ds(pl.multiple_of(b * size, size), size)


def analyse_dense(rows_spec, table, dense):
    def one(b, carry):
        for mode in range(2):
            value = jnp.concatenate(
                [both(rows_spec, group(b * 4 + mode * 2 + part)) for part in range(2)], axis=0
            )
            full = matmul(table[mode], value.astype(BF16)).astype(BF16)
            for part in range(2):
                start = pl.multiple_of(b * 512 + part * 256 + mode * 128, 128)
                dense[pl.ds(start, 128), :] = full[128 * part : 128 * part + 128]
        return carry

    lax.fori_loop(0, LON_BLOCKS, one, 0, unroll=U_BLK)


def store_modes(b, part, modes, pieces, parts):
    for lat in range(4):
        tile = modes[32 * lat : 32 * lat + 32]
        starts = [piece_start(b, lat, *piece) for piece in pieces]
        if part == 0:
            parts[0][starts[0], :] = tile
        else:
            parts[1][starts[1], :] = tile[0:16]
            parts[2][starts[2], :] = tile[16:32]


def load_modes(b, pieces, full):
    tiles = [[], []]
    for lat in range(4):
        values = [full[i][piece_start(b, lat, *piece), :] for i, piece in enumerate(pieces)]
        tiles[0].append(values[0])
        tiles[1] += values[1:]
    return jnp.concatenate(tiles[0] + tiles[1], axis=0)


def select_modes(dense, slots, parts):
    def one(b, carry):
        hot = one_hot_turned(slots, b)
        for part in range(2):
            modes = matmul(hot, dense[spec_block(b * 2 + part), :]).astype(BF16)
            for h in range(2):
                here = modes[:, HALF * h : HALF * h + HALF]
                store_modes(b, part, here, HALVES[h], parts[h])
        return carry

    lax.fori_loop(0, LON_BLOCKS, one, 0, unroll=U_BLK)


def build_analysis(slots, table, out, low, high):
    def one(b, carry):
        hot = one_hot_turned(slots, b)
        for part in range(2):
            for mode in range(2):
                value = matmul(
                    hot[:, 128 * mode : 128 * mode + 128],
                    table[mode, 128 * part : 128 * part + 128, :],
                )
                start = pl.multiple_of(b * 256 + part * 128, 128)
                out[pl.ds(start, 128), 128 * mode : 128 * mode + 128] = value.astype(BF16)
        return carry

    lax.fori_loop(low, high, one, 0, unroll=U_BUILD)


def build_synthesis(slots, table, out, low, high):
    def one(b, carry):
        hot = one_hot(slots, b)
        for part in range(2):
            for mode in range(2):
                value = matmul(
                    table[mode, :, 128 * part : 128 * part + 128],
                    hot[128 * mode : 128 * mode + 128],
                )
                start = pl.multiple_of(b * 256 + mode * 128, 128)
                out[pl.ds(start, 128), 128 * part : 128 * part + 128] = value.astype(BF16)
        return carry

    lax.fori_loop(low, high, one, 0, unroll=U_BUILD)


def analyse_latitude(rows_spec, table, pieces, parts):
    def one(b, carry):
        value = jnp.concatenate([rows_spec[group(b * 4 + q), :] for q in range(4)], axis=0)
        modes = matmul(table[spec_block(b), :], value.astype(BF16)).astype(BF16)
        for part in range(2):
            store_modes(b, part, modes[128 * part : 128 * part + 128], pieces, parts)
        return carry

    lax.fori_loop(0, LON_BLOCKS, one, 0, unroll=U_BLK)


def synthesise_latitude(pieces, full, table, rows_spec):
    def one(b, carry):
        value = matmul(table[spec_block(b), :], load_modes(b, pieces, full))
        for q in range(4):
            rows_spec[group(b * 4 + q), :] = value[ROWS * q : ROWS * q + ROWS]
        return carry

    lax.fori_loop(0, LON_BLOCKS, one, 0, unroll=U_BLK)


def gelu_slope(x):
    c, a = math.sqrt(2.0 / math.pi), 0.044715
    cubic = (x * x) * jnp.asarray(c * a, x.dtype)
    linear = cubic + jnp.asarray(c, x.dtype)
    one = jnp.asarray(1.0, x.dtype)
    t = jnp.tanh(x * linear)
    return (one + t) * (one + (one - t) * (x * (linear + (cubic + cubic))))


def hidden_gradient(out_grad, w2, hidden, low, high):
    def one(i, carry):
        grad = out_grad[pl.ds(i * GROUP, GROUP)].reshape(GROUP * ROWS, CH)
        here = pl.ds(pl.multiple_of(i * (GROUP * ROWS), GROUP * ROWS), GROUP * ROWS)
        for k in range(HID // CHUNK):
            cols = slice(CHUNK * k, CHUNK * k + CHUNK)
            hidden[here, cols] = (0.5 * matmul(grad, w2[cols, :], (1, 1))).astype(BF16)
        return carry

    lax.fori_loop(low, high, one, 0)


def pointwise(points, hidden, w1, low, high):
    def one(i, carry):
        here = pl.ds(pl.multiple_of(i * (GROUP * ROWS), GROUP * ROWS), GROUP * ROWS)
        value = [both(points, group(i * GROUP + j)).astype(BF16) for j in range(GROUP)]
        value = jnp.concatenate(value, axis=0)
        total = None
        for k in range(HID // CHUNK):
            cols = slice(CHUNK * k, CHUNK * k + CHUNK)
            pre = matmul(value, w1[:, cols]).astype(BF16)
            pre_grad = gelu_slope(pre) * hidden[here, cols]
            term = matmul(pre_grad, w1[:, cols], (1, 1))
            total = term if total is None else total + term
        for j in range(GROUP):
            for h in range(2):
                points[h][group(i * GROUP + j), :] = total[
                    ROWS * j : ROWS * j + ROWS, HALF * h : HALF * h + HALF
                ]
        return carry

    lax.fori_loop(low, high, one, 0)


BETAS = HALF // BS
MIX = 16


def match_lanes(high, lane_first):
    shape = (CH, HALF) if lane_first else (HALF, CH)
    lane = lax.broadcasted_iota(jnp.int32, shape, 0 if lane_first else 1)
    channel = lax.broadcasted_iota(jnp.int32, shape, 1 if lane_first else 0) & (BS - 1)
    half = lax.shift_right_logical(lane, 4) if high else lane & (BS - 1)
    return jnp.where(channel == half, 1.0, 0.0).astype(BF16)


def block_mask():
    beta = lax.broadcasted_iota(jnp.int32, (BETAS, HALF), 0)
    channel = lax.broadcasted_iota(jnp.int32, (BETAS, HALF), 1)
    return jnp.where(beta == lax.shift_right_logical(channel, 4), 1.0, 0.0)[None]


def exact(value, ones):
    high = value.astype(BF16)
    low = (value - high.astype(F32)).astype(BF16)
    return matmul(high, ones) + matmul(low, ones)


def widen_weight(weight, wide):
    def one(e, carry):
        for part in range(2):
            value = weight[e, part].astype(F32)
            for h in range(2):
                start = pl.multiple_of((part * KEEP + e) * BETAS, BETAS)
                wide[h][pl.ds(start, BETAS), :] = value[BETAS * h : BETAS * h + BETAS]
        return carry

    lax.fori_loop(0, KEEP, one, 0, unroll=4)


def spread(modes, high, out):
    mask, match = block_mask(), match_lanes(high, False)
    for i in range(2 * KEEP // MIX):
        value = modes[MIX * i : MIX * i + MIX, :]
        wide = (value[:, None, :] * mask).reshape(MIX * BETAS, HALF)
        out[MIX * BETAS * i : MIX * BETAS * (i + 1), :] = exact(wide, match)


def mixing_rows(i):
    return [
        slice((part * KEEP + MIX * i) * BETAS, (part * KEEP + MIX * (i + 1)) * BETAS)
        for part in range(2)
    ]


def mix(wide, weight, backward):
    mask, sums = block_mask(), match_lanes(backward, True)
    out = [[], []]
    for i in range(KEEP // MIX):
        first, second = mixing_rows(i)
        re, im, wr, wi = wide[first, :], wide[second, :], weight[first, :], weight[second, :]
        if backward:
            terms = re * wr + im * wi, im * wr - re * wi
        else:
            terms = re * wr - im * wi, re * wi + im * wr
        for part, term in enumerate(terms):
            total = exact(term, sums).reshape(MIX, BETAS, HALF) * mask
            out[part].append(jnp.sum(total, axis=1))
    return jnp.concatenate(out[0] + out[1], axis=0).astype(BF16)


def weight_gradient(h, wide_in, wide_grad, out):
    for i in range(KEEP // MIX):
        first, second = mixing_rows(i)
        ar, ai, br, bi = wide_in[first, :], wide_in[second, :], wide_grad[first, :], wide_grad[second, :]
        here, betas = slice(MIX * i, MIX * i + MIX), slice(BETAS * h, BETAS * h + BETAS)
        out[here, 0, betas, :] = (ar * br + ai * bi).reshape(MIX, BETAS, CH)
        out[here, 1, betas, :] = (ar * bi - ai * br).reshape(MIX, BETAS, CH)


def kernel(fwd_scale, syn_scale, *refs):
    refs = list(refs)

    def take(n):
        taken = refs[:n]
        del refs[:n]
        return taken

    field_hbm, out_grad_hbm, weight_hbm, w1_hbm, w2_hbm, kept = take(6)
    basis_hbm, back_hbm, plain_hbm, doubled_hbm, plain_back_hbm, doubled_back_hbm = take(6)
    part_hbm, grad_hbm = take(2)
    field, out_grad, weight, w1, w2 = take(5)
    basis, basis_back, plain, doubled, plain_back, doubled_back = take(6)
    load_sems, store_sems = take(2)
    (spectral_grad,) = take(1)
    points, rows_spec = take(2), take(2)
    parts, full = [take(3), take(3)], [take(3), take(3)]
    tables, hidden, slots, own, other, slots_full = take(6)
    modes, weights, wide_in, wide_grad = take(2), take(2), take(2), take(2)
    slot_sems = take(2)
    gather_sems = [take(4), take(4)]
    scatter = [take(27), take(27)]
    analysis, synthesis = tables.at[0:8192], tables.at[8192:16384]

    at = own_place()
    lat, lon = lax.axis_index("lat"), lax.axis_index("lon")
    greeted = greet(at)
    loads = []
    for i, (src, dst) in enumerate(
        [
            (field_hbm, field),
            (basis_hbm.at[lon], basis),
            (doubled_hbm.at[lat], doubled),
            (plain_hbm.at[lat], plain),
            (plain_back_hbm.at[lat], plain_back),
            (weight_hbm, weight),
            (w2_hbm, w2),
            (out_grad_hbm, out_grad),
            (back_hbm.at[lon], basis_back),
            (w1_hbm, w1),
            (doubled_back_hbm.at[lat], doubled_back),
        ]
    ):
        copy = pltpu.make_async_copy(src, dst, load_sems.at[i])
        copy.start()
        loads.append(copy)
    own[...] = own_slots(at, kept)
    loads[0].wait()
    fill_points(field, points)
    pl.semaphore_wait(pltpu.get_barrier_semaphore(), greeted)

    collecting = gather_slots(at, own, other, slots_full, slot_sems)
    next(collecting)
    loads[1].wait()
    analyse_longitude(points, basis, rows_spec)
    next(collecting)
    loads[2].wait()
    analyse_dense(rows_spec, doubled, tables)
    next(collecting, None)
    collect_slots(slots_full, slots)
    select_modes(tables, slots, parts)

    stores = []

    def store(src, dst):
        stores.append(pltpu.make_async_copy(src, dst, store_sems.at[len(stores)]))
        stores[-1].start()

    def finish(h):
        lanes = slice(HALF * h, HALF * h + HALF)

        def one(j, carry):
            field[j, :, lanes] = points[h][group(j), :].astype(BF16)
            return carry

        lax.fori_loop(0, LONS, one, 0, unroll=U_FILL)
        store(field.at[:, :, lanes], part_hbm.at[:, :, lanes])

    def exchange(h, scale, backward, synthesised):
        wide = (wide_grad if backward else wide_in)[h]
        yield from reduce_scatter(at, HALVES[h], parts[h], scale, modes[h], scatter[h])
        spread(modes[h], not backward, wide)
        put_own(at, HALVES[h], mix(wide, weights[h], backward), full[h])
        yield from gather(at, HALVES[h], full[h], gather_sems[h])
        synthesise_latitude(HALVES[h], full[h], synthesis, rows_spec[h])
        synthesise_longitude(rows_spec[h], basis_back, points[h], synthesised)
        if backward:
            finish(h)

    def drive(first, second, work, before=lambda: None):
        next(first)
        before()
        next(second)
        for tasks in work:
            for task in tasks:
                task()
            next(first)
            next(second)
        next(first)
        next(first, None)
        next(second)
        next(second, None)

    quarter = LON_BLOCKS // 4
    tasks = []
    for low in range(0, LON_BLOCKS, quarter):
        span = (low, low + quarter)
        tasks += [
            functools.partial(build_analysis, slots, plain, analysis, *span),
            functools.partial(build_synthesis, slots, plain_back, synthesis, *span),
        ]
    for i in range(LONS // GROUP):
        tasks.append(functools.partial(hidden_gradient, out_grad, w2, hidden, i, i + 1))

    def prepare():
        for copy in loads[3:]:
            copy.wait()
        widen_weight(weight, weights)

    work = [[prepare]]
    for count in (3, 2, 2, 1, 2, 1, 2):
        work.append(tasks[:count])
        del tasks[:count]
    drive(*[exchange(h, fwd_scale, False, syn_scale) for h in range(2)], work)

    pointwise(points, hidden, w1, 0, LONS // GROUP)

    def analyse(h):
        analyse_longitude(points[h : h + 1], basis, rows_spec[h : h + 1])
        analyse_latitude(rows_spec[h], analysis, HALVES[h], parts[h])

    analyse(0)
    tables_back = [
        functools.partial(build_synthesis, slots, doubled_back, synthesis, low, low + quarter)
        for low in range(0, LON_BLOCKS, quarter)
    ]
    gradients = [
        functools.partial(weight_gradient, h, wide_in[h], wide_grad[h], spectral_grad)
        for h in range(2)
    ]
    work = [[], tables_back[:2], tables_back[2:], [], [], gradients[:1], gradients[1:]]
    work.append([lambda: store(spectral_grad, grad_hbm)])
    drive(
        *[exchange(h, syn_scale, True, fwd_scale) for h in range(2)],
        work,
        lambda: analyse(1),
    )

    for copy in stores:
        copy.wait()


def kernel_scratch():
    v = pltpu.VMEM
    pieces = [v((128 * size, HALF), BF16) for half in HALVES for size, _ in half]
    return [
        v((LONS, ROWS, CH), BF16),
        v((LONS, ROWS, CH), BF16),
        v((KEEP, 2, CH // BS, BS * BS), BF16),
        v((CH, HID), BF16),
        v((HID, CH), BF16),
        v((2 * KM, LONS_PAD), BF16),
        v((LONS_PAD, 2 * KM), BF16),
        v((2, 2 * KLAT, 2 * ROWS), BF16),
        v((2, 2 * KLAT, 2 * ROWS), BF16),
        v((2, 2 * ROWS, 2 * KLAT), BF16),
        v((2, 2 * ROWS, 2 * KLAT), BF16),
        dma(11),
        dma(3),
        v((KEEP, 2, CH // BS, BS * BS), F32),
        *[v((LONS_PAD * STRIDE, HALF), F32)] * 2,
        *[v((2 * KM * STRIDE, HALF), F32)] * 2,
        *pieces,
        *pieces,
        v((16384, CH), BF16),
        v((LONS * ROWS, HID), BF16),
        v((LON_BLOCKS, 128), F32),
        v((8, 128), F32),
        v((8, 128), F32),
        v((512, 128), F32),
        *[v((2 * KEEP, HALF), F32)] * 2,
        *[v((2 * KEEP * BETAS, CH), F32)] * 6,
        dma(6),
        pltpu.SemaphoreType.REGULAR,
        *gather_sems(),
        *gather_sems(),
        *scatter_scratch(HALVES[0]),
        *scatter_scratch(HALVES[1]),
    ]


def result_kernel(out_grad, part, grad, out, grad_out):
    out[...] = (out_grad[...].astype(F32) + part[...].astype(F32)).astype(BF16)
    grad_out[...] = grad[...]


def result_call(out_grad, part, grad):
    blocks = 2
    point = pl.BlockSpec((LONS * ROWS // blocks, CH), lambda i: (i, 0))
    mode = pl.BlockSpec((2 * KEEP * CH // BS // blocks, BS * BS), lambda i: (i, 0))
    return pl.pallas_call(
        result_kernel,
        grid=(blocks,),
        out_shape=(
            jax.ShapeDtypeStruct(out_grad.shape, BF16),
            jax.ShapeDtypeStruct(grad.shape, F32),
        ),
        in_specs=[point, point, mode],
        out_specs=(point, mode),
        compiler_params=pltpu.CompilerParams(vmem_limit_bytes=LIMIT),
        name="results",
    )(out_grad, part, grad)


def longitude_tables(lon_total):
    j = np.arange(lon_total).reshape(-1, LONS)
    j = np.pad(j, ((0, 0), (0, LONS_PAD - LONS)))
    q = np.arange(2 * KM)
    angles = (j[:, None, :] * (q // 2)[None, :, None] % lon_total) * (2.0 * math.pi / lon_total)
    basis = np.where((q % 2)[None, :, None] == 0, np.cos(angles), -np.sin(angles))
    basis[:, :, LONS:] = 0.0
    basis = basis.astype(np.float32)
    return jnp.asarray(basis, BF16), jnp.asarray(np.swapaxes(basis, 1, 2), BF16)


def latitude_tables(lat_total):
    wave = np.arange(KLAT) - KLAT // 2

    def angles(ids):
        return (wave[None, :, None] * ids[:, None, :] % (2 * lat_total)) * (math.pi / lat_total)

    ids = np.arange(lat_total).reshape(-1, ROWS)
    upper, lower = angles(ids), angles(2 * lat_total - 1 - ids)
    cu, su, cl, sl = np.cos(upper), np.sin(upper), np.cos(lower), np.sin(lower)

    def table(c, s):
        top, bottom = np.concatenate([c, s], axis=2), np.concatenate([-s, c], axis=2)
        return np.concatenate([top, bottom], axis=1)

    plain = np.stack([table(cu, su)] * 2, axis=1)
    doubled = np.stack([table(cu + cl, su + sl), table(cu - cl, su - sl)], axis=1)
    tables = []
    for value in (plain, doubled, np.swapaxes(plain, 2, 3), np.swapaxes(doubled, 2, 3)):
        tables.append(jnp.asarray(value.astype(np.float32), BF16))
    return tables


def body(in_field, out_grad, spec_weight, inner_weight, output_projection_weight, kept_modes):
    lat_parts, lon_parts = lax.axis_size("lat"), lax.axis_size("lon")
    lat_total, lon_total = ROWS * lat_parts, LONS * lon_parts
    fwd_scale = 1.0 / math.sqrt(2 * lat_total * lon_total)
    syn_scale = 1.0 / math.sqrt(KEEP * lat_parts * lon_parts)
    hbm = pl.BlockSpec(memory_space=pl.ANY)
    spectral_part, spectral_grad = pl.pallas_call(
        functools.partial(kernel, fwd_scale, syn_scale),
        out_shape=(
            jax.ShapeDtypeStruct((LONS, ROWS, CH), BF16),
            jax.ShapeDtypeStruct((KEEP, 2, CH // BS, BS * BS), F32),
        ),
        in_specs=[hbm] * 5 + [VMEM] + [hbm] * 6,
        out_specs=(hbm, hbm),
        scratch_shapes=kernel_scratch(),
        compiler_params=pltpu.CompilerParams(
            collective_id=0, has_side_effects=True, vmem_limit_bytes=LIMIT
        ),
        name="layer_gradients",
    )(
        jnp.swapaxes(in_field, 0, 1),
        jnp.swapaxes(out_grad, 0, 1),
        spec_weight,
        inner_weight,
        output_projection_weight,
        kept_modes.reshape(1, KEEP),
        *longitude_tables(lon_total),
        *latitude_tables(lat_total),
    )
    input_grad, spectral_grad = result_call(
        jnp.swapaxes(out_grad, 0, 1).reshape(LONS * ROWS, CH),
        spectral_part.reshape(LONS * ROWS, CH),
        spectral_grad.reshape(2 * KEEP * CH // BS, BS * BS),
    )
    return (
        jnp.swapaxes(input_grad.reshape(LONS, ROWS, CH), 0, 1),
        spectral_grad.reshape(KEEP, 2, CH // BS, BS * BS),
    )


def solution(mesh):
    return jax.shard_map(
        body,
        mesh=mesh,
        in_specs=(
            P("lat", "lon", None),
            P("lat", "lon", None),
            P(("lat", "lon"), None, None, None),
            P(),
            P(),
            P(("lat", "lon")),
        ),
        out_specs=(P("lat", "lon", None), P(("lat", "lon"), None, None, None)),
        check_vma=False,
    )
```

```python
import functools
import math

import jax
import jax.numpy as jnp
import numpy as np
from jax import lax
from jax.experimental import pallas as pl
from jax.experimental.pallas import tpu as pltpu
from jax.sharding import PartitionSpec as P

BS = 16
KM = 64
KLAT = 128
RING = 4
STEPS = (2, 1, 3)
ROWS, LONS, CH, HID = 64, 45, 256, 1024
LONS_PAD = 48
LON_BLOCKS = 32
KEEP = 32
ORDERS = (("xyz", "yzx"), ("yzx", "zxy"), ("zxy", "xyz"))
HALVES = (
    ((32, ORDERS[0]), (16, ORDERS[1]), (16, ORDERS[2])),
    ((32, ORDERS[1]), (16, ORDERS[2]), (16, ORDERS[0])),
)
HALF = 128
STRIDE = 72
MESH = pl.DeviceIdType.MESH
F32, BF16 = jnp.float32, jnp.bfloat16
VMEM = pl.BlockSpec(memory_space=pltpu.VMEM)
LIMIT = 60 << 20
U_FILL, U_ROW, U_BLK, U_BUILD, GROUP, CHUNK = 5, 16, 8, 4, 9, 256
U_HALF_ROW, U_HALF_BLK = 64, 32


def matmul(a, b, contract=(1, 0)):
    dims = (((contract[0],), (contract[1],)), ((), ()))
    return lax.dot_general(a, b, dims, preferred_element_type=F32)


def own_place():
    lat, lon = lax.axis_index("lat"), lax.axis_index("lon")
    return {
        "x": lax.div(lon, 8),
        "y": lax.rem(lon, 4),
        "z": lax.rem(lax.div(lon, 4), 2) * 2 + lax.div(lat, 2),
        "core": lax.rem(lat, 2),
    }


def moved(at, axis, step):
    return {**at, axis: lax.rem(at[axis] + step, 2 if axis == "core" else RING)}


def device_of(at):
    return (lax.rem(at["z"], 2) * 2 + at["core"], at["x"] * 8 + lax.div(at["z"], 2) * 4 + at["y"])


def greet(at):
    partners = [moved(at, axis, step) for axis in "xyz" for step in STEPS] + [moved(at, "core", 1)]
    for partner in partners:
        pl.semaphore_signal(
            pltpu.get_barrier_semaphore(),
            inc=1,
            device_id=device_of(partner),
            device_id_type=MESH,
        )
    return len(partners)


def send(src, dst, sems, target):
    copy = pltpu.make_async_remote_copy(
        src_ref=src,
        dst_ref=dst,
        send_sem=sems[0],
        recv_sem=sems[1],
        device_id=device_of(target),
        device_id_type=MESH,
    )
    copy.start()
    return copy


def rows(start, size):
    return pl.ds(pl.multiple_of(start, math.gcd(size, 16)), size)


def index_of(at, order):
    index = 0
    for name in order:
        index = index * RING + at[name]
    return index


def by_core(core, values):
    return values[0] + (values[1] - values[0]) * core


def piece_index(at, core, orders, depth=3):
    return by_core(core, [index_of(at, order[:depth]) for order in orders])


def along(at, orders, depth, step):
    moves = [moved(at, order[depth], step) for order in orders]
    there = {name: by_core(at["core"], [move[name] for move in moves]) for name in "xyz"}
    return {**there, "core": at["core"]}


def wait_bytes(ref, sem):
    pltpu.make_async_copy(ref, ref, sem).wait()


def dma(*shape):
    return pltpu.SemaphoreType.DMA(shape)


def gather_sems():
    return [dma(3), dma(3, 2), dma(3, 3), dma(3)]


def gather(at, pieces, full, sems):
    sent, recv, far_recv, core_recv = sems
    core = at["core"]
    sibling = moved(at, "core", 1)

    def slab(i, step, first, count):
        size, orders = pieces[i]
        place = lax.rem(piece_index(at, core, orders, 1) + step, RING)
        start = core * (64 * size) + place * (16 * size) + first * (8 * size)
        return full[i].at[rows(start, count * (8 * size))]

    def give(i, here, sem, target):
        send(here, here, (sent.at[i], sem), target)

    for phase in range(2):
        for i in (1, 2, 0):
            size, orders = pieces[i]
            if phase:
                wait_bytes(full[i].at[0 : 3 * size], recv.at[i, 0])
            block = size * RING**phase
            index = piece_index(at, core, orders, 3 - phase)
            here = full[i].at[rows(core * (64 * size) + index * block, block)]
            for step in STEPS:
                give(i, here, recv.at[i, phase], along(at, orders, 2 - phase, step))
        yield
    for i in (1, 2, 0):
        size, orders = pieces[i]
        wait_bytes(full[i].at[0 : 12 * size], recv.at[i, 1])
        right, left = along(at, orders, 0, 1), along(at, orders, 0, 3)
        give(i, slab(i, 0, 0, 1), far_recv.at[i, 0], right)
        give(i, slab(i, 0, 1, 1), far_recv.at[i, 0], left)
        give(i, slab(i, 0, 1, 1), far_recv.at[i, 1], right)
        give(i, slab(i, 0, 0, 1), far_recv.at[i, 1], left)
    for i in range(3):
        give(i, slab(i, 0, 0, 2), core_recv.at[i], sibling)
    yield
    for i in (1, 2, 0):
        size, orders = pieces[i]
        wait_bytes(full[i].at[0 : 16 * size], far_recv.at[i, 0])
        give(i, slab(i, 3, 0, 1), far_recv.at[i, 2], along(at, orders, 0, 1))
        give(i, slab(i, 1, 1, 1), far_recv.at[i, 2], along(at, orders, 0, 3))
    yield
    for kind, steps in ((1, (1, 3)), (2, (2,))):
        for i in (1, 2, 0):
            size, _ = pieces[i]
            wait_bytes(full[i].at[0 : 16 * size], far_recv.at[i, kind])
            for step in steps:
                give(i, slab(i, step, 0, 2), core_recv.at[i], sibling)
    yield
    for i, (size, _) in enumerate(pieces):
        wait_bytes(full[i].at[0 : 64 * size], core_recv.at[i])


def wait_sent(pieces, buffers, sent):
    for i, (size, _) in enumerate(pieces):
        wait_bytes(buffers[i].at[0 : 127 * size], sent.at[i])


def scatter_scratch(pieces):
    scratch = [dma(3), dma(3, 4), dma(3, 4)]
    for size, _ in pieces:
        scratch += [
            pltpu.VMEM((64 * size, HALF), BF16),
            pltpu.VMEM((64 * size, HALF), BF16),
            pltpu.VMEM((2, 8 * size, HALF), BF16),
            pltpu.VMEM((2, 16 * size, HALF), BF16),
            pltpu.VMEM((16 * size, HALF), BF16),
            pltpu.VMEM((3, 4 * size, HALF), BF16),
            pltpu.VMEM((4 * size, HALF), BF16),
            pltpu.VMEM((3, size, HALF), BF16),
        ]
    return scratch


def reduce_scatter(at, pieces, parts, scale, out, scratch):
    sent, core_recv, recv = scratch[:3]
    bufs = [scratch[3 + 8 * i : 11 + 8 * i] for i in range(3)]
    core = at["core"]
    sibling = moved(at, "core", 1)

    def slab(i, owner, step):
        size, orders = pieces[i]
        return lax.rem(piece_index(at, owner, orders, 1) + step, RING) * (16 * size)

    for s, step in enumerate((2, 1, 3, 0)):
        for i, (size, orders) in enumerate(pieces):
            start = slab(i, 1 - core, step)
            send(
                parts[i].at[rows((1 - core) * (64 * size) + start, 16 * size)],
                bufs[i][0].at[rows(start, 16 * size)],
                (sent.at[i], core_recv.at[i, s]),
                sibling,
            )
    yield

    def give(i, step, first, kind, dst, target):
        size, _ = pieces[i]
        here = rows(slab(i, core, step) + first * (8 * size), 8 * size)
        send(bufs[i][1].at[here], dst, (sent.at[i], recv.at[i, kind]), target)

    for s, step in enumerate((2, 1, 3, 0)):
        for i, (size, orders) in enumerate(pieces):
            sib, total, onward, landed = bufs[i][:4]
            right, left = along(at, orders, 0, 1), along(at, orders, 0, 3)
            start = slab(i, core, step)
            here = rows(start, 16 * size)
            wait_bytes(sib.at[here], core_recv.at[i, s])
            mine = parts[i][rows(core * (64 * size) + start, 16 * size), :]
            total[here, :] = mine + sib[here, :]
            if step == 2:
                give(i, 2, 0, 0, onward.at[0], right)
                give(i, 2, 1, 0, onward.at[1], left)
            elif step == 1:
                give(i, 1, 1, 1, landed.at[0, 8 * size : 16 * size], right)
            elif step == 3:
                give(i, 3, 0, 1, landed.at[1, 0 : 8 * size], left)
    yield
    for i in (1, 2, 0):
        size, orders = pieces[i]
        _, total, onward, landed = bufs[i][:4]
        wait_bytes(onward, recv.at[i, 0])
        for way, (step, first) in enumerate(((1, 0), (3, 1))):
            here = rows(slab(i, core, step) + first * (8 * size), 8 * size)
            total[here, :] = total[here, :] + onward[way]
            dst = landed.at[way, first * (8 * size) : (first + 1) * (8 * size)]
            give(i, step, first, 1, dst, along(at, orders, 0, step))
    yield
    for phase in range(3):
        for i in (1, 2, 0):
            size, orders = pieces[i]
            mine, landed = ((1, 3), (4, 5), (6, 7))[phase]
            mine, landed = bufs[i][mine], bufs[i][landed]
            block = size * RING ** (2 - phase)
            place = by_core(core, [at[order[phase]] for order in orders])
            total = mine[rows(place * block, block), :].astype(F32)
            wait_bytes(landed, recv.at[i, phase + 1])
            for s in range(landed.shape[0]):
                total = total + landed[s].astype(F32)
            if phase == 2:
                first = sum(before for before, _ in pieces[:i])
                out[first : first + size, :] = total * scale
                continue
            after, there = bufs[i][4 + 2 * phase], bufs[i][5 + 2 * phase]
            after[...] = total.astype(BF16)
            small = block // RING
            place = by_core(core, [at[order[phase + 1]] for order in orders])
            for s, step in enumerate(STEPS):
                send(
                    after.at[rows(lax.rem(place + step, RING) * small, small)],
                    there.at[s],
                    (sent.at[i], recv.at[i, phase + 2]),
                    along(at, orders, phase + 1, step),
                )
        if phase < 2:
            yield


def put_own(at, pieces, modes, full):
    first = 0
    for i, (size, orders) in enumerate(pieces):
        here = rows((at["core"] * 64 + piece_index(at, at["core"], orders)) * size, size)
        full[i][here, :] = modes[first : first + size]
        first += size


def own_slots(at, kept):
    lat = lax.rem(at["z"], 2) * 2 + at["core"]
    value = jnp.concatenate([kept[...]] * 4, axis=1)
    slot = (value & 1) * KLAT + lat * KEEP + lax.shift_right_logical(value, 1)
    slot = jnp.broadcast_to(slot.astype(F32), (8, 128))
    lane = lax.broadcasted_iota(jnp.int32, (8, 128), 1)
    row = lax.broadcasted_iota(jnp.int32, (8, 128), 0)
    here = (lax.shift_right_logical(lane, 5) == lat) & (row == at["x"])
    return jnp.where(here, slot, 0.0)


def gather_slots(at, own, other, line, full, sems):
    sems, past = sems
    copy = send(own, other, (sems.at[0], sems.at[1]), moved(at, "core", 1))
    for step in STEPS:
        pl.semaphore_signal(
            past, inc=1, device_id=device_of(moved(at, "y", step)), device_id_type=MESH
        )
    copy.wait_recv()
    mine = full.at[rows(index_of(at, "yz") * 8, 8)]
    both_cores = own[...] + other[...]
    line[3] = both_cores
    for s, step in enumerate(STEPS):
        send(line.at[3], line.at[s], (sems.at[2], sems.at[3]), moved(at, "x", step))
    yield
    wait_bytes(line.at[0:3], sems.at[3])
    pl.semaphore_wait(past, len(STEPS))
    mine[...] = (line[0] + line[1]) + (line[2] + line[3])
    ways = [(dy, dz) for dy in STEPS for dz in STEPS]
    for step in STEPS:
        ways += [(step, 0), (0, step)]
    for dy, dz in ways:
        send(mine, mine, (sems.at[4], sems.at[5]), moved(moved(at, "y", dy), "z", dz))
    yield
    wait_bytes(full.at[0:120], sems.at[5])
    yield
    copy.wait_send()
    wait_bytes(line.at[0:3], sems.at[2])
    wait_bytes(full.at[0:120], sems.at[4])


def collect_slots(full, slots):
    for b in range(LON_BLOCKS):
        x, zhi, y = b // 8, b // 4 % 2, b % 4
        first = (y * 4 + zhi * 2) * 8 + x
        slots[b : b + 1, :] = full[first : first + 1, :] + full[first + 8 : first + 9, :]


def piece_start(b, lat, size, orders):
    order = orders[lat % 2]
    place = {"x": lax.div(b, 8), "z": lax.rem(lax.div(b, 4), 2) * 2 + lat // 2, "y": lax.rem(b, 4)}
    return rows((lat % 2 * 64 + index_of(place, order)) * size, size)


def group(i):
    return pl.ds(pl.multiple_of(i * STRIDE, 8), ROWS)


def one_hot(slots, b):
    ids = lax.broadcasted_iota(jnp.int32, (256, 128), 0).astype(F32)
    return jnp.where(ids == slots[pl.ds(b, 1), :], 1.0, 0.0).astype(BF16)


def one_hot_turned(slots, b):
    columns = jnp.transpose(jnp.broadcast_to(slots[pl.ds(b, 1), :], (128, 128)))
    ids = lax.broadcasted_iota(jnp.int32, (128, 128), 1).astype(F32)
    hot = [jnp.where(ids == columns - 128.0 * mode, 1.0, 0.0).astype(BF16) for mode in range(2)]
    return jnp.concatenate(hot, axis=1)


def both(halves, where):
    return jnp.concatenate([half[where, :] for half in halves], axis=1)


def fill_points(field, points):
    def one(j, carry):
        value = field[j].astype(F32)
        for h in range(2):
            points[h][group(j), :] = value[:, HALF * h : HALF * h + HALF]
        return carry

    lax.fori_loop(0, LONS, one, 0, unroll=U_FILL)
    for j in range(LONS, LONS_PAD):
        for h in range(2):
            points[h][group(j), :] = jnp.zeros((ROWS, HALF), F32)


def analyse_longitude(points, basis, rows_spec):
    def one(g, carry):
        value = both(points, pl.ds(g, LONS_PAD, stride=STRIDE)).astype(BF16)
        spec = matmul(basis[...], value)
        for h, half in enumerate(rows_spec):
            half[pl.ds(g, 2 * KM, stride=STRIDE), :] = spec[:, HALF * h : HALF * h + HALF]
        return carry

    lax.fori_loop(0, ROWS, one, 0, unroll=U_ROW if len(rows_spec) == 2 else U_HALF_ROW)


def synthesise_longitude(rows_spec, basis_back, points, scale):
    def one(g, carry):
        spec = rows_spec[pl.ds(g, 2 * KM, stride=STRIDE), :].astype(BF16)
        points[pl.ds(g, LONS_PAD, stride=STRIDE), :] = matmul(basis_back[...], spec) * scale
        return carry

    lax.fori_loop(0, ROWS, one, 0, unroll=U_HALF_ROW)


def spec_block(b, size=256):
    return pl.ds(pl.multiple_of(b * size, size), size)


def analyse_dense(rows_spec, table, dense):
    def one(b, carry):
        for mode in range(2):
            value = jnp.concatenate(
                [both(rows_spec, group(b * 4 + mode * 2 + part)) for part in range(2)], axis=0
            )
            full = matmul(table[mode], value.astype(BF16)).astype(BF16)
            for part in range(2):
                start = pl.multiple_of(b * 512 + part * 256 + mode * 128, 128)
                dense[pl.ds(start, 128), :] = full[128 * part : 128 * part + 128]
        return carry

    lax.fori_loop(0, LON_BLOCKS, one, 0, unroll=U_BLK)


def store_modes(b, part, modes, pieces, parts):
    for lat in range(4):
        tile = modes[32 * lat : 32 * lat + 32]
        starts = [piece_start(b, lat, *piece) for piece in pieces]
        if part == 0:
            parts[0][starts[0], :] = tile
        else:
            parts[1][starts[1], :] = tile[0:16]
            parts[2][starts[2], :] = tile[16:32]


def load_modes(b, pieces, full):
    tiles = [[], []]
    for lat in range(4):
        values = [full[i][piece_start(b, lat, *piece), :] for i, piece in enumerate(pieces)]
        tiles[0].append(values[0])
        tiles[1] += values[1:]
    return jnp.concatenate(tiles[0] + tiles[1], axis=0)


def select_modes(dense, slots, parts):
    def one(b, carry):
        hot = one_hot_turned(slots, b)
        for part in range(2):
            modes = matmul(hot, dense[spec_block(b * 2 + part), :]).astype(BF16)
            for h in range(2):
                here = modes[:, HALF * h : HALF * h + HALF]
                store_modes(b, part, here, HALVES[h], parts[h])
        return carry

    lax.fori_loop(0, LON_BLOCKS, one, 0, unroll=U_BLK)


def build_analysis(slots, table, out, low, high):
    def one(b, carry):
        hot = one_hot_turned(slots, b)
        for part in range(2):
            for mode in range(2):
                value = matmul(
                    hot[:, 128 * mode : 128 * mode + 128],
                    table[mode, 128 * part : 128 * part + 128, :],
                )
                start = pl.multiple_of(b * 256 + part * 128, 128)
                out[pl.ds(start, 128), 128 * mode : 128 * mode + 128] = value.astype(BF16)
        return carry

    lax.fori_loop(low, high, one, 0, unroll=U_BUILD)


def build_synthesis(slots, table, out, low, high):
    def one(b, carry):
        hot = one_hot(slots, b)
        for part in range(2):
            for mode in range(2):
                value = matmul(
                    table[mode, :, 128 * part : 128 * part + 128],
                    hot[128 * mode : 128 * mode + 128],
                )
                start = pl.multiple_of(b * 256 + mode * 128, 128)
                out[pl.ds(start, 128), 128 * part : 128 * part + 128] = value.astype(BF16)
        return carry

    lax.fori_loop(low, high, one, 0, unroll=U_BUILD)


def analyse_latitude(rows_spec, table, pieces, parts):
    def one(b, carry):
        value = jnp.concatenate([rows_spec[group(b * 4 + q), :] for q in range(4)], axis=0)
        modes = matmul(table[spec_block(b), :], value.astype(BF16)).astype(BF16)
        for part in range(2):
            store_modes(b, part, modes[128 * part : 128 * part + 128], pieces, parts)
        return carry

    lax.fori_loop(0, LON_BLOCKS, one, 0, unroll=U_HALF_BLK)


def synthesise_latitude(pieces, full, table, rows_spec):
    def one(b, carry):
        value = matmul(table[spec_block(b), :], load_modes(b, pieces, full))
        for q in range(4):
            rows_spec[group(b * 4 + q), :] = value[ROWS * q : ROWS * q + ROWS]
        return carry

    lax.fori_loop(0, LON_BLOCKS, one, 0, unroll=U_HALF_BLK)


def gelu_slope(x):
    c, a = math.sqrt(2.0 / math.pi), 0.044715
    cubic = (x * x) * jnp.asarray(c * a, x.dtype)
    linear = cubic + jnp.asarray(c, x.dtype)
    one = jnp.asarray(1.0, x.dtype)
    t = jnp.tanh(x * linear)
    return (one + t) * (one + (one - t) * (x * (linear + (cubic + cubic))))


def hidden_gradient(out_grad, w2, hidden, low, high):
    def one(i, carry):
        grad = out_grad[pl.ds(i * GROUP, GROUP)].reshape(GROUP * ROWS, CH)
        here = pl.ds(pl.multiple_of(i * (GROUP * ROWS), GROUP * ROWS), GROUP * ROWS)
        for k in range(HID // CHUNK):
            cols = slice(CHUNK * k, CHUNK * k + CHUNK)
            hidden[here, cols] = (0.5 * matmul(grad, w2[cols, :], (1, 1))).astype(BF16)
        return carry

    lax.fori_loop(low, high, one, 0)


def pointwise(points, hidden, w1, low, high):
    def one(i, carry):
        here = pl.ds(pl.multiple_of(i * (GROUP * ROWS), GROUP * ROWS), GROUP * ROWS)
        value = [both(points, group(i * GROUP + j)).astype(BF16) for j in range(GROUP)]
        value = jnp.concatenate(value, axis=0)
        total = None
        for k in range(HID // CHUNK):
            cols = slice(CHUNK * k, CHUNK * k + CHUNK)
            pre = matmul(value, w1[:, cols]).astype(BF16)
            pre_grad = gelu_slope(pre) * hidden[here, cols]
            term = matmul(pre_grad, w1[:, cols], (1, 1))
            total = term if total is None else total + term
        for j in range(GROUP):
            for h in range(2):
                points[h][group(i * GROUP + j), :] = total[
                    ROWS * j : ROWS * j + ROWS, HALF * h : HALF * h + HALF
                ]
        return carry

    lax.fori_loop(low, high, one, 0)


BETAS = HALF // BS
MIX = 16


def match_lanes(high, lane_first):
    shape = (CH, HALF) if lane_first else (HALF, CH)
    lane = lax.broadcasted_iota(jnp.int32, shape, 0 if lane_first else 1)
    channel = lax.broadcasted_iota(jnp.int32, shape, 1 if lane_first else 0) & (BS - 1)
    half = lax.shift_right_logical(lane, 4) if high else lane & (BS - 1)
    return jnp.where(channel == half, 1.0, 0.0).astype(BF16)


def block_mask():
    beta = lax.broadcasted_iota(jnp.int32, (BETAS, HALF), 0)
    channel = lax.broadcasted_iota(jnp.int32, (BETAS, HALF), 1)
    return jnp.where(beta == lax.shift_right_logical(channel, 4), 1.0, 0.0)[None]


def widen_weight(weight, wide):
    def one(e, carry):
        for part in range(2):
            value = weight[e, part].astype(F32)
            for h in range(2):
                start = pl.multiple_of((part * KEEP + e) * BETAS, BETAS)
                wide[h][pl.ds(start, BETAS), :] = value[BETAS * h : BETAS * h + BETAS]
        return carry

    lax.fori_loop(0, KEEP, one, 0, unroll=4)


def spread(modes, high, out):
    mask, match = block_mask(), match_lanes(high, False)
    for i in range(2 * KEEP // MIX):
        value = modes[MIX * i : MIX * i + MIX, :]
        wide = (value[:, None, :] * mask).reshape(MIX * BETAS, HALF)
        out[MIX * BETAS * i : MIX * BETAS * (i + 1), :] = matmul(wide.astype(BF16), match)


def mixing_rows(i):
    return [
        slice((part * KEEP + MIX * i) * BETAS, (part * KEEP + MIX * (i + 1)) * BETAS)
        for part in range(2)
    ]


def mix(wide, weight, backward):
    mask, sums = block_mask(), match_lanes(backward, True)
    out = [[], []]
    for i in range(KEEP // MIX):
        first, second = mixing_rows(i)
        re, im, wr, wi = wide[first, :], wide[second, :], weight[first, :], weight[second, :]
        if backward:
            terms = re * wr + im * wi, im * wr - re * wi
        else:
            terms = re * wr - im * wi, re * wi + im * wr
        for part, term in enumerate(terms):
            total = matmul(term.astype(BF16), sums).reshape(MIX, BETAS, HALF) * mask
            out[part].append(jnp.sum(total, axis=1))
    return jnp.concatenate(out[0] + out[1], axis=0).astype(BF16)


def weight_gradient(h, wide_in, wide_grad, out):
    for i in range(KEEP // MIX):
        first, second = mixing_rows(i)
        ar, ai, br, bi = wide_in[first, :], wide_in[second, :], wide_grad[first, :], wide_grad[second, :]
        here, betas = slice(MIX * i, MIX * i + MIX), slice(BETAS * h, BETAS * h + BETAS)
        out[here, 0, betas, :] = (ar * br + ai * bi).reshape(MIX, BETAS, CH)
        out[here, 1, betas, :] = (ar * bi - ai * br).reshape(MIX, BETAS, CH)


def kernel(fwd_scale, syn_scale, *refs):
    refs = list(refs)

    def take(n):
        taken = refs[:n]
        del refs[:n]
        return taken

    field_hbm, out_grad_hbm, weight_hbm, w1_hbm, w2_hbm, kept = take(6)
    basis_hbm, back_hbm, plain_hbm, doubled_hbm, plain_back_hbm, doubled_back_hbm = take(6)
    part_hbm, grad_hbm = take(2)
    field, out_grad, weight, w1, w2 = take(5)
    basis, basis_back, plain, doubled, plain_back, doubled_back = take(6)
    load_sems, store_sems = take(2)
    (spectral_grad,) = take(1)
    points, rows_spec = take(2), take(2)
    parts, full = [take(3), take(3)], [take(3), take(3)]
    tables, hidden, slots, own, other, slots_line, slots_full = take(7)
    modes, weights, wide_in, wide_grad = take(2), take(2), take(2), take(2)
    slot_sems = take(2)
    gather_sems = [take(4), take(4)]
    scatter = [take(27), take(27)]
    analysis, synthesis = tables.at[0:8192], tables.at[8192:16384]

    at = own_place()
    lat, lon = lax.axis_index("lat"), lax.axis_index("lon")
    greeted = greet(at)
    loads = []
    for i, (src, dst) in enumerate(
        [
            (field_hbm, field),
            (basis_hbm.at[lon], basis),
            (doubled_hbm.at[lat], doubled),
            (plain_hbm.at[lat], plain),
            (plain_back_hbm.at[lat], plain_back),
            (weight_hbm, weight),
            (w2_hbm, w2),
            (out_grad_hbm, out_grad),
            (back_hbm.at[lon], basis_back),
            (w1_hbm, w1),
            (doubled_back_hbm.at[lat], doubled_back),
        ]
    ):
        copy = pltpu.make_async_copy(src, dst, load_sems.at[i])
        copy.start()
        loads.append(copy)
    own[...] = own_slots(at, kept)
    loads[0].wait()
    fill_points(field, points)
    pl.semaphore_wait(pltpu.get_barrier_semaphore(), greeted)

    collecting = gather_slots(at, own, other, slots_line, slots_full, slot_sems)
    next(collecting)
    loads[1].wait()
    analyse_longitude(points, basis, rows_spec)
    next(collecting)
    loads[2].wait()
    analyse_dense(rows_spec, doubled, tables)
    next(collecting)
    collect_slots(slots_full, slots)
    select_modes(tables, slots, parts)

    stores = []

    def store(src, dst):
        stores.append(pltpu.make_async_copy(src, dst, store_sems.at[len(stores)]))
        stores[-1].start()

    def finish(h):
        lanes = slice(HALF * h, HALF * h + HALF)

        def one(j, carry):
            field[j, :, lanes] = points[h][group(j), :].astype(BF16)
            return carry

        lax.fori_loop(0, LONS, one, 0, unroll=U_FILL)
        store(field.at[:, :, lanes], part_hbm.at[:, :, lanes])

    def exchange(h, scale, backward, synthesised):
        wide = (wide_grad if backward else wide_in)[h]
        yield from reduce_scatter(at, HALVES[h], parts[h], scale, modes[h], scatter[h])
        spread(modes[h], not backward, wide)
        put_own(at, HALVES[h], mix(wide, weights[h], backward), full[h])
        yield from gather(at, HALVES[h], full[h], gather_sems[h])
        wait_sent(HALVES[h], parts[h], scatter[h][0])
        synthesise_latitude(HALVES[h], full[h], synthesis, rows_spec[h])
        synthesise_longitude(rows_spec[h], basis_back, points[h], synthesised)
        wait_sent(HALVES[h], full[h], gather_sems[h][0])
        if backward:
            finish(h)

    def drive(first, second, work, before=lambda: None):
        next(first)
        before()
        next(second)
        for tasks in work:
            for task in tasks:
                task()
            next(first)
            next(second)
        next(first)
        next(first, None)
        next(second)
        next(second, None)

    quarter = LON_BLOCKS // 4
    tasks = []
    for low in range(0, LON_BLOCKS, quarter):
        span = (low, low + quarter)
        tasks += [
            functools.partial(build_analysis, slots, plain, analysis, *span),
            functools.partial(build_synthesis, slots, plain_back, synthesis, *span),
        ]
    for i in range(LONS // GROUP):
        tasks.append(functools.partial(hidden_gradient, out_grad, w2, hidden, i, i + 1))

    def prepare():
        next(collecting, None)
        for copy in loads[3:]:
            copy.wait()
        widen_weight(weight, weights)

    work = [[prepare]]
    for count in (3, 2, 2, 1, 2, 1, 2):
        work.append(tasks[:count])
        del tasks[:count]
    drive(*[exchange(h, fwd_scale, False, syn_scale) for h in range(2)], work)

    pointwise(points, hidden, w1, 0, LONS // GROUP)

    def analyse(h):
        analyse_longitude(points[h : h + 1], basis, rows_spec[h : h + 1])
        analyse_latitude(rows_spec[h], analysis, HALVES[h], parts[h])

    analyse(0)
    tables_back = [
        functools.partial(build_synthesis, slots, doubled_back, synthesis, low, low + quarter)
        for low in range(0, LON_BLOCKS, quarter)
    ]
    gradients = [
        functools.partial(weight_gradient, h, wide_in[h], wide_grad[h], spectral_grad)
        for h in range(2)
    ]
    work = [[], tables_back[:2], tables_back[2:], [], [], gradients[:1], gradients[1:]]
    work.append([lambda: store(spectral_grad, grad_hbm)])
    drive(
        *[exchange(h, syn_scale, True, fwd_scale) for h in range(2)],
        work,
        lambda: analyse(1),
    )

    for copy in stores:
        copy.wait()


def kernel_scratch():
    v = pltpu.VMEM
    pieces = [v((128 * size, HALF), BF16) for half in HALVES for size, _ in half]
    return [
        v((LONS, ROWS, CH), BF16),
        v((LONS, ROWS, CH), BF16),
        v((KEEP, 2, CH // BS, BS * BS), BF16),
        v((CH, HID), BF16),
        v((HID, CH), BF16),
        v((2 * KM, LONS_PAD), BF16),
        v((LONS_PAD, 2 * KM), BF16),
        v((2, 2 * KLAT, 2 * ROWS), BF16),
        v((2, 2 * KLAT, 2 * ROWS), BF16),
        v((2, 2 * ROWS, 2 * KLAT), BF16),
        v((2, 2 * ROWS, 2 * KLAT), BF16),
        dma(11),
        dma(3),
        v((KEEP, 2, CH // BS, BS * BS), F32),
        *[v((LONS_PAD * STRIDE, HALF), F32)] * 2,
        *[v((2 * KM * STRIDE, HALF), F32)] * 2,
        *pieces,
        *pieces,
        v((16384, CH), BF16),
        v((LONS * ROWS, HID), BF16),
        v((LON_BLOCKS, 128), F32),
        v((8, 128), F32),
        v((8, 128), F32),
        v((4, 8, 128), F32),
        v((128, 128), F32),
        *[v((2 * KEEP, HALF), F32)] * 2,
        *[v((2 * KEEP * BETAS, CH), F32)] * 6,
        dma(6),
        pltpu.SemaphoreType.REGULAR,
        *gather_sems(),
        *gather_sems(),
        *scatter_scratch(HALVES[0]),
        *scatter_scratch(HALVES[1]),
    ]


def result_kernel(out_grad, part, grad, out, grad_out):
    out[...] = (out_grad[...].astype(F32) + part[...].astype(F32)).astype(BF16)
    grad_out[...] = grad[...]


def result_call(out_grad, part, grad):
    blocks = 2
    point = pl.BlockSpec((LONS * ROWS // blocks, CH), lambda i: (i, 0))
    mode = pl.BlockSpec((2 * KEEP * CH // BS // blocks, BS * BS), lambda i: (i, 0))
    return pl.pallas_call(
        result_kernel,
        grid=(blocks,),
        out_shape=(
            jax.ShapeDtypeStruct(out_grad.shape, BF16),
            jax.ShapeDtypeStruct(grad.shape, F32),
        ),
        in_specs=[point, point, mode],
        out_specs=(point, mode),
        compiler_params=pltpu.CompilerParams(vmem_limit_bytes=LIMIT),
        name="results",
    )(out_grad, part, grad)


def longitude_tables(lon_total):
    j = np.arange(lon_total).reshape(-1, LONS)
    j = np.pad(j, ((0, 0), (0, LONS_PAD - LONS)))
    q = np.arange(2 * KM)
    angles = (j[:, None, :] * (q // 2)[None, :, None] % lon_total) * (2.0 * math.pi / lon_total)
    basis = np.where((q % 2)[None, :, None] == 0, np.cos(angles), -np.sin(angles))
    basis[:, :, LONS:] = 0.0
    basis = basis.astype(np.float32)
    return jnp.asarray(basis, BF16), jnp.asarray(np.swapaxes(basis, 1, 2), BF16)


def latitude_tables(lat_total):
    wave = np.arange(KLAT) - KLAT // 2

    def angles(ids):
        return (wave[None, :, None] * ids[:, None, :] % (2 * lat_total)) * (math.pi / lat_total)

    ids = np.arange(lat_total).reshape(-1, ROWS)
    upper, lower = angles(ids), angles(2 * lat_total - 1 - ids)
    cu, su, cl, sl = np.cos(upper), np.sin(upper), np.cos(lower), np.sin(lower)

    def table(c, s):
        top, bottom = np.concatenate([c, s], axis=2), np.concatenate([-s, c], axis=2)
        return np.concatenate([top, bottom], axis=1)

    plain = np.stack([table(cu, su)] * 2, axis=1)
    doubled = np.stack([table(cu + cl, su + sl), table(cu - cl, su - sl)], axis=1)
    tables = []
    for value in (plain, doubled, np.swapaxes(plain, 2, 3), np.swapaxes(doubled, 2, 3)):
        tables.append(jnp.asarray(value.astype(np.float32), BF16))
    return tables


def body(in_field, out_grad, spec_weight, inner_weight, output_projection_weight, kept_modes):
    lat_parts, lon_parts = lax.axis_size("lat"), lax.axis_size("lon")
    lat_total, lon_total = ROWS * lat_parts, LONS * lon_parts
    fwd_scale = 1.0 / math.sqrt(2 * lat_total * lon_total)
    syn_scale = 1.0 / math.sqrt(KEEP * lat_parts * lon_parts)
    hbm = pl.BlockSpec(memory_space=pl.ANY)
    spectral_part, spectral_grad = pl.pallas_call(
        functools.partial(kernel, fwd_scale, syn_scale),
        out_shape=(
            jax.ShapeDtypeStruct((LONS, ROWS, CH), BF16),
            jax.ShapeDtypeStruct((KEEP, 2, CH // BS, BS * BS), F32),
        ),
        in_specs=[hbm] * 5 + [VMEM] + [hbm] * 6,
        out_specs=(hbm, hbm),
        scratch_shapes=kernel_scratch(),
        compiler_params=pltpu.CompilerParams(
            collective_id=0, has_side_effects=True, vmem_limit_bytes=LIMIT
        ),
        name="layer_gradients",
    )(
        jnp.swapaxes(in_field, 0, 1),
        jnp.swapaxes(out_grad, 0, 1),
        spec_weight,
        inner_weight,
        output_projection_weight,
        kept_modes.reshape(1, KEEP),
        *longitude_tables(lon_total),
        *latitude_tables(lat_total),
    )
    input_grad, spectral_grad = result_call(
        jnp.swapaxes(out_grad, 0, 1).reshape(LONS * ROWS, CH),
        spectral_part.reshape(LONS * ROWS, CH),
        spectral_grad.reshape(2 * KEEP * CH // BS, BS * BS),
    )
    return (
        jnp.swapaxes(input_grad.reshape(LONS, ROWS, CH), 0, 1),
        spectral_grad.reshape(KEEP, 2, CH // BS, BS * BS),
    )


def solution(mesh):
    return jax.shard_map(
        body,
        mesh=mesh,
        in_specs=(
            P("lat", "lon", None),
            P("lat", "lon", None),
            P(("lat", "lon"), None, None, None),
            P(),
            P(),
            P(("lat", "lon")),
        ),
        out_specs=(P("lat", "lon", None), P(("lat", "lon"), None, None, None)),
        check_vma=False,
    )
```

```python
import functools
import math

import jax
import jax.numpy as jnp
import numpy as np
from jax import lax
from jax.experimental import pallas as pl
from jax.experimental.pallas import tpu as pltpu
from jax.sharding import PartitionSpec as P

BS = 16
KM = 64
KLAT = 128
RING = 4
STEPS = (2, 1, 3)
ROWS, LONS, CH, HID = 64, 45, 256, 1024
LONS_PAD = 48
LON_BLOCKS = 32
KEEP = 32
ORDERS = (("xyz", "yzx"), ("yzx", "zxy"), ("zxy", "xyz"))
HALVES = (
    ((32, ORDERS[0]), (16, ORDERS[1]), (16, ORDERS[2])),
    ((32, ORDERS[1]), (16, ORDERS[2]), (16, ORDERS[0])),
)
HALF = 128
STRIDE = 72
MESH = pl.DeviceIdType.MESH
F32, BF16 = jnp.float32, jnp.bfloat16
VMEM = pl.BlockSpec(memory_space=pltpu.VMEM)
LIMIT = 60 << 20
U_FILL, U_ROW, U_BLK, U_BUILD, GROUP, CHUNK = 5, 16, 8, 4, 9, 256
U_HALF_ROW, U_HALF_BLK = 64, 32


def matmul(a, b, contract=(1, 0)):
    dims = (((contract[0],), (contract[1],)), ((), ()))
    return lax.dot_general(a, b, dims, preferred_element_type=F32)


def own_place():
    lat, lon = lax.axis_index("lat"), lax.axis_index("lon")
    return {
        "x": lax.div(lon, 8),
        "y": lax.rem(lon, 4),
        "z": lax.rem(lax.div(lon, 4), 2) * 2 + lax.div(lat, 2),
        "core": lax.rem(lat, 2),
    }


def moved(at, axis, step):
    return {**at, axis: lax.rem(at[axis] + step, 2 if axis == "core" else RING)}


def device_of(at):
    return (lax.rem(at["z"], 2) * 2 + at["core"], at["x"] * 8 + lax.div(at["z"], 2) * 4 + at["y"])


def greet(at):
    partners = [moved(at, axis, step) for axis in "xyz" for step in STEPS] + [moved(at, "core", 1)]
    for partner in partners:
        pl.semaphore_signal(
            pltpu.get_barrier_semaphore(),
            inc=1,
            device_id=device_of(partner),
            device_id_type=MESH,
        )
    return len(partners)


def send(src, dst, sems, target):
    copy = pltpu.make_async_remote_copy(
        src_ref=src,
        dst_ref=dst,
        send_sem=sems[0],
        recv_sem=sems[1],
        device_id=target,
        device_id_type=MESH,
    )
    copy.start()
    return copy


def rows(start, size):
    return pl.ds(pl.multiple_of(start, math.gcd(size, 16)), size)


def index_of(at, order):
    index = 0
    for name in order:
        index = index * RING + at[name]
    return index


def by_core(core, values):
    return values[0] + (values[1] - values[0]) * core


def once(at, key, work):
    if key not in at["known"]:
        at["known"][key] = work()
    return at["known"][key]


def place_on(at, axis, step):
    return once(at, (axis, step), lambda: lax.rem(at[axis] + step, RING))


def piece_index(at, orders, depth=3, own=True):
    def work():
        core = at["core"] if own else 1 - at["core"]
        return by_core(core, [index_of(at, order[:depth]) for order in orders])

    return once(at, (orders, depth, own), work)


def piece_place(at, orders, depth, step, own=True):
    def work():
        core = at["core"] if own else 1 - at["core"]
        return by_core(core, [place_on(at, order[depth], step) for order in orders])

    return once(at, (orders, depth, step, own), work)


def along(at, orders, depth, step):
    def work():
        devices = [device_of(moved(at, order[depth], step)) for order in orders]
        return tuple(by_core(at["core"], pair) for pair in zip(*devices, strict=True))

    return once(at, (orders, depth, step, "device"), work)


def other_core(at):
    return once(at, "other", lambda: device_of(moved(at, "core", 1)))


def wait_bytes(ref, sem):
    pltpu.make_async_copy(ref, ref, sem).wait()


def dma(*shape):
    return pltpu.SemaphoreType.DMA(shape)


def gather_sems():
    return [dma(3), dma(3, 2), dma(3, 3), dma(3)]


def gather(at, pieces, full, sems):
    sent, recv, far_recv, core_recv = sems
    core = at["core"]
    sibling = other_core(at)

    def slab(i, step, first, count):
        size, orders = pieces[i]
        place = piece_place(at, orders, 0, step)
        start = core * (64 * size) + place * (16 * size) + first * (8 * size)
        return full[i].at[rows(start, count * (8 * size))]

    def give(i, here, sem, target):
        send(here, here, (sent.at[i], sem), target)

    for phase in range(2):
        for i in (1, 2, 0):
            size, orders = pieces[i]
            if phase:
                wait_bytes(full[i].at[0 : 3 * size], recv.at[i, 0])
            block = size * RING**phase
            index = piece_index(at, orders, 3 - phase)
            here = full[i].at[rows(core * (64 * size) + index * block, block)]
            for step in STEPS:
                give(i, here, recv.at[i, phase], along(at, orders, 2 - phase, step))
        yield
    for i in (1, 2, 0):
        size, orders = pieces[i]
        wait_bytes(full[i].at[0 : 12 * size], recv.at[i, 1])
        right, left = along(at, orders, 0, 1), along(at, orders, 0, 3)
        give(i, slab(i, 0, 0, 1), far_recv.at[i, 0], right)
        give(i, slab(i, 0, 1, 1), far_recv.at[i, 0], left)
        give(i, slab(i, 0, 1, 1), far_recv.at[i, 1], right)
        give(i, slab(i, 0, 0, 1), far_recv.at[i, 1], left)
    for i in range(3):
        give(i, slab(i, 0, 0, 2), core_recv.at[i], sibling)
    yield
    for i in (1, 2, 0):
        size, orders = pieces[i]
        wait_bytes(full[i].at[0 : 16 * size], far_recv.at[i, 0])
        give(i, slab(i, 3, 0, 1), far_recv.at[i, 2], along(at, orders, 0, 1))
        give(i, slab(i, 1, 1, 1), far_recv.at[i, 2], along(at, orders, 0, 3))
    yield
    for kind, steps in ((1, (1, 3)), (2, (2,))):
        for i in (1, 2, 0):
            size, _ = pieces[i]
            wait_bytes(full[i].at[0 : 16 * size], far_recv.at[i, kind])
            for step in steps:
                give(i, slab(i, step, 0, 2), core_recv.at[i], sibling)
    yield
    for i, (size, _) in enumerate(pieces):
        wait_bytes(full[i].at[0 : 64 * size], core_recv.at[i])


def wait_sent(pieces, buffers, sent):
    for i, (size, _) in enumerate(pieces):
        wait_bytes(buffers[i].at[0 : 127 * size], sent.at[i])


def scatter_scratch(pieces):
    scratch = [dma(3), dma(3, 4), dma(3, 4)]
    for size, _ in pieces:
        scratch += [
            pltpu.VMEM((64 * size, HALF), BF16),
            pltpu.VMEM((64 * size, HALF), BF16),
            pltpu.VMEM((2, 8 * size, HALF), BF16),
            pltpu.VMEM((2, 16 * size, HALF), BF16),
            pltpu.VMEM((16 * size, HALF), BF16),
            pltpu.VMEM((3, 4 * size, HALF), BF16),
            pltpu.VMEM((4 * size, HALF), BF16),
            pltpu.VMEM((3, size, HALF), BF16),
        ]
    return scratch


def reduce_scatter(at, pieces, parts, scale, out, scratch):
    sent, core_recv, recv = scratch[:3]
    bufs = [scratch[3 + 8 * i : 11 + 8 * i] for i in range(3)]
    core = at["core"]
    sibling = other_core(at)

    def slab(i, own, step):
        size, orders = pieces[i]
        return piece_place(at, orders, 0, step, own) * (16 * size)

    for s, step in enumerate((2, 1, 3, 0)):
        for i, (size, orders) in enumerate(pieces):
            start = slab(i, False, step)
            send(
                parts[i].at[rows((1 - core) * (64 * size) + start, 16 * size)],
                bufs[i][0].at[rows(start, 16 * size)],
                (sent.at[i], core_recv.at[i, s]),
                sibling,
            )
    yield

    def give(i, step, first, kind, dst, target):
        size, _ = pieces[i]
        here = rows(slab(i, True, step) + first * (8 * size), 8 * size)
        send(bufs[i][1].at[here], dst, (sent.at[i], recv.at[i, kind]), target)

    for s, step in enumerate((2, 1, 3, 0)):
        for i, (size, orders) in enumerate(pieces):
            sib, total, onward, landed = bufs[i][:4]
            right, left = along(at, orders, 0, 1), along(at, orders, 0, 3)
            start = slab(i, True, step)
            here = rows(start, 16 * size)
            wait_bytes(sib.at[here], core_recv.at[i, s])
            mine = parts[i][rows(core * (64 * size) + start, 16 * size), :]
            total[here, :] = mine + sib[here, :]
            if step == 2:
                give(i, 2, 0, 0, onward.at[0], right)
                give(i, 2, 1, 0, onward.at[1], left)
            elif step == 1:
                give(i, 1, 1, 1, landed.at[0, 8 * size : 16 * size], right)
            elif step == 3:
                give(i, 3, 0, 1, landed.at[1, 0 : 8 * size], left)
    yield
    for i in (1, 2, 0):
        size, orders = pieces[i]
        _, total, onward, landed = bufs[i][:4]
        wait_bytes(onward, recv.at[i, 0])
        for way, (step, first) in enumerate(((1, 0), (3, 1))):
            here = rows(slab(i, True, step) + first * (8 * size), 8 * size)
            total[here, :] = total[here, :] + onward[way]
            dst = landed.at[way, first * (8 * size) : (first + 1) * (8 * size)]
            give(i, step, first, 1, dst, along(at, orders, 0, step))
    yield
    for phase in range(3):
        for i in (1, 2, 0):
            size, orders = pieces[i]
            mine, landed = ((1, 3), (4, 5), (6, 7))[phase]
            mine, landed = bufs[i][mine], bufs[i][landed]
            block = size * RING ** (2 - phase)
            place = piece_place(at, orders, phase, 0)
            total = mine[rows(place * block, block), :].astype(F32)
            wait_bytes(landed, recv.at[i, phase + 1])
            for s in range(landed.shape[0]):
                total = total + landed[s].astype(F32)
            if phase == 2:
                first = sum(before for before, _ in pieces[:i])
                out[first : first + size, :] = total * scale
                continue
            after, there = bufs[i][4 + 2 * phase], bufs[i][5 + 2 * phase]
            after[...] = total.astype(BF16)
            small = block // RING
            for s, step in enumerate(STEPS):
                send(
                    after.at[rows(piece_place(at, orders, phase + 1, step) * small, small)],
                    there.at[s],
                    (sent.at[i], recv.at[i, phase + 2]),
                    along(at, orders, phase + 1, step),
                )
        if phase < 2:
            yield


def put_own(at, pieces, modes, full):
    first = 0
    for i, (size, orders) in enumerate(pieces):
        here = rows((at["core"] * 64 + piece_index(at, orders)) * size, size)
        full[i][here, :] = modes[first : first + size]
        first += size


def own_slots(at, kept):
    lat = lax.rem(at["z"], 2) * 2 + at["core"]
    value = jnp.concatenate([kept[...]] * 4, axis=1)
    slot = (value & 1) * KLAT + lat * KEEP + lax.shift_right_logical(value, 1)
    slot = jnp.broadcast_to(slot.astype(F32), (8, 128))
    lane = lax.broadcasted_iota(jnp.int32, (8, 128), 1)
    row = lax.broadcasted_iota(jnp.int32, (8, 128), 0)
    here = (lax.shift_right_logical(lane, 5) == lat) & (row == at["x"])
    return jnp.where(here, slot, 0.0)


def gather_slots(at, own, other, line, full, sems):
    sems, past = sems
    copy = send(own, other, (sems.at[0], sems.at[1]), other_core(at))
    for step in STEPS:
        pl.semaphore_signal(
            past, inc=1, device_id=device_of(moved(at, "y", step)), device_id_type=MESH
        )
    copy.wait_recv()
    mine = full.at[rows(index_of(at, "yz") * 8, 8)]
    both_cores = own[...] + other[...]
    line[3] = both_cores
    for s, step in enumerate(STEPS):
        send(line.at[3], line.at[s], (sems.at[2], sems.at[3]), device_of(moved(at, "x", step)))
    yield
    wait_bytes(line.at[0:3], sems.at[3])
    pl.semaphore_wait(past, len(STEPS))
    mine[...] = (line[0] + line[1]) + (line[2] + line[3])
    ways = [(dy, dz) for dy in STEPS for dz in STEPS]
    for step in STEPS:
        ways += [(step, 0), (0, step)]
    for dy, dz in ways:
        send(
            mine,
            mine,
            (sems.at[4], sems.at[5]),
            device_of(moved(moved(at, "y", dy), "z", dz)),
        )
    yield
    wait_bytes(full.at[0:120], sems.at[5])
    yield
    copy.wait_send()
    wait_bytes(line.at[0:3], sems.at[2])
    wait_bytes(full.at[0:120], sems.at[4])


def collect_slots(full, slots):
    for b in range(LON_BLOCKS):
        x, zhi, y = b // 8, b // 4 % 2, b % 4
        first = (y * 4 + zhi * 2) * 8 + x
        slots[b : b + 1, :] = full[first : first + 1, :] + full[first + 8 : first + 9, :]


def piece_start(b, lat, size, orders):
    order = orders[lat % 2]
    place = {"x": lax.div(b, 8), "z": lax.rem(lax.div(b, 4), 2) * 2 + lat // 2, "y": lax.rem(b, 4)}
    return rows((lat % 2 * 64 + index_of(place, order)) * size, size)


def group(i):
    return pl.ds(pl.multiple_of(i * STRIDE, 8), ROWS)


def one_hot(slots, b):
    ids = lax.broadcasted_iota(jnp.int32, (256, 128), 0).astype(F32)
    return jnp.where(ids == slots[pl.ds(b, 1), :], 1.0, 0.0).astype(BF16)


def one_hot_turned(slots, b):
    columns = jnp.transpose(jnp.broadcast_to(slots[pl.ds(b, 1), :], (128, 128)))
    ids = lax.broadcasted_iota(jnp.int32, (128, 128), 1).astype(F32)
    hot = [jnp.where(ids == columns - 128.0 * mode, 1.0, 0.0).astype(BF16) for mode in range(2)]
    return jnp.concatenate(hot, axis=1)


def both(halves, where):
    return jnp.concatenate([half[where, :] for half in halves], axis=1)


def fill_points(field, points):
    def one(j, carry):
        value = field[j].astype(F32)
        for h in range(2):
            points[h][group(j), :] = value[:, HALF * h : HALF * h + HALF]
        return carry

    lax.fori_loop(0, LONS, one, 0, unroll=U_FILL)
    for j in range(LONS, LONS_PAD):
        for h in range(2):
            points[h][group(j), :] = jnp.zeros((ROWS, HALF), F32)


def analyse_longitude(points, basis, rows_spec):
    def one(g, carry):
        value = both(points, pl.ds(g, LONS_PAD, stride=STRIDE)).astype(BF16)
        spec = matmul(basis[...], value)
        for h, half in enumerate(rows_spec):
            half[pl.ds(g, 2 * KM, stride=STRIDE), :] = spec[:, HALF * h : HALF * h + HALF]
        return carry

    lax.fori_loop(0, ROWS, one, 0, unroll=U_ROW if len(rows_spec) == 2 else U_HALF_ROW)


def synthesise_longitude(rows_spec, basis_back, points, scale):
    def one(g, carry):
        spec = rows_spec[pl.ds(g, 2 * KM, stride=STRIDE), :].astype(BF16)
        points[pl.ds(g, LONS_PAD, stride=STRIDE), :] = matmul(basis_back[...], spec) * scale
        return carry

    lax.fori_loop(0, ROWS, one, 0, unroll=U_HALF_ROW)


def spec_block(b, size=256):
    return pl.ds(pl.multiple_of(b * size, size), size)


def analyse_dense(rows_spec, table, dense):
    def one(b, carry):
        for mode in range(2):
            value = jnp.concatenate(
                [both(rows_spec, group(b * 4 + mode * 2 + part)) for part in range(2)], axis=0
            )
            full = matmul(table[mode], value.astype(BF16)).astype(BF16)
            for part in range(2):
                start = pl.multiple_of(b * 512 + part * 256 + mode * 128, 128)
                dense[pl.ds(start, 128), :] = full[128 * part : 128 * part + 128]
        return carry

    lax.fori_loop(0, LON_BLOCKS, one, 0, unroll=U_BLK)


def store_modes(b, part, modes, pieces, parts):
    for lat in range(4):
        tile = modes[32 * lat : 32 * lat + 32]
        starts = [piece_start(b, lat, *piece) for piece in pieces]
        if part == 0:
            parts[0][starts[0], :] = tile
        else:
            parts[1][starts[1], :] = tile[0:16]
            parts[2][starts[2], :] = tile[16:32]


def load_modes(b, pieces, full):
    tiles = [[], []]
    for lat in range(4):
        values = [full[i][piece_start(b, lat, *piece), :] for i, piece in enumerate(pieces)]
        tiles[0].append(values[0])
        tiles[1] += values[1:]
    return jnp.concatenate(tiles[0] + tiles[1], axis=0)


def select_modes(dense, slots, parts):
    def one(b, carry):
        hot = one_hot_turned(slots, b)
        for part in range(2):
            modes = matmul(hot, dense[spec_block(b * 2 + part), :]).astype(BF16)
            for h in range(2):
                here = modes[:, HALF * h : HALF * h + HALF]
                store_modes(b, part, here, HALVES[h], parts[h])
        return carry

    lax.fori_loop(0, LON_BLOCKS, one, 0, unroll=U_HALF_BLK)


def build_analysis(slots, table, out, low, high):
    def one(b, carry):
        hot = one_hot_turned(slots, b)
        for part in range(2):
            for mode in range(2):
                value = matmul(
                    hot[:, 128 * mode : 128 * mode + 128],
                    table[mode, 128 * part : 128 * part + 128, :],
                )
                start = pl.multiple_of(b * 256 + part * 128, 128)
                out[pl.ds(start, 128), 128 * mode : 128 * mode + 128] = value.astype(BF16)
        return carry

    lax.fori_loop(low, high, one, 0, unroll=U_BUILD)


def build_synthesis(slots, table, out, low, high):
    def one(b, carry):
        hot = one_hot(slots, b)
        for part in range(2):
            for mode in range(2):
                value = matmul(
                    table[mode, :, 128 * part : 128 * part + 128],
                    hot[128 * mode : 128 * mode + 128],
                )
                start = pl.multiple_of(b * 256 + mode * 128, 128)
                out[pl.ds(start, 128), 128 * part : 128 * part + 128] = value.astype(BF16)
        return carry

    lax.fori_loop(low, high, one, 0, unroll=U_BUILD)


def analyse_latitude(rows_spec, table, pieces, parts):
    def one(b, carry):
        value = jnp.concatenate([rows_spec[group(b * 4 + q), :] for q in range(4)], axis=0)
        modes = matmul(table[spec_block(b), :], value.astype(BF16)).astype(BF16)
        for part in range(2):
            store_modes(b, part, modes[128 * part : 128 * part + 128], pieces, parts)
        return carry

    lax.fori_loop(0, LON_BLOCKS, one, 0, unroll=U_HALF_BLK)


def synthesise_latitude(pieces, full, table, rows_spec):
    def one(b, carry):
        value = matmul(table[spec_block(b), :], load_modes(b, pieces, full))
        for q in range(4):
            rows_spec[group(b * 4 + q), :] = value[ROWS * q : ROWS * q + ROWS]
        return carry

    lax.fori_loop(0, LON_BLOCKS, one, 0, unroll=U_HALF_BLK)


def gelu_slope(x):
    c, a = math.sqrt(2.0 / math.pi), 0.044715
    cubic = (x * x) * jnp.asarray(c * a, x.dtype)
    linear = cubic + jnp.asarray(c, x.dtype)
    one = jnp.asarray(1.0, x.dtype)
    t = jnp.tanh(x * linear)
    return (one + t) * (one + (one - t) * (x * (linear + (cubic + cubic))))


def hidden_gradient(out_grad, w2, hidden, low, high):
    def one(i, carry):
        grad = out_grad[pl.ds(i * GROUP, GROUP)].reshape(GROUP * ROWS, CH)
        here = pl.ds(pl.multiple_of(i * (GROUP * ROWS), GROUP * ROWS), GROUP * ROWS)
        for k in range(HID // CHUNK):
            cols = slice(CHUNK * k, CHUNK * k + CHUNK)
            hidden[here, cols] = (0.5 * matmul(grad, w2[cols, :], (1, 1))).astype(BF16)
        return carry

    lax.fori_loop(low, high, one, 0)


def pointwise(points, hidden, w1, low, high):
    def one(i, carry):
        here = pl.ds(pl.multiple_of(i * (GROUP * ROWS), GROUP * ROWS), GROUP * ROWS)
        value = [both(points, group(i * GROUP + j)).astype(BF16) for j in range(GROUP)]
        value = jnp.concatenate(value, axis=0)
        total = None
        for k in range(HID // CHUNK):
            cols = slice(CHUNK * k, CHUNK * k + CHUNK)
            pre = matmul(value, w1[:, cols]).astype(BF16)
            pre_grad = gelu_slope(pre) * hidden[here, cols]
            term = matmul(pre_grad, w1[:, cols], (1, 1))
            total = term if total is None else total + term
        for j in range(GROUP):
            for h in range(2):
                points[h][group(i * GROUP + j), :] = total[
                    ROWS * j : ROWS * j + ROWS, HALF * h : HALF * h + HALF
                ]
        return carry

    lax.fori_loop(low, high, one, 0)


BETAS = HALF // BS
MIX = 16


def match_lanes(high, lane_first):
    shape = (CH, HALF) if lane_first else (HALF, CH)
    lane = lax.broadcasted_iota(jnp.int32, shape, 0 if lane_first else 1)
    channel = lax.broadcasted_iota(jnp.int32, shape, 1 if lane_first else 0) & (BS - 1)
    half = lax.shift_right_logical(lane, 4) if high else lane & (BS - 1)
    return jnp.where(channel == half, 1.0, 0.0).astype(BF16)


def block_mask():
    beta = lax.broadcasted_iota(jnp.int32, (BETAS, HALF), 0)
    channel = lax.broadcasted_iota(jnp.int32, (BETAS, HALF), 1)
    return jnp.where(beta == lax.shift_right_logical(channel, 4), 1.0, 0.0)[None]


def widen_weight(weight, wide):
    def one(e, carry):
        for part in range(2):
            value = weight[e, part].astype(F32)
            for h in range(2):
                start = pl.multiple_of((part * KEEP + e) * BETAS, BETAS)
                wide[h][pl.ds(start, BETAS), :] = value[BETAS * h : BETAS * h + BETAS]
        return carry

    lax.fori_loop(0, KEEP, one, 0, unroll=4)


def spread(modes, high, out):
    mask, match = block_mask(), match_lanes(high, False)
    for i in range(2 * KEEP // MIX):
        value = modes[MIX * i : MIX * i + MIX, :]
        wide = (value[:, None, :] * mask).reshape(MIX * BETAS, HALF)
        out[MIX * BETAS * i : MIX * BETAS * (i + 1), :] = matmul(wide.astype(BF16), match)


def mixing_rows(i):
    return [
        slice((part * KEEP + MIX * i) * BETAS, (part * KEEP + MIX * (i + 1)) * BETAS)
        for part in range(2)
    ]


def mix(wide, weight, backward):
    mask, sums = block_mask(), match_lanes(backward, True)
    out = [[], []]
    for i in range(KEEP // MIX):
        first, second = mixing_rows(i)
        re, im, wr, wi = wide[first, :], wide[second, :], weight[first, :], weight[second, :]
        if backward:
            terms = re * wr + im * wi, im * wr - re * wi
        else:
            terms = re * wr - im * wi, re * wi + im * wr
        for part, term in enumerate(terms):
            total = matmul(term.astype(BF16), sums).reshape(MIX, BETAS, HALF) * mask
            out[part].append(jnp.sum(total, axis=1))
    return jnp.concatenate(out[0] + out[1], axis=0).astype(BF16)


def weight_gradient(h, wide_in, wide_grad, out):
    for i in range(KEEP // MIX):
        first, second = mixing_rows(i)
        ar, ai, br, bi = wide_in[first, :], wide_in[second, :], wide_grad[first, :], wide_grad[second, :]
        here, betas = slice(MIX * i, MIX * i + MIX), slice(BETAS * h, BETAS * h + BETAS)
        out[here, 0, betas, :] = (ar * br + ai * bi).reshape(MIX, BETAS, CH)
        out[here, 1, betas, :] = (ar * bi - ai * br).reshape(MIX, BETAS, CH)


def kernel(fwd_scale, syn_scale, *refs):
    refs = list(refs)

    def take(n):
        taken = refs[:n]
        del refs[:n]
        return taken

    field_hbm, out_grad_hbm, weight_hbm, w1_hbm, w2_hbm, kept = take(6)
    basis_hbm, back_hbm, plain_hbm, doubled_hbm, plain_back_hbm, doubled_back_hbm = take(6)
    part_hbm, grad_hbm = take(2)
    field, out_grad, weight, w1, w2 = take(5)
    basis, basis_back, plain, doubled, plain_back, doubled_back = take(6)
    load_sems, store_sems = take(2)
    (spectral_grad,) = take(1)
    points, rows_spec = take(2), take(2)
    parts, full = [take(3), take(3)], [take(3), take(3)]
    tables, hidden, slots, own, other, slots_line, slots_full = take(7)
    modes, weights, wide_in, wide_grad = take(2), take(2), take(2), take(2)
    slot_sems = take(2)
    gather_sems = [take(4), take(4)]
    scatter = [take(27), take(27)]
    analysis, synthesis = tables.at[0:8192], tables.at[8192:16384]

    at = {**own_place(), "known": {}}
    lat, lon = lax.axis_index("lat"), lax.axis_index("lon")
    greeted = greet(at)
    loads = []
    for i, (src, dst) in enumerate(
        [
            (field_hbm, field),
            (basis_hbm.at[lon], basis),
            (doubled_hbm.at[lat], doubled),
            (plain_hbm.at[lat], plain),
            (plain_back_hbm.at[lat], plain_back),
            (weight_hbm, weight),
            (w2_hbm, w2),
            (out_grad_hbm, out_grad),
            (back_hbm.at[lon], basis_back),
            (w1_hbm, w1),
            (doubled_back_hbm.at[lat], doubled_back),
        ]
    ):
        copy = pltpu.make_async_copy(src, dst, load_sems.at[i])
        copy.start()
        loads.append(copy)
    own[...] = own_slots(at, kept)
    loads[0].wait()
    fill_points(field, points)
    pl.semaphore_wait(pltpu.get_barrier_semaphore(), greeted)

    collecting = gather_slots(at, own, other, slots_line, slots_full, slot_sems)
    next(collecting)
    loads[1].wait()
    analyse_longitude(points, basis, rows_spec)
    next(collecting)
    loads[2].wait()
    analyse_dense(rows_spec, doubled, tables)
    next(collecting)
    collect_slots(slots_full, slots)
    select_modes(tables, slots, parts)

    stores = []

    def store(src, dst):
        stores.append(pltpu.make_async_copy(src, dst, store_sems.at[len(stores)]))
        stores[-1].start()

    def finish(h):
        lanes = slice(HALF * h, HALF * h + HALF)

        def one(j, carry):
            field[j, :, lanes] = points[h][group(j), :].astype(BF16)
            return carry

        lax.fori_loop(0, LONS, one, 0, unroll=U_FILL)
        store(field.at[:, :, lanes], part_hbm.at[:, :, lanes])

    def exchange(h, scale, backward, synthesised):
        wide = (wide_grad if backward else wide_in)[h]
        yield from reduce_scatter(at, HALVES[h], parts[h], scale, modes[h], scatter[h])
        spread(modes[h], not backward, wide)
        put_own(at, HALVES[h], mix(wide, weights[h], backward), full[h])
        yield from gather(at, HALVES[h], full[h], gather_sems[h])
        wait_sent(HALVES[h], parts[h], scatter[h][0])
        synthesise_latitude(HALVES[h], full[h], synthesis, rows_spec[h])
        synthesise_longitude(rows_spec[h], basis_back, points[h], synthesised)
        wait_sent(HALVES[h], full[h], gather_sems[h][0])
        if backward:
            finish(h)

    def drive(first, second, work, before=lambda: None):
        next(first)
        before()
        next(second)
        for tasks in work:
            for task in tasks:
                task()
            next(first)
            next(second)
        next(first)
        next(first, None)
        next(second)
        next(second, None)

    quarter = LON_BLOCKS // 4
    tasks = []
    for low in range(0, LON_BLOCKS, quarter):
        span = (low, low + quarter)
        tasks += [
            functools.partial(build_analysis, slots, plain, analysis, *span),
            functools.partial(build_synthesis, slots, plain_back, synthesis, *span),
        ]
    for i in range(LONS // GROUP):
        tasks.append(functools.partial(hidden_gradient, out_grad, w2, hidden, i, i + 1))

    def prepare():
        next(collecting, None)
        for copy in loads[3:]:
            copy.wait()
        widen_weight(weight, weights)

    tasks.insert(0, prepare)
    work = [[]]
    for count in (3, 3, 2, 1, 2, 1, 2):
        work.append(tasks[:count])
        del tasks[:count]
    drive(*[exchange(h, fwd_scale, False, syn_scale) for h in range(2)], work)

    pointwise(points, hidden, w1, 0, LONS // GROUP)

    def analyse(h):
        analyse_longitude(points[h : h + 1], basis, rows_spec[h : h + 1])
        analyse_latitude(rows_spec[h], analysis, HALVES[h], parts[h])

    analyse(0)
    tables_back = [
        functools.partial(build_synthesis, slots, doubled_back, synthesis, low, low + quarter)
        for low in range(0, LON_BLOCKS, quarter)
    ]
    gradients = [
        functools.partial(weight_gradient, h, wide_in[h], wide_grad[h], spectral_grad)
        for h in range(2)
    ]
    work = [[], tables_back[:2], tables_back[2:], [], [], gradients[:1], gradients[1:]]
    work.append([lambda: store(spectral_grad, grad_hbm)])
    drive(
        *[exchange(h, syn_scale, True, fwd_scale) for h in range(2)],
        work,
        lambda: analyse(1),
    )

    for copy in stores:
        copy.wait()


def kernel_scratch():
    v = pltpu.VMEM
    pieces = [v((128 * size, HALF), BF16) for half in HALVES for size, _ in half]
    return [
        v((LONS, ROWS, CH), BF16),
        v((LONS, ROWS, CH), BF16),
        v((KEEP, 2, CH // BS, BS * BS), BF16),
        v((CH, HID), BF16),
        v((HID, CH), BF16),
        v((2 * KM, LONS_PAD), BF16),
        v((LONS_PAD, 2 * KM), BF16),
        v((2, 2 * KLAT, 2 * ROWS), BF16),
        v((2, 2 * KLAT, 2 * ROWS), BF16),
        v((2, 2 * ROWS, 2 * KLAT), BF16),
        v((2, 2 * ROWS, 2 * KLAT), BF16),
        dma(11),
        dma(3),
        v((KEEP, 2, CH // BS, BS * BS), F32),
        *[v((LONS_PAD * STRIDE, HALF), F32)] * 2,
        *[v((2 * KM * STRIDE, HALF), F32)] * 2,
        *pieces,
        *pieces,
        v((16384, CH), BF16),
        v((LONS * ROWS, HID), BF16),
        v((LON_BLOCKS, 128), F32),
        v((8, 128), F32),
        v((8, 128), F32),
        v((4, 8, 128), F32),
        v((128, 128), F32),
        *[v((2 * KEEP, HALF), F32)] * 2,
        *[v((2 * KEEP * BETAS, CH), F32)] * 6,
        dma(6),
        pltpu.SemaphoreType.REGULAR,
        *gather_sems(),
        *gather_sems(),
        *scatter_scratch(HALVES[0]),
        *scatter_scratch(HALVES[1]),
    ]


def result_kernel(out_grad, part, grad, out, grad_out):
    out[...] = (out_grad[...].astype(F32) + part[...].astype(F32)).astype(BF16)
    grad_out[...] = grad[...]


def result_call(out_grad, part, grad):
    blocks = 2
    point = pl.BlockSpec((LONS * ROWS // blocks, CH), lambda i: (i, 0))
    mode = pl.BlockSpec((2 * KEEP * CH // BS // blocks, BS * BS), lambda i: (i, 0))
    return pl.pallas_call(
        result_kernel,
        grid=(blocks,),
        out_shape=(
            jax.ShapeDtypeStruct(out_grad.shape, BF16),
            jax.ShapeDtypeStruct(grad.shape, F32),
        ),
        in_specs=[point, point, mode],
        out_specs=(point, mode),
        compiler_params=pltpu.CompilerParams(vmem_limit_bytes=LIMIT),
        name="results",
    )(out_grad, part, grad)


def longitude_tables(lon_total):
    j = np.arange(lon_total).reshape(-1, LONS)
    j = np.pad(j, ((0, 0), (0, LONS_PAD - LONS)))
    q = np.arange(2 * KM)
    angles = (j[:, None, :] * (q // 2)[None, :, None] % lon_total) * (2.0 * math.pi / lon_total)
    basis = np.where((q % 2)[None, :, None] == 0, np.cos(angles), -np.sin(angles))
    basis[:, :, LONS:] = 0.0
    basis = basis.astype(np.float32)
    return jnp.asarray(basis, BF16), jnp.asarray(np.swapaxes(basis, 1, 2), BF16)


def latitude_tables(lat_total):
    wave = np.arange(KLAT) - KLAT // 2

    def angles(ids):
        return (wave[None, :, None] * ids[:, None, :] % (2 * lat_total)) * (math.pi / lat_total)

    ids = np.arange(lat_total).reshape(-1, ROWS)
    upper, lower = angles(ids), angles(2 * lat_total - 1 - ids)
    cu, su, cl, sl = np.cos(upper), np.sin(upper), np.cos(lower), np.sin(lower)

    def table(c, s):
        top, bottom = np.concatenate([c, s], axis=2), np.concatenate([-s, c], axis=2)
        return np.concatenate([top, bottom], axis=1)

    plain = np.stack([table(cu, su)] * 2, axis=1)
    doubled = np.stack([table(cu + cl, su + sl), table(cu - cl, su - sl)], axis=1)
    tables = []
    for value in (plain, doubled, np.swapaxes(plain, 2, 3), np.swapaxes(doubled, 2, 3)):
        tables.append(jnp.asarray(value.astype(np.float32), BF16))
    return tables


def body(in_field, out_grad, spec_weight, inner_weight, output_projection_weight, kept_modes):
    lat_parts, lon_parts = lax.axis_size("lat"), lax.axis_size("lon")
    lat_total, lon_total = ROWS * lat_parts, LONS * lon_parts
    fwd_scale = 1.0 / math.sqrt(2 * lat_total * lon_total)
    syn_scale = 1.0 / math.sqrt(KEEP * lat_parts * lon_parts)
    hbm = pl.BlockSpec(memory_space=pl.ANY)
    spectral_part, spectral_grad = pl.pallas_call(
        functools.partial(kernel, fwd_scale, syn_scale),
        out_shape=(
            jax.ShapeDtypeStruct((LONS, ROWS, CH), BF16),
            jax.ShapeDtypeStruct((KEEP, 2, CH // BS, BS * BS), F32),
        ),
        in_specs=[hbm] * 5 + [VMEM] + [hbm] * 6,
        out_specs=(hbm, hbm),
        scratch_shapes=kernel_scratch(),
        compiler_params=pltpu.CompilerParams(
            collective_id=0, has_side_effects=True, vmem_limit_bytes=LIMIT
        ),
        name="layer_gradients",
    )(
        jnp.swapaxes(in_field, 0, 1),
        jnp.swapaxes(out_grad, 0, 1),
        spec_weight,
        inner_weight,
        output_projection_weight,
        kept_modes.reshape(1, KEEP),
        *longitude_tables(lon_total),
        *latitude_tables(lat_total),
    )
    input_grad, spectral_grad = result_call(
        jnp.swapaxes(out_grad, 0, 1).reshape(LONS * ROWS, CH),
        spectral_part.reshape(LONS * ROWS, CH),
        spectral_grad.reshape(2 * KEEP * CH // BS, BS * BS),
    )
    return (
        jnp.swapaxes(input_grad.reshape(LONS, ROWS, CH), 0, 1),
        spectral_grad.reshape(KEEP, 2, CH // BS, BS * BS),
    )


def solution(mesh):
    return jax.shard_map(
        body,
        mesh=mesh,
        in_specs=(
            P("lat", "lon", None),
            P("lat", "lon", None),
            P(("lat", "lon"), None, None, None),
            P(),
            P(),
            P(("lat", "lon")),
        ),
        out_specs=(P("lat", "lon", None), P(("lat", "lon"), None, None, None)),
        check_vma=False,
    )
```

```python
import functools
import math

import jax
import jax.numpy as jnp
import numpy as np
from jax import lax
from jax.experimental import pallas as pl
from jax.experimental.pallas import tpu as pltpu
from jax.sharding import PartitionSpec as P

BS = 16
KM = 64
KLAT = 128
RING = 4
STEPS = (2, 1, 3)
ROWS, LONS, CH, HID = 64, 45, 256, 1024
LONS_PAD = 48
LON_BLOCKS = 32
KEEP = 32
ORDERS = (("xyz", "yzx"), ("yzx", "zxy"), ("zxy", "xyz"))
HALVES = (
    ((32, ORDERS[0]), (16, ORDERS[1]), (16, ORDERS[2])),
    ((32, ORDERS[1]), (16, ORDERS[2]), (16, ORDERS[0])),
)
HALF = 128
STRIDE = 72
MESH = pl.DeviceIdType.MESH
F32, BF16 = jnp.float32, jnp.bfloat16
VMEM = pl.BlockSpec(memory_space=pltpu.VMEM)
LIMIT = 60 << 20
U_FILL, U_ROW, U_BLK, U_BUILD, GROUP, CHUNK = 15, 16, 8, 8, 9, 256
U_HALF_ROW, U_HALF_BLK = 64, 32


def matmul(a, b, contract=(1, 0)):
    dims = (((contract[0],), (contract[1],)), ((), ()))
    return lax.dot_general(a, b, dims, preferred_element_type=F32)


def own_place():
    lat, lon = lax.axis_index("lat"), lax.axis_index("lon")
    return {
        "x": lax.div(lon, 8),
        "y": lax.rem(lon, 4),
        "z": lax.rem(lax.div(lon, 4), 2) * 2 + lax.div(lat, 2),
        "core": lax.rem(lat, 2),
    }


def moved(at, axis, step):
    return {**at, axis: lax.rem(at[axis] + step, 2 if axis == "core" else RING)}


def device_of(at):
    return (lax.rem(at["z"], 2) * 2 + at["core"], at["x"] * 8 + lax.div(at["z"], 2) * 4 + at["y"])


def greet(at):
    partners = [moved(at, axis, step) for axis in "xyz" for step in STEPS] + [moved(at, "core", 1)]
    for partner in partners:
        pl.semaphore_signal(
            pltpu.get_barrier_semaphore(),
            inc=1,
            device_id=device_of(partner),
            device_id_type=MESH,
        )
    return len(partners)


def send(src, dst, sems, target):
    copy = pltpu.make_async_remote_copy(
        src_ref=src,
        dst_ref=dst,
        send_sem=sems[0],
        recv_sem=sems[1],
        device_id=target,
        device_id_type=MESH,
    )
    copy.start()
    return copy


def rows(start, size):
    return pl.ds(pl.multiple_of(start, math.gcd(size, 16)), size)


def index_of(at, order):
    index = 0
    for name in order:
        index = index * RING + at[name]
    return index


def by_core(core, values):
    return values[0] + (values[1] - values[0]) * core


def once(at, key, work):
    if key not in at["known"]:
        at["known"][key] = work()
    return at["known"][key]


def place_on(at, axis, step):
    return once(at, (axis, step), lambda: lax.rem(at[axis] + step, RING))


def piece_index(at, orders, depth=3, own=True):
    def work():
        core = at["core"] if own else 1 - at["core"]
        return by_core(core, [index_of(at, order[:depth]) for order in orders])

    return once(at, (orders, depth, own), work)


def piece_place(at, orders, depth, step, own=True):
    def work():
        core = at["core"] if own else 1 - at["core"]
        return by_core(core, [place_on(at, order[depth], step) for order in orders])

    return once(at, (orders, depth, step, own), work)


def along(at, orders, depth, step):
    def work():
        devices = [device_of(moved(at, order[depth], step)) for order in orders]
        return tuple(by_core(at["core"], pair) for pair in zip(*devices, strict=True))

    return once(at, (orders, depth, step, "device"), work)


def other_core(at):
    return once(at, "other", lambda: device_of(moved(at, "core", 1)))


def wait_bytes(ref, sem):
    pltpu.make_async_copy(ref, ref, sem).wait()


def dma(*shape):
    return pltpu.SemaphoreType.DMA(shape)


def gather_sems():
    return [dma(3), dma(3, 2), dma(3, 3), dma(3)]


def gather(at, pieces, full, sems):
    sent, recv, far_recv, core_recv = sems
    core = at["core"]
    sibling = other_core(at)

    def slab(i, step, first, count):
        size, orders = pieces[i]
        place = piece_place(at, orders, 0, step)
        start = core * (64 * size) + place * (16 * size) + first * (8 * size)
        return full[i].at[rows(start, count * (8 * size))]

    def give(i, here, sem, target):
        send(here, here, (sent.at[i], sem), target)

    for phase in range(2):
        for i in (1, 2, 0):
            size, orders = pieces[i]
            if phase:
                wait_bytes(full[i].at[0 : 3 * size], recv.at[i, 0])
            block = size * RING**phase
            index = piece_index(at, orders, 3 - phase)
            here = full[i].at[rows(core * (64 * size) + index * block, block)]
            for step in STEPS:
                give(i, here, recv.at[i, phase], along(at, orders, 2 - phase, step))
        yield
    for i in (1, 2, 0):
        size, orders = pieces[i]
        wait_bytes(full[i].at[0 : 12 * size], recv.at[i, 1])
        right, left = along(at, orders, 0, 1), along(at, orders, 0, 3)
        give(i, slab(i, 0, 0, 1), far_recv.at[i, 0], right)
        give(i, slab(i, 0, 1, 1), far_recv.at[i, 0], left)
        give(i, slab(i, 0, 1, 1), far_recv.at[i, 1], right)
        give(i, slab(i, 0, 0, 1), far_recv.at[i, 1], left)
    for i in range(3):
        give(i, slab(i, 0, 0, 2), core_recv.at[i], sibling)
    yield
    for i in (1, 2, 0):
        size, orders = pieces[i]
        wait_bytes(full[i].at[0 : 16 * size], far_recv.at[i, 0])
        give(i, slab(i, 3, 0, 1), far_recv.at[i, 2], along(at, orders, 0, 1))
        give(i, slab(i, 1, 1, 1), far_recv.at[i, 2], along(at, orders, 0, 3))
    yield
    for kind, steps in ((1, (1, 3)), (2, (2,))):
        for i in (1, 2, 0):
            size, _ = pieces[i]
            wait_bytes(full[i].at[0 : 16 * size], far_recv.at[i, kind])
            for step in steps:
                give(i, slab(i, step, 0, 2), core_recv.at[i], sibling)
    yield
    for i, (size, _) in enumerate(pieces):
        wait_bytes(full[i].at[0 : 64 * size], core_recv.at[i])


def wait_sent(pieces, buffers, sent):
    for i, (size, _) in enumerate(pieces):
        wait_bytes(buffers[i].at[0 : 127 * size], sent.at[i])


def scatter_scratch(pieces):
    scratch = [dma(3), dma(3, 4), dma(3, 4)]
    for size, _ in pieces:
        scratch += [
            pltpu.VMEM((64 * size, HALF), BF16),
            pltpu.VMEM((64 * size, HALF), BF16),
            pltpu.VMEM((2, 8 * size, HALF), BF16),
            pltpu.VMEM((2, 16 * size, HALF), BF16),
            pltpu.VMEM((16 * size, HALF), BF16),
            pltpu.VMEM((3, 4 * size, HALF), BF16),
            pltpu.VMEM((4 * size, HALF), BF16),
            pltpu.VMEM((3, size, HALF), BF16),
        ]
    return scratch


def reduce_scatter(at, pieces, parts, scale, out, scratch):
    sent, core_recv, recv = scratch[:3]
    bufs = [scratch[3 + 8 * i : 11 + 8 * i] for i in range(3)]
    core = at["core"]
    sibling = other_core(at)

    def slab(i, own, step):
        size, orders = pieces[i]
        return piece_place(at, orders, 0, step, own) * (16 * size)

    for s, step in enumerate((2, 1, 3, 0)):
        for i, (size, orders) in enumerate(pieces):
            start = slab(i, False, step)
            send(
                parts[i].at[rows((1 - core) * (64 * size) + start, 16 * size)],
                bufs[i][0].at[rows(start, 16 * size)],
                (sent.at[i], core_recv.at[i, s]),
                sibling,
            )
    yield

    def give(i, step, first, kind, dst, target):
        size, _ = pieces[i]
        here = rows(slab(i, True, step) + first * (8 * size), 8 * size)
        send(bufs[i][1].at[here], dst, (sent.at[i], recv.at[i, kind]), target)

    for s, step in enumerate((2, 1, 3, 0)):
        for i, (size, orders) in enumerate(pieces):
            sib, total, onward, landed = bufs[i][:4]
            right, left = along(at, orders, 0, 1), along(at, orders, 0, 3)
            start = slab(i, True, step)
            here = rows(start, 16 * size)
            wait_bytes(sib.at[here], core_recv.at[i, s])
            mine = parts[i][rows(core * (64 * size) + start, 16 * size), :]
            total[here, :] = mine + sib[here, :]
            if step == 2:
                give(i, 2, 0, 0, onward.at[0], right)
                give(i, 2, 1, 0, onward.at[1], left)
            elif step == 1:
                give(i, 1, 1, 1, landed.at[0, 8 * size : 16 * size], right)
            elif step == 3:
                give(i, 3, 0, 1, landed.at[1, 0 : 8 * size], left)
    yield
    for i in (1, 2, 0):
        size, orders = pieces[i]
        _, total, onward, landed = bufs[i][:4]
        wait_bytes(onward, recv.at[i, 0])
        for way, (step, first) in enumerate(((1, 0), (3, 1))):
            here = rows(slab(i, True, step) + first * (8 * size), 8 * size)
            total[here, :] = total[here, :] + onward[way]
            dst = landed.at[way, first * (8 * size) : (first + 1) * (8 * size)]
            give(i, step, first, 1, dst, along(at, orders, 0, step))
    yield
    for phase in range(3):
        for i in (1, 2, 0):
            size, orders = pieces[i]
            mine, landed = ((1, 3), (4, 5), (6, 7))[phase]
            mine, landed = bufs[i][mine], bufs[i][landed]
            block = size * RING ** (2 - phase)
            place = piece_place(at, orders, phase, 0)
            total = mine[rows(place * block, block), :].astype(F32)
            wait_bytes(landed, recv.at[i, phase + 1])
            for s in range(landed.shape[0]):
                total = total + landed[s].astype(F32)
            if phase == 2:
                first = sum(before for before, _ in pieces[:i])
                out[first : first + size, :] = total * scale
                continue
            after, there = bufs[i][4 + 2 * phase], bufs[i][5 + 2 * phase]
            after[...] = total.astype(BF16)
            small = block // RING
            for s, step in enumerate(STEPS):
                send(
                    after.at[rows(piece_place(at, orders, phase + 1, step) * small, small)],
                    there.at[s],
                    (sent.at[i], recv.at[i, phase + 2]),
                    along(at, orders, phase + 1, step),
                )
        if phase < 2:
            yield


def put_own(at, pieces, modes, full):
    first = 0
    for i, (size, orders) in enumerate(pieces):
        here = rows((at["core"] * 64 + piece_index(at, orders)) * size, size)
        full[i][here, :] = modes[first : first + size]
        first += size


def own_slots(at, kept):
    lat = lax.rem(at["z"], 2) * 2 + at["core"]
    value = jnp.concatenate([kept[...]] * 4, axis=1)
    slot = (value & 1) * KLAT + lat * KEEP + lax.shift_right_logical(value, 1)
    slot = jnp.broadcast_to(slot.astype(F32), (8, 128))
    lane = lax.broadcasted_iota(jnp.int32, (8, 128), 1)
    row = lax.broadcasted_iota(jnp.int32, (8, 128), 0)
    here = (lax.shift_right_logical(lane, 5) == lat) & (row == at["x"])
    return jnp.where(here, slot, 0.0)


def gather_slots(at, own, other, line, full, sems):
    sems, past = sems
    copy = send(own, other, (sems.at[0], sems.at[1]), other_core(at))
    for step in STEPS:
        pl.semaphore_signal(
            past, inc=1, device_id=device_of(moved(at, "y", step)), device_id_type=MESH
        )
    copy.wait_recv()
    mine = full.at[rows(index_of(at, "yz") * 8, 8)]
    both_cores = own[...] + other[...]
    line[3] = both_cores
    for s, step in enumerate(STEPS):
        send(line.at[3], line.at[s], (sems.at[2], sems.at[3]), device_of(moved(at, "x", step)))
    yield
    wait_bytes(line.at[0:3], sems.at[3])
    pl.semaphore_wait(past, len(STEPS))
    mine[...] = (line[0] + line[1]) + (line[2] + line[3])
    ways = [(dy, dz) for dy in STEPS for dz in STEPS]
    for step in STEPS:
        ways += [(step, 0), (0, step)]
    for dy, dz in ways:
        send(
            mine,
            mine,
            (sems.at[4], sems.at[5]),
            device_of(moved(moved(at, "y", dy), "z", dz)),
        )
    yield
    wait_bytes(full.at[0:120], sems.at[5])
    yield
    copy.wait_send()
    wait_bytes(line.at[0:3], sems.at[2])
    wait_bytes(full.at[0:120], sems.at[4])


def collect_slots(full, slots):
    for b in range(LON_BLOCKS):
        x, zhi, y = b // 8, b // 4 % 2, b % 4
        first = (y * 4 + zhi * 2) * 8 + x
        slots[b : b + 1, :] = full[first : first + 1, :] + full[first + 8 : first + 9, :]


def piece_start(b, lat, size, orders):
    order = orders[lat % 2]
    place = {"x": lax.div(b, 8), "z": lax.rem(lax.div(b, 4), 2) * 2 + lat // 2, "y": lax.rem(b, 4)}
    return rows((lat % 2 * 64 + index_of(place, order)) * size, size)


def group(i):
    return pl.ds(pl.multiple_of(i * STRIDE, 8), ROWS)


def one_hot(slots, b):
    ids = lax.broadcasted_iota(jnp.int32, (256, 128), 0).astype(F32)
    return jnp.where(ids == slots[pl.ds(b, 1), :], 1.0, 0.0).astype(BF16)


def one_hot_turned(slots, b):
    columns = jnp.transpose(jnp.broadcast_to(slots[pl.ds(b, 1), :], (128, 128)))
    ids = lax.broadcasted_iota(jnp.int32, (128, 128), 1).astype(F32)
    hot = [jnp.where(ids == columns - 128.0 * mode, 1.0, 0.0).astype(BF16) for mode in range(2)]
    return jnp.concatenate(hot, axis=1)


def both(halves, where):
    return jnp.concatenate([half[where, :] for half in halves], axis=1)


def fill_points(field, points):
    def one(j, carry):
        value = field[j].astype(F32)
        for h in range(2):
            points[h][group(j), :] = value[:, HALF * h : HALF * h + HALF]
        return carry

    lax.fori_loop(0, LONS, one, 0, unroll=U_FILL)
    for j in range(LONS, LONS_PAD):
        for h in range(2):
            points[h][group(j), :] = jnp.zeros((ROWS, HALF), F32)


def analyse_longitude(points, basis, rows_spec):
    def one(g, carry):
        value = both(points, pl.ds(g, LONS_PAD, stride=STRIDE)).astype(BF16)
        spec = matmul(basis[...], value)
        for h, half in enumerate(rows_spec):
            half[pl.ds(g, 2 * KM, stride=STRIDE), :] = spec[:, HALF * h : HALF * h + HALF]
        return carry

    lax.fori_loop(0, ROWS, one, 0, unroll=U_ROW if len(rows_spec) == 2 else U_HALF_ROW)


def synthesise_longitude(rows_spec, basis_back, points, scale):
    def one(g, carry):
        spec = rows_spec[pl.ds(g, 2 * KM, stride=STRIDE), :].astype(BF16)
        points[pl.ds(g, LONS_PAD, stride=STRIDE), :] = matmul(basis_back[...], spec) * scale
        return carry

    lax.fori_loop(0, ROWS, one, 0, unroll=U_HALF_ROW)


def spec_block(b, size=256):
    return pl.ds(pl.multiple_of(b * size, size), size)


def analyse_dense(rows_spec, table, dense):
    def one(b, carry):
        for mode in range(2):
            value = jnp.concatenate(
                [both(rows_spec, group(b * 4 + mode * 2 + part)) for part in range(2)], axis=0
            )
            full = matmul(table[mode], value.astype(BF16)).astype(BF16)
            for part in range(2):
                start = pl.multiple_of(b * 512 + part * 256 + mode * 128, 128)
                dense[pl.ds(start, 128), :] = full[128 * part : 128 * part + 128]
        return carry

    lax.fori_loop(0, LON_BLOCKS, one, 0, unroll=U_BLK)


def store_modes(b, part, modes, pieces, parts):
    for lat in range(4):
        tile = modes[32 * lat : 32 * lat + 32]
        starts = [piece_start(b, lat, *piece) for piece in pieces]
        if part == 0:
            parts[0][starts[0], :] = tile
        else:
            parts[1][starts[1], :] = tile[0:16]
            parts[2][starts[2], :] = tile[16:32]


def load_modes(b, pieces, full):
    tiles = [[], []]
    for lat in range(4):
        values = [full[i][piece_start(b, lat, *piece), :] for i, piece in enumerate(pieces)]
        tiles[0].append(values[0])
        tiles[1] += values[1:]
    return jnp.concatenate(tiles[0] + tiles[1], axis=0)


def select_modes(dense, slots, parts):
    def one(b, carry):
        hot = one_hot_turned(slots, b)
        for part in range(2):
            modes = matmul(hot, dense[spec_block(b * 2 + part), :]).astype(BF16)
            for h in range(2):
                here = modes[:, HALF * h : HALF * h + HALF]
                store_modes(b, part, here, HALVES[h], parts[h])
        return carry

    lax.fori_loop(0, LON_BLOCKS, one, 0, unroll=U_HALF_BLK)


def build_analysis(slots, table, out, low, high):
    def one(b, carry):
        hot = one_hot_turned(slots, b)
        for part in range(2):
            for mode in range(2):
                value = matmul(
                    hot[:, 128 * mode : 128 * mode + 128],
                    table[mode, 128 * part : 128 * part + 128, :],
                )
                start = pl.multiple_of(b * 256 + part * 128, 128)
                out[pl.ds(start, 128), 128 * mode : 128 * mode + 128] = value.astype(BF16)
        return carry

    lax.fori_loop(low, high, one, 0, unroll=U_BUILD)


def build_synthesis(slots, table, out, low, high):
    def one(b, carry):
        hot = one_hot(slots, b)
        for part in range(2):
            for mode in range(2):
                value = matmul(
                    table[mode, :, 128 * part : 128 * part + 128],
                    hot[128 * mode : 128 * mode + 128],
                )
                start = pl.multiple_of(b * 256 + mode * 128, 128)
                out[pl.ds(start, 128), 128 * part : 128 * part + 128] = value.astype(BF16)
        return carry

    lax.fori_loop(low, high, one, 0, unroll=U_BUILD)


def analyse_latitude(rows_spec, table, pieces, parts):
    def one(b, carry):
        value = jnp.concatenate([rows_spec[group(b * 4 + q), :] for q in range(4)], axis=0)
        modes = matmul(table[spec_block(b), :], value.astype(BF16)).astype(BF16)
        for part in range(2):
            store_modes(b, part, modes[128 * part : 128 * part + 128], pieces, parts)
        return carry

    lax.fori_loop(0, LON_BLOCKS, one, 0, unroll=U_HALF_BLK)


def synthesise_latitude(pieces, full, table, rows_spec):
    def one(b, carry):
        value = matmul(table[spec_block(b), :], load_modes(b, pieces, full))
        for q in range(4):
            rows_spec[group(b * 4 + q), :] = value[ROWS * q : ROWS * q + ROWS]
        return carry

    lax.fori_loop(0, LON_BLOCKS, one, 0, unroll=U_HALF_BLK)


def gelu_slope(x):
    c, a = math.sqrt(2.0 / math.pi), 0.044715
    cubic = (x * x) * jnp.asarray(c * a, x.dtype)
    linear = cubic + jnp.asarray(c, x.dtype)
    one = jnp.asarray(1.0, x.dtype)
    t = jnp.tanh(x * linear)
    return (one + t) * (one + (one - t) * (x * (linear + (cubic + cubic))))


def hidden_gradient(out_grad, w2, hidden, low, high):
    def one(i, carry):
        grad = out_grad[pl.ds(i * GROUP, GROUP)].reshape(GROUP * ROWS, CH)
        here = pl.ds(pl.multiple_of(i * (GROUP * ROWS), GROUP * ROWS), GROUP * ROWS)
        for k in range(HID // CHUNK):
            cols = slice(CHUNK * k, CHUNK * k + CHUNK)
            hidden[here, cols] = (0.5 * matmul(grad, w2[cols, :], (1, 1))).astype(BF16)
        return carry

    lax.fori_loop(low, high, one, 0)


def pointwise(points, hidden, w1, low, high):
    def one(i, carry):
        here = pl.ds(pl.multiple_of(i * (GROUP * ROWS), GROUP * ROWS), GROUP * ROWS)
        value = [both(points, group(i * GROUP + j)).astype(BF16) for j in range(GROUP)]
        value = jnp.concatenate(value, axis=0)
        total = None
        for k in range(HID // CHUNK):
            cols = slice(CHUNK * k, CHUNK * k + CHUNK)
            pre = matmul(value, w1[:, cols]).astype(BF16)
            pre_grad = gelu_slope(pre) * hidden[here, cols]
            term = matmul(pre_grad, w1[:, cols], (1, 1))
            total = term if total is None else total + term
        for j in range(GROUP):
            for h in range(2):
                points[h][group(i * GROUP + j), :] = total[
                    ROWS * j : ROWS * j + ROWS, HALF * h : HALF * h + HALF
                ]
        return carry

    lax.fori_loop(low, high, one, 0, unroll=high - low)


BETAS = HALF // BS
MIX = 16


def match_lanes(high, lane_first):
    shape = (CH, HALF) if lane_first else (HALF, CH)
    lane = lax.broadcasted_iota(jnp.int32, shape, 0 if lane_first else 1)
    channel = lax.broadcasted_iota(jnp.int32, shape, 1 if lane_first else 0) & (BS - 1)
    half = lax.shift_right_logical(lane, 4) if high else lane & (BS - 1)
    return jnp.where(channel == half, 1.0, 0.0).astype(BF16)


def block_mask():
    beta = lax.broadcasted_iota(jnp.int32, (BETAS, HALF), 0)
    channel = lax.broadcasted_iota(jnp.int32, (BETAS, HALF), 1)
    return jnp.where(beta == lax.shift_right_logical(channel, 4), 1.0, 0.0)[None]


def widen_weight(weight, wide):
    def one(e, carry):
        for part in range(2):
            value = weight[e, part].astype(F32)
            for h in range(2):
                start = pl.multiple_of((part * KEEP + e) * BETAS, BETAS)
                wide[h][pl.ds(start, BETAS), :] = value[BETAS * h : BETAS * h + BETAS]
        return carry

    lax.fori_loop(0, KEEP, one, 0, unroll=4)


def spread(modes, high, out):
    mask, match = block_mask(), match_lanes(high, False)
    for i in range(2 * KEEP // MIX):
        value = modes[MIX * i : MIX * i + MIX, :]
        wide = (value[:, None, :] * mask).reshape(MIX * BETAS, HALF)
        out[MIX * BETAS * i : MIX * BETAS * (i + 1), :] = matmul(wide.astype(BF16), match)


def mixing_rows(i):
    return [
        slice((part * KEEP + MIX * i) * BETAS, (part * KEEP + MIX * (i + 1)) * BETAS)
        for part in range(2)
    ]


def mix(wide, weight, backward):
    mask, sums = block_mask(), match_lanes(backward, True)
    out = [[], []]
    for i in range(KEEP // MIX):
        first, second = mixing_rows(i)
        re, im, wr, wi = wide[first, :], wide[second, :], weight[first, :], weight[second, :]
        if backward:
            terms = re * wr + im * wi, im * wr - re * wi
        else:
            terms = re * wr - im * wi, re * wi + im * wr
        for part, term in enumerate(terms):
            total = matmul(term.astype(BF16), sums).reshape(MIX, BETAS, HALF) * mask
            out[part].append(jnp.sum(total, axis=1))
    return jnp.concatenate(out[0] + out[1], axis=0).astype(BF16)


def weight_gradient(h, wide_in, wide_grad, out):
    for i in range(KEEP // MIX):
        first, second = mixing_rows(i)
        ar, ai, br, bi = wide_in[first, :], wide_in[second, :], wide_grad[first, :], wide_grad[second, :]
        here, betas = slice(MIX * i, MIX * i + MIX), slice(BETAS * h, BETAS * h + BETAS)
        out[here, 0, betas, :] = (ar * br + ai * bi).reshape(MIX, BETAS, CH)
        out[here, 1, betas, :] = (ar * bi - ai * br).reshape(MIX, BETAS, CH)


def kernel(fwd_scale, syn_scale, *refs):
    refs = list(refs)

    def take(n):
        taken = refs[:n]
        del refs[:n]
        return taken

    field_hbm, out_grad_hbm, weight_hbm, w1_hbm, w2_hbm, kept = take(6)
    basis_hbm, back_hbm, plain_hbm, doubled_hbm, plain_back_hbm, doubled_back_hbm = take(6)
    part_hbm, grad_hbm = take(2)
    field, out_grad, weight, w1, w2 = take(5)
    basis, basis_back, plain, doubled, plain_back, doubled_back = take(6)
    load_sems, store_sems = take(2)
    (spectral_grad,) = take(1)
    points, rows_spec = take(2), take(2)
    parts, full = [take(3), take(3)], [take(3), take(3)]
    tables, hidden, slots, own, other, slots_line, slots_full = take(7)
    modes, weights, wide_in, wide_grad = take(2), take(2), take(2), take(2)
    slot_sems = take(2)
    gather_sems = [take(4), take(4)]
    scatter = [take(27), take(27)]
    analysis, synthesis = tables.at[0:8192], tables.at[8192:16384]

    at = {**own_place(), "known": {}}
    lat, lon = lax.axis_index("lat"), lax.axis_index("lon")
    greeted = greet(at)
    loads = []
    for i, (src, dst) in enumerate(
        [
            (field_hbm, field),
            (basis_hbm.at[lon], basis),
            (doubled_hbm.at[lat], doubled),
            (plain_hbm.at[lat], plain),
            (plain_back_hbm.at[lat], plain_back),
            (weight_hbm, weight),
            (w2_hbm, w2),
            (out_grad_hbm, out_grad),
            (back_hbm.at[lon], basis_back),
            (w1_hbm, w1),
            (doubled_back_hbm.at[lat], doubled_back),
        ]
    ):
        copy = pltpu.make_async_copy(src, dst, load_sems.at[i])
        copy.start()
        loads.append(copy)
    own[...] = own_slots(at, kept)
    loads[0].wait()
    fill_points(field, points)
    pl.semaphore_wait(pltpu.get_barrier_semaphore(), greeted)

    collecting = gather_slots(at, own, other, slots_line, slots_full, slot_sems)
    next(collecting)
    loads[1].wait()
    analyse_longitude(points, basis, rows_spec)
    next(collecting)
    loads[2].wait()
    analyse_dense(rows_spec, doubled, tables)
    next(collecting)
    collect_slots(slots_full, slots)
    select_modes(tables, slots, parts)

    stores = []

    def store(src, dst):
        stores.append(pltpu.make_async_copy(src, dst, store_sems.at[len(stores)]))
        stores[-1].start()

    def finish(h):
        lanes = slice(HALF * h, HALF * h + HALF)

        def one(j, carry):
            field[j, :, lanes] = points[h][group(j), :].astype(BF16)
            return carry

        lax.fori_loop(0, LONS, one, 0, unroll=U_FILL)
        store(field.at[:, :, lanes], part_hbm.at[:, :, lanes])

    def exchange(h, scale, backward, synthesised):
        wide = (wide_grad if backward else wide_in)[h]
        yield from reduce_scatter(at, HALVES[h], parts[h], scale, modes[h], scatter[h])
        spread(modes[h], not backward, wide)
        put_own(at, HALVES[h], mix(wide, weights[h], backward), full[h])
        yield from gather(at, HALVES[h], full[h], gather_sems[h])
        wait_sent(HALVES[h], parts[h], scatter[h][0])
        synthesise_latitude(HALVES[h], full[h], synthesis, rows_spec[h])
        synthesise_longitude(rows_spec[h], basis_back, points[h], synthesised)
        wait_sent(HALVES[h], full[h], gather_sems[h][0])
        if backward:
            finish(h)

    def drive(first, second, work, before=lambda: None):
        next(first)
        before()
        next(second)
        for tasks in work:
            for task in tasks:
                task()
            next(first)
            next(second)
        next(first)
        next(first, None)
        next(second)
        next(second, None)

    quarter = LON_BLOCKS // 4
    tasks = []
    for low in range(0, LON_BLOCKS, quarter):
        span = (low, low + quarter)
        tasks += [
            functools.partial(build_analysis, slots, plain, analysis, *span),
            functools.partial(build_synthesis, slots, plain_back, synthesis, *span),
        ]
    for i in range(LONS // GROUP):
        tasks.append(functools.partial(hidden_gradient, out_grad, w2, hidden, i, i + 1))

    def prepare():
        next(collecting, None)
        for copy in loads[3:]:
            copy.wait()
        widen_weight(weight, weights)

    tasks.insert(0, prepare)
    work = [[]]
    for count in (3, 3, 2, 1, 2, 1, 2):
        work.append(tasks[:count])
        del tasks[:count]
    drive(*[exchange(h, fwd_scale, False, syn_scale) for h in range(2)], work)

    pointwise(points, hidden, w1, 0, LONS // GROUP)

    def analyse(h):
        analyse_longitude(points[h : h + 1], basis, rows_spec[h : h + 1])
        analyse_latitude(rows_spec[h], analysis, HALVES[h], parts[h])

    analyse(0)
    tables_back = [
        functools.partial(build_synthesis, slots, doubled_back, synthesis, low, low + quarter)
        for low in range(0, LON_BLOCKS, quarter)
    ]
    gradients = [
        functools.partial(weight_gradient, h, wide_in[h], wide_grad[h], spectral_grad)
        for h in range(2)
    ]
    work = [[], tables_back[:2], tables_back[2:], [], [], gradients[:1], gradients[1:]]
    work.append([lambda: store(spectral_grad, grad_hbm)])
    drive(
        *[exchange(h, syn_scale, True, fwd_scale) for h in range(2)],
        work,
        lambda: analyse(1),
    )

    for copy in stores:
        copy.wait()


def kernel_scratch():
    v = pltpu.VMEM
    pieces = [v((128 * size, HALF), BF16) for half in HALVES for size, _ in half]
    return [
        v((LONS, ROWS, CH), BF16),
        v((LONS, ROWS, CH), BF16),
        v((KEEP, 2, CH // BS, BS * BS), BF16),
        v((CH, HID), BF16),
        v((HID, CH), BF16),
        v((2 * KM, LONS_PAD), BF16),
        v((LONS_PAD, 2 * KM), BF16),
        v((2, 2 * KLAT, 2 * ROWS), BF16),
        v((2, 2 * KLAT, 2 * ROWS), BF16),
        v((2, 2 * ROWS, 2 * KLAT), BF16),
        v((2, 2 * ROWS, 2 * KLAT), BF16),
        dma(11),
        dma(3),
        v((KEEP, 2, CH // BS, BS * BS), F32),
        *[v((LONS_PAD * STRIDE, HALF), F32)] * 2,
        *[v((2 * KM * STRIDE, HALF), F32)] * 2,
        *pieces,
        *pieces,
        v((16384, CH), BF16),
        v((LONS * ROWS, HID), BF16),
        v((LON_BLOCKS, 128), F32),
        v((8, 128), F32),
        v((8, 128), F32),
        v((4, 8, 128), F32),
        v((128, 128), F32),
        *[v((2 * KEEP, HALF), F32)] * 2,
        *[v((2 * KEEP * BETAS, CH), F32)] * 6,
        dma(6),
        pltpu.SemaphoreType.REGULAR,
        *gather_sems(),
        *gather_sems(),
        *scatter_scratch(HALVES[0]),
        *scatter_scratch(HALVES[1]),
    ]


def result_kernel(out_grad, part, grad, out, grad_out):
    out[...] = (out_grad[...].astype(F32) + part[...].astype(F32)).astype(BF16)
    grad_out[...] = grad[...]


def result_call(out_grad, part, grad):
    blocks = 2
    point = pl.BlockSpec((LONS * ROWS // blocks, CH), lambda i: (i, 0))
    mode = pl.BlockSpec((2 * KEEP * CH // BS // blocks, BS * BS), lambda i: (i, 0))
    return pl.pallas_call(
        result_kernel,
        grid=(blocks,),
        out_shape=(
            jax.ShapeDtypeStruct(out_grad.shape, BF16),
            jax.ShapeDtypeStruct(grad.shape, F32),
        ),
        in_specs=[point, point, mode],
        out_specs=(point, mode),
        compiler_params=pltpu.CompilerParams(vmem_limit_bytes=LIMIT),
        name="results",
    )(out_grad, part, grad)


def longitude_tables(lon_total):
    j = np.arange(lon_total).reshape(-1, LONS)
    j = np.pad(j, ((0, 0), (0, LONS_PAD - LONS)))
    q = np.arange(2 * KM)
    angles = (j[:, None, :] * (q // 2)[None, :, None] % lon_total) * (2.0 * math.pi / lon_total)
    basis = np.where((q % 2)[None, :, None] == 0, np.cos(angles), -np.sin(angles))
    basis[:, :, LONS:] = 0.0
    basis = basis.astype(np.float32)
    return jnp.asarray(basis, BF16), jnp.asarray(np.swapaxes(basis, 1, 2), BF16)


def latitude_tables(lat_total):
    wave = np.arange(KLAT) - KLAT // 2

    def angles(ids):
        return (wave[None, :, None] * ids[:, None, :] % (2 * lat_total)) * (math.pi / lat_total)

    ids = np.arange(lat_total).reshape(-1, ROWS)
    upper, lower = angles(ids), angles(2 * lat_total - 1 - ids)
    cu, su, cl, sl = np.cos(upper), np.sin(upper), np.cos(lower), np.sin(lower)

    def table(c, s):
        top, bottom = np.concatenate([c, s], axis=2), np.concatenate([-s, c], axis=2)
        return np.concatenate([top, bottom], axis=1)

    plain = np.stack([table(cu, su)] * 2, axis=1)
    doubled = np.stack([table(cu + cl, su + sl), table(cu - cl, su - sl)], axis=1)
    tables = []
    for value in (plain, doubled, np.swapaxes(plain, 2, 3), np.swapaxes(doubled, 2, 3)):
        tables.append(jnp.asarray(value.astype(np.float32), BF16))
    return tables


def body(in_field, out_grad, spec_weight, inner_weight, output_projection_weight, kept_modes):
    lat_parts, lon_parts = lax.axis_size("lat"), lax.axis_size("lon")
    lat_total, lon_total = ROWS * lat_parts, LONS * lon_parts
    fwd_scale = 1.0 / math.sqrt(2 * lat_total * lon_total)
    syn_scale = 1.0 / math.sqrt(KEEP * lat_parts * lon_parts)
    hbm = pl.BlockSpec(memory_space=pl.ANY)
    spectral_part, spectral_grad = pl.pallas_call(
        functools.partial(kernel, fwd_scale, syn_scale),
        out_shape=(
            jax.ShapeDtypeStruct((LONS, ROWS, CH), BF16),
            jax.ShapeDtypeStruct((KEEP, 2, CH // BS, BS * BS), F32),
        ),
        in_specs=[hbm] * 5 + [VMEM] + [hbm] * 6,
        out_specs=(hbm, hbm),
        scratch_shapes=kernel_scratch(),
        compiler_params=pltpu.CompilerParams(
            collective_id=0, has_side_effects=True, vmem_limit_bytes=LIMIT
        ),
        name="layer_gradients",
    )(
        jnp.swapaxes(in_field, 0, 1),
        jnp.swapaxes(out_grad, 0, 1),
        spec_weight,
        inner_weight,
        output_projection_weight,
        kept_modes.reshape(1, KEEP),
        *longitude_tables(lon_total),
        *latitude_tables(lat_total),
    )
    input_grad, spectral_grad = result_call(
        jnp.swapaxes(out_grad, 0, 1).reshape(LONS * ROWS, CH),
        spectral_part.reshape(LONS * ROWS, CH),
        spectral_grad.reshape(2 * KEEP * CH // BS, BS * BS),
    )
    return (
        jnp.swapaxes(input_grad.reshape(LONS, ROWS, CH), 0, 1),
        spectral_grad.reshape(KEEP, 2, CH // BS, BS * BS),
    )


def solution(mesh):
    return jax.shard_map(
        body,
        mesh=mesh,
        in_specs=(
            P("lat", "lon", None),
            P("lat", "lon", None),
            P(("lat", "lon"), None, None, None),
            P(),
            P(),
            P(("lat", "lon")),
        ),
        out_specs=(P("lat", "lon", None), P(("lat", "lon"), None, None, None)),
        check_vma=False,
    )
```
